32 devices in a mesh: groups: 2 (over y), rec: 4 (over z), lig: 2 (over x), fft: 2 (over core).
Axes of the slice: x: 2, y: 2, z: 4, core: 2. Of those that a mesh axis runs over, the one named last changes fastest.
Arguments:
- receptor_occupancy: int32 [16, 4, 64, 4096], P(('groups', 'rec', 'lig'), None, 'fft'), parts along dimension 0, may hold values from 0 to 3
- ligand_occupancy: int32 [16, 4, 64, 4096], P(('groups', 'rec', 'lig'), None, 'fft'), parts along dimension 0, may hold values from 0 to 3
- rot_index: int32 [16], P(('groups', 'rec', 'lig')), parts along dimension 0, may hold values from 0 to 3
- receptor_extent: int32 [16], P(('groups', 'rec', 'lig')), parts along dimension 0, may hold values from 16 to 64, as said below
- channel_weight: float32 [4], replicated, may hold values from -1 to 2
Outputs:
- plane_top: float32 [16, 3, 2, 64], P(('groups', 'rec', 'lig'), None, None, 'fft'), parts along dimension 0
The draws below stay inside these ranges and needn't reach their ends.
There are 2 independent parts, one for each index of `groups`. The reference program is written for one: setup_inputs(seed, part) draws one part's arguments, and reference() takes and returns one part's arrays. A program takes and returns all parts, laid end to end along the dimension named above; an argument that names none is the same for every part. Nothing has to cross between parts.
Inputs may be any that keep to these rules, and one draw needn't show every extreme that they name: `rot_index`: quarter turns. `receptor_extent`: some receptor has extent 64.
All inputs are finite; a program needn't handle non-finite values.
Results may differ from the reference program's by a relative error of at most 0.0062.
Values may be sent and summed in bfloat16 or wider, within the bound.
No kernel may reach another device: no remote copies, remote signals or barrier semaphores. Data moves between devices by JAX's collectives and lax.ppermute only.
A program may use at most 128 MiB of HBM per device.

```python
import math
from functools import partial
import jax
import jax.numpy as jnp
from jax import lax

G = 64
C = 4
REC_STEPS = 3
LIG_STEPS = 2
RECS = 8
POSES = 8
N_REC = 4
N_LIG = 2


def draw_receptor_extent(key, part):
    extents = jax.random.randint(key, (RECS,), G // 4, G + 1)
    chosen = jax.random.randint(jax.random.fold_in(key, 7), (), 0, RECS)
    return jnp.where(jnp.arange(RECS) == chosen, G, extents).astype(jnp.int32)


def set_ends(entries, rng, smallest, largest):
    longest = entries.shape.index(max(entries.shape))
    spots = []
    for shift in (0, 1):
        where = [jax.random.randint(jax.random.fold_in(rng, axis), (), 0, length) for axis, length in enumerate(entries.shape)]
        where[longest] = (where[longest] + shift) % entries.shape[longest]
        spots.append(tuple(where))
    return entries.at[spots[0]].set(smallest).at[spots[1]].set(largest)


def setup_inputs(seed: int = 0, part: int = 0) -> dict:
    arg_keys = jax.random.split(jax.random.key(seed), 6)
    own_keys = jax.random.split(jax.random.fold_in(arg_keys[5], part), 6)
    return {
        "receptor_occupancy": set_ends(jax.random.randint(own_keys[0], (RECS, C, G, G * G), 0, 4), jax.random.fold_in(own_keys[0], 1), 0, 3).astype(jnp.int32),
        "ligand_occupancy": set_ends(jax.random.randint(own_keys[1], (POSES, C, G, G * G), 0, 4), jax.random.fold_in(own_keys[1], 1), 0, 3).astype(jnp.int32),
        "rot_index": set_ends(jax.random.randint(own_keys[2], (POSES,), 0, 4), jax.random.fold_in(own_keys[2], 1), 0, 3).astype(jnp.int32),
        "receptor_extent": draw_receptor_extent(jax.random.fold_in(jax.random.fold_in(arg_keys[5], part), 71), part),
        "channel_weight": jnp.clip(jax.random.uniform(arg_keys[4], (C,), jnp.float32, -1.0, 2.0), -1.0, 2.0),
    }


def trig_tables(cells):
    indices = jnp.arange(cells, dtype=jnp.int32)
    phases = indices[:, None] * indices[None, :] % cells
    angles = phases.astype(jnp.float32) * (2.0 * math.pi / cells)
    return (jnp.cos(angles), jnp.sin(angles))

def mixing(cosine_table, sine_table, direction):
    row_real = jnp.stack([cosine_table, -direction * sine_table], axis=-1)
    row_imag = jnp.stack([direction * sine_table, cosine_table], axis=-1)
    return jnp.stack([row_real, row_imag], axis=-2)

def rounded(values):
    return lax.optimization_barrier(values.astype(jnp.bfloat16)).astype(jnp.float32)

def rotate_quarter(occupancy, turns):
    branches = [partial(jnp.rot90, k=quarter, axes=(2, 3)) for quarter in range(4)]
    return lax.switch(turns, branches, occupancy)

def unfold_grid(occupancy):
    cells = occupancy.shape[1]
    return occupancy.reshape(occupancy.shape[0], cells, cells, cells)

def forward_grid(occupancy, z_forward, forward_mix):
    channels = occupancy.shape[0]
    cells = occupancy.shape[-1]
    values = occupancy.astype(jnp.float32)
    section_one = rounded(jnp.einsum('cxyz,zw->cxyw', values, z_forward))
    section_one = section_one.reshape(channels, cells, cells, 2, cells)
    section_two = rounded(jnp.einsum('cxypz,kyqp->cxkqz', section_one, forward_mix))
    section_three = jnp.einsum('cxbpz,kxqp->ckbqz', section_two, forward_mix)
    return section_three.astype(jnp.bfloat16).reshape(channels, cells, cells, 2 * cells)

def cross_spectrum(receptor, ligand, weights, nonzero, volume):
    cells = receptor.shape[1]
    receptor = receptor.astype(jnp.float32)
    ligand = ligand.astype(jnp.float32)
    rec_real = receptor[..., :cells]
    rec_imag = receptor[..., cells:]
    lig_real = ligand[..., :cells]
    lig_imag = ligand[..., cells:]
    scaled = weights[:, None, None, None]
    real_part = lax.optimization_barrier(jnp.sum(scaled * (rec_real * lig_real + rec_imag * lig_imag), axis=0))
    imag_part = lax.optimization_barrier(jnp.sum(scaled * (rec_imag * lig_real - rec_real * lig_imag), axis=0))
    joined = jnp.concatenate([real_part, imag_part], axis=-1) * volume
    return rounded(jnp.where(nonzero, joined, 0.0))

def inverse_pair(cross, extent_now, inverse_mix, z_inverse, real_rows, score_scale):
    cells = cross.shape[0]
    spread = cross.reshape(cells, cells, 2, cells)
    back_one = rounded(jnp.einsum('xbpz,nxqp->nbqz', spread, inverse_mix)).reshape(cells, cells, 2 * cells)
    back_two = rounded(jnp.einsum('xbw,wv->xbv', back_one, z_inverse)).reshape(cells, cells, 2, cells)
    scores = jnp.einsum('xkpz,ykp->xyz', back_two, real_rows) * score_scale
    plane_max = lax.optimization_barrier(jnp.max(scores, axis=(1, 2)))
    planes = jnp.arange(cells, dtype=jnp.int32)
    return jnp.where(planes < extent_now, plane_max, 0.0)

def reference(receptor_occupancy, ligand_occupancy, rot_index, receptor_extent, channel_weight):
    cells = G
    cosine_table, sine_table = trig_tables(cells)
    forward_mix = rounded(mixing(cosine_table, sine_table, -1.0))
    inverse_mix = rounded(mixing(cosine_table, sine_table, 1.0))
    z_forward = rounded(jnp.concatenate([cosine_table, -sine_table], axis=1))
    z_inverse = jnp.transpose(inverse_mix, (3, 1, 2, 0)).reshape(2 * cells, 2 * cells)
    real_rows = inverse_mix[:, :, 0, :]
    volume = 1.0 / float(cells) ** 3
    score_scale = 1.0 / (cells * math.sqrt(cells))
    kx_index = lax.broadcasted_iota(jnp.int32, (cells, cells, 2 * cells), 0)
    ky_index = lax.broadcasted_iota(jnp.int32, (cells, cells, 2 * cells), 1)
    kz_index = lax.broadcasted_iota(jnp.int32, (cells, cells, 2 * cells), 2) % cells
    nonzero = kx_index + ky_index + kz_index > 0

    def receptor_spectrum(occupancy):
        return forward_grid(unfold_grid(occupancy), z_forward, forward_mix)

    def pose_spectrum(pose_pair):
        occupancy, turns = pose_pair
        return forward_grid(rotate_quarter(unfold_grid(occupancy), turns), z_forward, forward_mix)
    receptor_spectra = lax.map(receptor_spectrum, receptor_occupancy)
    pose_spectra = lax.map(pose_spectrum, (ligand_occupancy, rot_index))

    def device_row(position):
        cycle_row = position // N_LIG
        cycle_col = position % N_LIG
        outputs = []
        for rec_step in range(REC_STEPS):
            receptor_index = ((cycle_row - rec_step) % N_REC * N_LIG + cycle_col).astype(jnp.int32)
            receptor = receptor_spectra[receptor_index]
            extent_now = receptor_extent[receptor_index]
            row_scores = []
            for lig_step in range(LIG_STEPS):
                pose_index = (cycle_row * N_LIG + (cycle_col - lig_step) % N_LIG).astype(jnp.int32)
                cross = cross_spectrum(receptor, pose_spectra[pose_index], channel_weight, nonzero, volume)
                row_scores.append(inverse_pair(cross, extent_now, inverse_mix, z_inverse, real_rows, score_scale))
            outputs.append(jnp.stack(row_scores))
        return jnp.stack(outputs)
    return lax.map(device_row, jnp.arange(N_REC * N_LIG, dtype=jnp.int32))
```

```python
from functools import partial
import math

import jax
import jax.numpy as jnp
import ml_dtypes
import numpy as np
from jax import lax
from jax.experimental import pallas as pl
from jax.experimental.pallas import tpu as pltpu
from jax.sharding import PartitionSpec as P

REC_STEPS = 3
LIG_STEPS = 2
MIB = 1024 * 1024
F32 = jnp.float32
BF16 = jnp.bfloat16


def trig(cells):
    phases = np.arange(cells)[:, None] * np.arange(cells)[None, :] % cells
    angles = phases * (2.0 * math.pi / cells)
    pair = []
    for table in (np.cos(angles), np.sin(angles)):
        table = np.where(np.abs(table) < 1e-9, 0.0, table)
        pair.append(table.astype(np.float32).astype(ml_dtypes.bfloat16).astype(np.float32))
    return pair


def complex_rows(real, imag):
    return np.block([[real, -imag], [imag, real]])


def build_tables(cells, channels, slab, cores):
    cosine, sine = trig(cells)
    half = cells // 2
    own = half // cores
    sign = np.where(np.arange(cells) % 2 == 0, 1.0, -1.0).astype(np.float32)
    tables = {}

    def half_rows(core):
        order = [(core + turn) % cores * own + j for turn in range(cores) for j in range(own)]
        real = cosine[order].copy()
        imag = -sine[order]
        imag[order.index(0)] = sign
        return np.concatenate([real, imag], axis=0)

    def half_mix(core):
        order = [(core + turn) % cores * own + j for turn in range(cores) for j in range(own)]
        top = np.concatenate([cosine[order], sine[order]], axis=1)
        low = np.concatenate([-sine[order], cosine[order]], axis=1)
        at = order.index(0)
        one = np.ones(cells, np.float32)
        top[at] = np.concatenate([one, -sign])
        low[at] = np.concatenate([sign, one])
        return np.concatenate([top, low], axis=0)

    def flips(table, width):
        blocks = table.reshape(table.shape[0], -1, width)
        return np.stack([table, blocks[:, :, ::-1].reshape(table.shape)])

    two = np.eye(2, dtype=np.float32)
    full_rows = np.concatenate([cosine, -sine], axis=0)
    forward = complex_rows(cosine, -sine)
    inverse = complex_rows(cosine, sine)
    tables["z_even"] = np.stack([flips(np.kron(two, half_rows(core)), cells) for core in range(cores)], axis=1)
    tables["y_even"] = flips(forward, cells)
    tables["y_odd"] = flips(np.kron(two, full_rows), cells)
    tables["z_odd"] = np.stack([flips(half_mix(core), cells) for core in range(cores)], axis=1)

    spread = []
    for core in range(cores):
        blocks = []
        for turn in range(cores):
            start = (core + turn) % cores * slab
            mix = forward.reshape(2, cells, 2, cells)[:, :, :, start:start + slab]
            for part in range(2):
                block = np.zeros((channels, slab, channels, 2, cells), np.float32)
                for channel in range(channels):
                    block[channel, :, channel] = mix[:, :, part].transpose(2, 0, 1)
                blocks.append(block.reshape(channels * slab, channels * 2 * cells))
        spread.append(np.concatenate(blocks, axis=0))
    tables["x_forward"] = np.stack(spread)

    mirror = np.zeros((cells, cells), np.float32)
    mirror[np.arange(cells), -np.arange(cells) % cells] = 1.0
    eye = np.eye(cells, dtype=np.float32)
    none = np.zeros((cells, cells), np.float32)
    low = 0.5 * np.block([[eye + mirror, none], [none, eye - mirror]])
    high = 0.5 * np.block([[none, eye + mirror], [mirror - eye, none]])
    plain = np.eye(2 * cells, dtype=np.float32)
    tables["unpack"] = np.stack(
        [np.concatenate([low, high] if core == 0 else [plain, 0.0 * plain], axis=0) for core in range(cores)]
    )

    back = []
    for core in range(cores):
        block = np.zeros((LIG_STEPS, 2, cells, 2, cores, LIG_STEPS, slab), np.float32)
        parts = inverse.reshape(2, cells, 2, cells)
        for turn in range(cores):
            start = (core + turn) % cores * slab
            for pose in range(LIG_STEPS):
                block[pose, :, :, :, turn, pose] = parts[:, start:start + slab].transpose(2, 3, 0, 1)
        back.append(block.reshape(LIG_STEPS * 2 * cells, 2 * cores * LIG_STEPS * slab))
    tables["x_inverse"] = np.stack(back)
    tables["y_inverse"] = inverse

    last = []
    for core in range(cores):
        order = [(core + turn) % cores * own + j for turn in range(cores) for j in range(own)]
        real = 2.0 * cosine[order]
        imag = -2.0 * sine[order]
        at = order.index(0)
        real[at] = 1.0
        imag[at] = sign
        last.append(np.stack([real, imag], axis=1).reshape(2 * half, cells).T)
    tables["z_inverse"] = np.stack(last)
    return {name: jnp.asarray(table.astype(ml_dtypes.bfloat16)) for name, table in tables.items()}


def params(limit=48):
    return pltpu.CompilerParams(vmem_limit_bytes=limit * MIB)


def cost(flops, moved):
    return pl.CostEstimate(flops=int(flops), bytes_accessed=int(moved), transcendentals=0)


def lines(value):
    return value.astype(F32).astype(BF16)


def dot(left, right):
    return jnp.dot(left, right, preferred_element_type=F32)


def dot_lanes(left, right):
    return lax.dot_general(left, right, (((1,), (1,)), ((), ())), preferred_element_type=F32)


class Sizes:
    def __init__(self, channels, slab, plane, cores):
        self.channels, self.slab, self.cores = channels, slab, cores
        self.cells = slab * cores
        self.lanes = channels * slab
        self.fold = self.lanes // self.cells
        self.tiles = plane // self.lanes
        self.own = self.cells // 2 // cores
        self.chunks = 2
        self.chunk = self.own // self.chunks
        self.body = self.chunk * 2 * self.cells
        self.extra = 16


def section_kernel(s, steps, rotated, meta, occ, *refs):
    per = s.tiles // steps
    cells, lanes = s.cells, s.lanes
    if rotated:
        z_even, y_even, y_odd, z_odd = refs[:4]
        outs, (held, turned) = refs[4:-2], refs[-2:]
    else:
        z_even, y_even = refs[:2]
        outs, (held,) = refs[2:-1], refs[-1:]
    step = pl.program_id(0)

    def first(table, height):
        for pair in range(0, per, 2):
            rows = [
                lines(occ[0, :, :, (pair + k) * lanes:(pair + k + 1) * lanes].reshape(lanes, lanes)) for k in range(2)
            ]
            done = dot_lanes(table, jnp.concatenate(rows, axis=0))
            for k in range(2):
                for fold in range(s.fold):
                    at = (step * per + pair + k) * s.fold + fold
                    held[pl.ds(pl.multiple_of(at * height, 8), height), :] = done[
                        fold * height:(fold + 1) * height, k * lanes:(k + 1) * lanes
                    ]

    def column(ref, at, height):
        return ref[pl.ds(at, cells, stride=height), :]

    def put(index, value):
        group, plane = divmod(index, s.own)
        chunk, plane = divmod(plane, s.chunk)
        outs[group * s.chunks + chunk][plane * 2 * cells:(plane + 1) * 2 * cells, :] = value

    half = cells // 2

    def even():
        table = y_even[0]
        for pair in range(0, half, 2):
            rows = [
                jnp.concatenate([column(held, q * half + pair + k, cells) for q in range(2)], axis=0) for k in range(2)
            ]
            done = dot(table, jnp.concatenate(rows, axis=1).astype(BF16)).astype(BF16)
            for k in range(2):
                put(pair + k, done[:, k * lanes:(k + 1) * lanes])

    def odd():
        table = z_odd[0, 0]
        for pair in range(0, cells, 2):
            rows = [
                jnp.concatenate([column(held, q * cells + pair + k, 2 * cells) for q in range(2)], axis=0)
                for k in range(2)
            ]
            done = dot(table, jnp.concatenate(rows, axis=1).astype(BF16))
            for k in range(2):
                turned[(pair + k) * cells:(pair + k + 1) * cells, :] = done[:, k * lanes:(k + 1) * lanes]
        for plane in range(half):
            both = [column(turned, q * half + plane, cells) for q in range(2)]
            put(plane, jnp.concatenate(both, axis=0).astype(BF16))

    if rotated:
        is_odd = meta[2] % 2 == 1
        pl.when(jnp.logical_not(is_odd))(lambda: first(z_even[0, 0], cells))
        pl.when(is_odd)(lambda: first(y_odd[0], 2 * cells))
        pl.when(jnp.logical_and(step == steps - 1, jnp.logical_not(is_odd)))(even)
        pl.when(jnp.logical_and(step == steps - 1, is_odd))(odd)
    else:
        first(z_even[0, 0], cells)
        pl.when(step == steps - 1)(even)
        for chunk in range(s.chunks):
            outs[chunk][s.body:, :] = jnp.full((s.extra, lanes), meta[1].astype(F32)).astype(BF16)


def sections(s, t, meta, occ, rotated, steps=4):
    cells, lanes = s.cells, s.lanes
    extra = 0 if rotated else s.extra
    in_specs = [
        pl.BlockSpec((1, s.channels, s.slab, occ.shape[3] // steps), lambda i, m: (0, 0, 0, i)),
        pl.BlockSpec((1, 1) + t["z_even"].shape[2:], lambda i, m: (m[2] >> 1 if rotated else 0, m[0], 0, 0)),
        pl.BlockSpec((1,) + t["y_even"].shape[1:], lambda i, m: (m[2] >> 1 if rotated else 0, 0, 0)),
    ]
    operands = [occ, t["z_even"], t["y_even"]]
    scratch = [pltpu.VMEM((cells * (2 * cells if rotated else cells), lanes), F32)]
    if rotated:
        in_specs += [
            pl.BlockSpec((1,) + t["y_odd"].shape[1:], lambda i, m: (jnp.where(m[2] == 1, 1, 0), 0, 0)),
            pl.BlockSpec((1, 1) + t["z_odd"].shape[2:], lambda i, m: (jnp.where(m[2] == 3, 1, 0), m[0], 0, 0)),
        ]
        operands += [t["y_odd"], t["z_odd"]]
        scratch.append(pltpu.VMEM((cells * cells, lanes), F32))
    shapes = [jax.ShapeDtypeStruct((s.body + extra, lanes), BF16)] * s.chunks
    shapes += [jax.ShapeDtypeStruct((s.body, lanes), BF16)] * s.chunks
    out = pl.pallas_call(
        partial(section_kernel, s, steps, rotated),
        grid_spec=pltpu.PrefetchScalarGridSpec(
            num_scalar_prefetch=1,
            grid=(steps,),
            in_specs=in_specs,
            out_specs=[pl.BlockSpec(shape.shape, lambda i, m: (0, 0)) for shape in shapes],
            scratch_shapes=scratch,
        ),
        out_shape=shapes,
        compiler_params=params(),
        cost_estimate=cost(1.5e9, 4 * MIB),
    )(meta, *operands)
    return out[:s.chunks], out[s.chunks:]


def x_rows(s, own, other, base, planes, first_rows=None):
    stack = []
    for plane in planes:
        at = base + plane * 2 * s.cells
        parts = []
        for ref in (own, other):
            for p in range(2):
                parts.append(ref[at + p * s.cells:at + (p + 1) * s.cells, :])
        stack.append(jnp.concatenate(parts, axis=1))
    return stack


def unpacked_rows(s, own, other, unpack):
    cells = s.cells
    done = [dot(unpack, ref[:2 * cells, :]).astype(BF16) for ref in (own, other)]
    return [
        jnp.concatenate(
            [value[(2 * k + p) * cells:(2 * k + p + 1) * cells] for value in done for p in range(2)], axis=1
        )
        for k in range(2)
    ]


def spectrum_kernel(s, per, packed, meta, weight, own, other, table, unpack, main, *last):
    volume = 1.0 / float(s.cells) ** 3
    width = 2 * s.cells

    def put(ref, value):
        for channel in range(s.channels):
            lanes = slice(channel * width, (channel + 1) * width)
            ref[:, lanes] = (value[:, lanes] * (weight[channel] * volume)).astype(BF16)

    step = pl.program_id(0)
    rows = x_rows(s, own, other, 0, range(per))

    def first():
        low, high = unpacked_rows(s, own, other, unpack[0])
        done = dot(jnp.concatenate([low] + rows[1:] + [high], axis=0), table[0])
        put(main, done[:per * s.cells])
        put(last[0], done[per * s.cells:])

    def rest():
        put(main, dot(jnp.concatenate(rows, axis=0), table[0]))

    if packed:
        pl.when(step == 0)(first)
        pl.when(step > 0)(rest)
    else:
        rest()


def spectrum(s, t, meta, weight, own, other, chunk, per=4):
    rows, width = s.chunk * s.cells, s.channels * 2 * s.cells
    steps = s.chunk // per
    block = pl.BlockSpec((per * 2 * s.cells, s.lanes), lambda i, m, w: (i, 0))
    packed = chunk == 0
    out_specs = [
        pl.BlockSpec((per * s.cells, width), lambda i, m, w: (i, 0)),
        pl.BlockSpec((s.cells, width), lambda i, m, w: (0, 0)),
    ]
    shapes = [jax.ShapeDtypeStruct((rows, width), BF16), jax.ShapeDtypeStruct((s.cells, width), BF16)]
    return pl.pallas_call(
        partial(spectrum_kernel, s, per, packed),
        grid_spec=pltpu.PrefetchScalarGridSpec(
            num_scalar_prefetch=2,
            grid=(steps,),
            in_specs=[
                block,
                block,
                pl.BlockSpec((1,) + t["x_forward"].shape[1:], lambda i, m, w: (m[0], 0, 0)),
                pl.BlockSpec((1,) + t["unpack"].shape[1:], lambda i, m, w: (m[0], 0, 0)),
            ],
            out_specs=out_specs if packed else out_specs[:1],
        ),
        out_shape=shapes if packed else shapes[:1],
        compiler_params=params(),
        cost_estimate=cost(1.2e9, 2 * MIB),
    )(meta, weight, own, other, t["x_forward"], t["unpack"])


def cross_kernel(s, per, packed, meta, own, other, table, unpack, x_inverse, y_inverse, *refs):
    poses = refs[:LIG_STEPS]
    tops = refs[LIG_STEPS:2 * LIG_STEPS] if packed else ()
    keep, send = refs[-2:]
    cells = s.cells
    width = 2 * cells
    step = pl.program_id(0)
    lane = lax.broadcasted_iota(jnp.int32, (cells, width), 1)
    is_real = lane < cells

    def correlate(receptor, pose):
        straight = None
        for channel in range(s.channels):
            lanes = slice(channel * width, (channel + 1) * width)
            one = receptor[:, lanes]
            two = pose[:, lanes].astype(F32)
            here = (one * two, pltpu.roll(one, cells, 1) * two)
            straight = here if straight is None else (straight[0] + here[0], straight[1] + here[1])
        same, turned = straight
        return jnp.where(is_real, same + pltpu.roll(same, cells, 1), pltpu.roll(turned, cells, 1) - turned)

    def run(rows, first):
        done = dot(jnp.concatenate(rows, axis=0), table[0])
        cross = []
        for plane in range(per):
            here = slice(plane * cells, (plane + 1) * cells)
            both = []
            for pose in range(LIG_STEPS):
                value = correlate(done[here], poses[pose][here, :])
                if first and plane == 0:
                    row = lax.broadcasted_iota(jnp.int32, (cells, width), 0)
                    at_zero = (row == 0) & ((lane == 0) | (lane == cells)) & (meta[0] == 0)
                    value = jnp.where(at_zero, 0.0, value)
                    top = pltpu.roll(correlate(done[per * cells:], tops[pose][...]), cells, 1)
                    value = value + jnp.where(is_real, -top, top)
                both.append(value.astype(BF16))
            cross.append(jnp.concatenate(both, axis=1))
        back = dot(jnp.concatenate(cross, axis=0), x_inverse[0]).astype(BF16)
        lanes = s.cores * LIG_STEPS * s.slab
        kept = lax.broadcasted_iota(jnp.int32, (cells // 2, lanes), 1) < lanes // 2
        for pair in range(0, per, 2):
            planes = []
            for k in range(2):
                here = back[(pair + k) * cells:(pair + k + 1) * cells]
                planes.append(jnp.concatenate([here[:, :lanes], here[:, lanes:]], axis=0))
            out = dot(y_inverse[...], jnp.concatenate(planes, axis=1))
            for k in range(2):
                for q in range(2):
                    value = out[q * cells:(q + 1) * cells, k * lanes:(k + 1) * lanes]
                    low, high = value[:cells // 2], value[cells // 2:]
                    at = slice((pair + k) * cells + q * cells // 2, (pair + k) * cells + (q + 1) * cells // 2)
                    keep[at, :] = jnp.where(kept, low, pltpu.roll(high, lanes // 2, 1)).astype(BF16)
                    send[at, :] = jnp.where(kept, pltpu.roll(low, lanes // 2, 1), high).astype(BF16)

    rows = x_rows(s, own, other, 0, range(per))
    if packed:

        def opening():
            low, high = unpacked_rows(s, own, other, unpack[0])
            run([low] + rows[1:] + [high], True)

        pl.when(step == 0)(opening)
        pl.when(step > 0)(lambda: run(rows, False))
    else:
        run(rows, False)


def cross_back(s, t, meta, own, other, poses, tops, chunk, per=4):
    rows = s.chunk * s.cells
    steps = s.chunk // per
    packed = chunk == 0
    width = s.channels * 2 * s.cells
    block = pl.BlockSpec((per * 2 * s.cells, s.lanes), lambda i, m: (i, 0))
    in_specs = [
        block,
        block,
        pl.BlockSpec((1,) + t["x_forward"].shape[1:], lambda i, m: (m[0], 0, 0)),
        pl.BlockSpec((1,) + t["unpack"].shape[1:], lambda i, m: (m[0], 0, 0)),
        pl.BlockSpec((1,) + t["x_inverse"].shape[1:], lambda i, m: (m[0], 0, 0)),
        pl.BlockSpec(t["y_inverse"].shape, lambda i, m: (0, 0)),
    ]
    in_specs += [pl.BlockSpec((per * s.cells, width), lambda i, m: (i, 0))] * LIG_STEPS
    operands = [own, other, t["x_forward"], t["unpack"], t["x_inverse"], t["y_inverse"]]
    operands += [pose[chunk] for pose in poses]
    if packed:
        in_specs += [pl.BlockSpec((s.cells, width), lambda i, m: (0, 0))] * LIG_STEPS
        operands += tops
    lanes = s.cores * LIG_STEPS * s.slab
    out_block = pl.BlockSpec((per * s.cells, lanes), lambda i, m: (i, 0))
    return pl.pallas_call(
        partial(cross_kernel, s, per, packed),
        grid_spec=pltpu.PrefetchScalarGridSpec(
            num_scalar_prefetch=1, grid=(steps,), in_specs=in_specs, out_specs=[out_block] * 2
        ),
        out_shape=[jax.ShapeDtypeStruct((rows, lanes), BF16)] * 2,
        compiler_params=params(),
        cost_estimate=cost(1.5e9, 4 * MIB),
    )(meta, *operands)


def peak_kernel(s, last, meta, load, table, *refs):
    count = s.chunks * s.cores
    parts = refs[:count]
    earlier, out, held = refs[count:-2], refs[-2], refs[-1]
    cells = s.cells
    rows = s.chunk * cells
    for index, part in enumerate(parts):
        held[index * rows:(index + 1) * rows, :] = part[...].astype(F32)
    best = None
    low = cells // 2
    for pair in range(0, low, 2):
        columns = [held[pl.ds(pair + k, cells, stride=low), :] for k in range(2)]
        scores = dot(table[0], jnp.concatenate(columns, axis=1).astype(BF16))
        lanes = scores.shape[1] // 2
        here = jnp.maximum(scores[:, :lanes], scores[:, lanes:])
        best = here if best is None else jnp.maximum(best, here)
    row = jnp.max(best, axis=0, keepdims=True)
    row = jnp.maximum(row, pltpu.roll(row, row.shape[1] // 2, 1)) * (1.0 / (cells * math.sqrt(cells)))
    plane = lax.broadcasted_iota(jnp.int32, row.shape, 1) % s.slab + meta[0] * s.slab
    row = jnp.where(plane.astype(F32) < load[0:1, :].astype(F32), row, 0.0)
    if not last:
        out[...] = row
        return
    for index, value in enumerate([ref[...] for ref in earlier] + [row]):
        for pose in range(LIG_STEPS):
            out[0, index, pose:pose + 1, :] = value[:, pose * s.slab:(pose + 1) * s.slab]


def peaks(s, t, meta, load, kept, received, earlier, last):
    parts = [part for pair in (kept, received) for part in pair]
    lanes = parts[0].shape[1]
    in_specs = [
        pl.BlockSpec((s.extra, s.lanes), lambda i, m: (s.body // s.extra, 0)),
        pl.BlockSpec((1,) + t["z_inverse"].shape[1:], lambda i, m: (m[0], 0, 0)),
    ]
    in_specs += [pl.BlockSpec(part.shape, lambda i, m: (0, 0)) for part in parts]
    in_specs += [pl.BlockSpec((1, lanes), lambda i, m: (0, 0)) for _ in earlier]
    if last:
        shape = (1, REC_STEPS, LIG_STEPS, s.slab)
        out_spec = pl.BlockSpec(shape, lambda i, m: (0, 0, 0, 0))
    else:
        shape = (1, lanes)
        out_spec = pl.BlockSpec(shape, lambda i, m: (0, 0))
    return pl.pallas_call(
        partial(peak_kernel, s, last),
        grid_spec=pltpu.PrefetchScalarGridSpec(
            num_scalar_prefetch=1,
            grid=(1,),
            in_specs=in_specs,
            out_specs=out_spec,
            scratch_shapes=[pltpu.VMEM((len(parts) * parts[0].shape[0], lanes), F32)],
        ),
        out_shape=jax.ShapeDtypeStruct(shape, F32),
        compiler_params=params(),
        cost_estimate=cost(1e9, 2 * MIB),
    )(meta, load, t["z_inverse"], *parts, *earlier)


def passed_along(value, axis, steps=1):
    count = lax.axis_size(axis)
    return lax.ppermute(value, axis, [(source, (source + steps) % count) for source in range(count)])


def shards(tables, receptor_occupancy, ligand_occupancy, rot_index, receptor_extent, channel_weight):
    _, channels, slab, plane = receptor_occupancy.shape
    s = Sizes(channels, slab, plane, lax.axis_size("fft"))
    t = tables(s)
    core = lax.axis_index("fft").astype(jnp.int32)
    meta = jnp.concatenate([core[None], receptor_extent, rot_index])
    swapped = lambda parts: [passed_along(part, "fft") for part in parts]

    own, away = sections(s, t, meta, receptor_occupancy, False)
    other = swapped(away)
    receptors = [(own, other)]
    for _ in range(REC_STEPS - 1):
        own = [passed_along(part, "rec") for part in own]
        other = [passed_along(part, "rec") for part in other]
        receptors.append((own, other))

    pose_own, pose_away = sections(s, t, meta, ligand_occupancy, True)
    pose_other = swapped(pose_away)
    poses, tops = [], []
    for step in range(LIG_STEPS):
        if step:
            pose_own = [passed_along(part, "lig") for part in pose_own]
            pose_other = [passed_along(part, "lig") for part in pose_other]
        done = [
            spectrum(s, t, meta, channel_weight, a, b, chunk) for chunk, (a, b) in enumerate(zip(pose_own, pose_other))
        ]
        poses.append([out[0] for out in done])
        tops.append(done[0][1])

    rows = []
    for step, (own, other) in enumerate(receptors):
        kept, received = [], []
        for chunk in range(s.chunks):
            keep, send = cross_back(s, t, meta, own[chunk], other[chunk], poses, tops, chunk)
            kept.append(keep)
            received += swapped([send])
        last = step + 1 == REC_STEPS
        rows.append(peaks(s, t, meta, own[0], kept, received, rows if last else [], last))
    return rows[-1]


def solution(mesh):
    placed = (
        P(("groups", "rec", "lig"), None, "fft", None),
        P(("groups", "rec", "lig"), None, "fft", None),
        P(("groups", "rec", "lig")),
        P(("groups", "rec", "lig")),
        P(),
    )
    tables = lambda s: build_tables(s.cells, s.channels, s.slab, s.cores)
    return jax.shard_map(
        partial(shards, tables),
        mesh=mesh,
        in_specs=placed,
        out_specs=P(("groups", "rec", "lig"), None, None, "fft"),
        check_vma=False,
    )
```

```python
from functools import partial
import math

import jax
import jax.numpy as jnp
import ml_dtypes
import numpy as np
from jax import lax
from jax.experimental import pallas as pl
from jax.experimental.pallas import tpu as pltpu
from jax.sharding import PartitionSpec as P

REC_STEPS = 3
LIG_STEPS = 2
MIB = 1024 * 1024
F32 = jnp.float32
BF16 = jnp.bfloat16


def trig(cells):
    phases = np.arange(cells)[:, None] * np.arange(cells)[None, :] % cells
    angles = phases * (2.0 * math.pi / cells)
    pair = []
    for table in (np.cos(angles), np.sin(angles)):
        table = np.where(np.abs(table) < 1e-9, 0.0, table)
        pair.append(table.astype(np.float32).astype(ml_dtypes.bfloat16).astype(np.float32))
    return pair


def complex_rows(real, imag):
    return np.block([[real, -imag], [imag, real]])


def build_tables(cells, channels, slab, cores):
    cosine, sine = trig(cells)
    half = cells // 2
    own = half // cores
    sign = np.where(np.arange(cells) % 2 == 0, 1.0, -1.0).astype(np.float32)
    tables = {}

    def half_rows(core):
        order = [(core + turn) % cores * own + j for turn in range(cores) for j in range(own)]
        real = cosine[order].copy()
        imag = -sine[order]
        imag[order.index(0)] = sign
        return np.concatenate([real, imag], axis=0)

    def half_mix(core):
        order = [(core + turn) % cores * own + j for turn in range(cores) for j in range(own)]
        top = np.concatenate([cosine[order], sine[order]], axis=1)
        low = np.concatenate([-sine[order], cosine[order]], axis=1)
        at = order.index(0)
        one = np.ones(cells, np.float32)
        top[at] = np.concatenate([one, -sign])
        low[at] = np.concatenate([sign, one])
        return np.concatenate([top, low], axis=0)

    def flips(table, width):
        blocks = table.reshape(table.shape[0], -1, width)
        return np.stack([table, blocks[:, :, ::-1].reshape(table.shape)])

    two = np.eye(2, dtype=np.float32)
    full_rows = np.concatenate([cosine, -sine], axis=0)
    forward = complex_rows(cosine, -sine)
    inverse = complex_rows(cosine, sine)
    tables["z_even"] = np.stack([flips(np.kron(two, half_rows(core)), cells) for core in range(cores)], axis=1)
    tables["y_even"] = flips(forward, cells)
    tables["y_odd"] = flips(np.kron(two, full_rows), cells)
    tables["z_odd"] = np.stack([flips(half_mix(core), cells) for core in range(cores)], axis=1)

    spread = []
    for core in range(cores):
        blocks = []
        for turn in range(cores):
            start = (core + turn) % cores * slab
            mix = forward.reshape(2, cells, 2, cells)[:, :, :, start:start + slab]
            for part in range(2):
                block = np.zeros((channels, slab, channels, 2, cells), np.float32)
                for channel in range(channels):
                    block[channel, :, channel] = mix[:, :, part].transpose(2, 0, 1)
                blocks.append(block.reshape(channels * slab, channels * 2 * cells))
        spread.append(np.concatenate(blocks, axis=0))
    tables["x_forward"] = np.stack(spread)

    mirror = np.zeros((cells, cells), np.float32)
    mirror[np.arange(cells), -np.arange(cells) % cells] = 1.0
    eye = np.eye(cells, dtype=np.float32)
    none = np.zeros((cells, cells), np.float32)
    low = 0.5 * np.block([[eye + mirror, none], [none, eye - mirror]])
    high = 0.5 * np.block([[none, eye + mirror], [mirror - eye, none]])
    plain = np.eye(2 * cells, dtype=np.float32)
    tables["unpack"] = np.stack(
        [np.concatenate([low, high] if core == 0 else [plain, 0.0 * plain], axis=0) for core in range(cores)]
    )

    back = []
    for core in range(cores):
        block = np.zeros((LIG_STEPS, 2, cells, 2, cores, LIG_STEPS, slab), np.float32)
        parts = inverse.reshape(2, cells, 2, cells)
        for turn in range(cores):
            start = (core + turn) % cores * slab
            for pose in range(LIG_STEPS):
                block[pose, :, :, :, turn, pose] = parts[:, start:start + slab].transpose(2, 3, 0, 1)
        back.append(block.reshape(LIG_STEPS * 2 * cells, 2 * cores * LIG_STEPS * slab))
    tables["x_inverse"] = np.stack(back)
    tables["y_inverse"] = inverse

    last = []
    for core in range(cores):
        order = [(core + turn) % cores * own + j for turn in range(cores) for j in range(own)]
        real = 2.0 * cosine[order]
        imag = -2.0 * sine[order]
        at = order.index(0)
        real[at] = 1.0
        imag[at] = sign
        last.append(np.stack([real, imag], axis=1).reshape(2 * half, cells).T)
    tables["z_inverse"] = np.stack(last)
    return {name: jnp.asarray(table.astype(ml_dtypes.bfloat16)) for name, table in tables.items()}


COST = pl.CostEstimate(flops=1000, bytes_accessed=1000, transcendentals=0)


def params(limit=24):
    return pltpu.CompilerParams(vmem_limit_bytes=limit * MIB)


def lines(value):
    return value.astype(F32).astype(BF16)


def dot(left, right):
    return jnp.dot(left, right, preferred_element_type=F32)


def dot_lanes(left, right):
    return lax.dot_general(left, right, (((1,), (1,)), ((), ())), preferred_element_type=F32)


def place(cuts, plane):
    return max(k for k in range(len(cuts) - 1) if cuts[k] <= plane)


class Sizes:
    def __init__(self, channels, slab, plane, cores):
        self.channels, self.slab, self.cores = channels, slab, cores
        self.cells = slab * cores
        self.lanes = channels * slab
        self.fold = self.lanes // self.cells
        self.tiles = plane // self.lanes
        self.own = self.cells // 2 // cores
        self.halves = (0, self.own)
        self.whole = (0, self.own)
        self.size = 2 * self.cells
        self.extra = 16
        self.back = cores * LIG_STEPS * slab


def section_kernel(s, pieces, rotated, cuts, occ, scalar, *refs):
    cells, lanes = s.cells, s.lanes
    half, size = cells // 2, s.size
    count = 4 if rotated else 2
    hbm, refs = refs[:count], refs[count:]
    outs, refs = refs[:len(cuts)], refs[len(cuts):]
    small, buffer, held = refs[:3]
    tables = refs[3:3 + count]
    turned = refs[-2] if rotated else None
    sems = refs[-1]
    core = lax.axis_index("fft")

    first = pltpu.make_async_copy(scalar, small, sems.at[0])
    first.start()
    if rotated:
        first.wait()
        turns = small[0]
        is_odd = turns % 2 == 1
        picks = (
            hbm[0].at[turns // 2, core],
            hbm[1].at[turns // 2],
            hbm[2].at[jnp.where(turns == 1, 1, 0)],
            hbm[3].at[jnp.where(turns == 3, 1, 0), core],
        )
    else:
        picks = (hbm[0].at[0, core], hbm[1].at[0])
    loads = [pltpu.make_async_copy(pick, table, sems.at[1 + k]) for k, (pick, table) in enumerate(zip(picks, tables))]
    width = s.tiles // pieces * lanes
    for k in range(pieces):
        here = slice(k * width, (k + 1) * width)
        loads.append(pltpu.make_async_copy(occ.at[0, :, :, here], buffer.at[:, :, here], sems.at[1 + count + k]))
    for load in loads:
        load.start()
    for load in loads[:count]:
        load.wait()

    def lay(table, height, step):
        for tile in range(0, s.tiles, 2):
            rows = [
                lines(buffer[:, :, (tile + k) * lanes:(tile + k + 1) * lanes].reshape(lanes, lanes)) for k in range(2)
            ]
            done = dot_lanes(table[...], jnp.concatenate(rows, axis=0))
            for k in range(2):
                for fold in range(s.fold):
                    at = ((tile + k) * s.fold + fold) * step
                    held[at:at + height, :] = done[fold * height:(fold + 1) * height, k * lanes:(k + 1) * lanes]

    def column(ref, at, step):
        return ref[pl.ds(at, cells, stride=step), :]

    def put(index, value):
        group, plane = divmod(index, s.own)
        if group == 0:
            outs[0][plane * size:(plane + 1) * size, :] = value
            return
        cut = place(cuts, plane)
        plane -= cuts[cut]
        outs[1 + cut][plane * size:(plane + 1) * size, :] = value

    def even():
        step = cells + 8
        for load in loads[count:]:
            load.wait()
        lay(tables[0], cells, step)
        for pair in range(0, half, 2):
            rows = [
                jnp.concatenate([column(held, q * half + pair + k, step) for q in range(2)], axis=0) for k in range(2)
            ]
            done = dot(tables[1][...], jnp.concatenate(rows, axis=1).astype(BF16)).astype(BF16)
            for k in range(2):
                put(pair + k, done[:, k * lanes:(k + 1) * lanes])

    def odd():
        step, short = size + 8, cells + 8
        for load in loads[count:]:
            load.wait()
        lay(tables[2], size, step)
        for pair in range(0, cells, 2):
            rows = [
                jnp.concatenate([column(held, q * cells + pair + k, step) for q in range(2)], axis=0) for k in range(2)
            ]
            done = dot(tables[3][...], jnp.concatenate(rows, axis=1).astype(BF16))
            for k in range(2):
                turned[(pair + k) * short:(pair + k) * short + cells, :] = done[:, k * lanes:(k + 1) * lanes]
        for plane in range(half):
            both = [column(turned, q * half + plane, short) for q in range(2)]
            put(plane, jnp.concatenate(both, axis=0).astype(BF16))

    if rotated:
        pl.when(jnp.logical_not(is_odd))(even)
        pl.when(is_odd)(odd)
    else:
        even()
        first.wait()
        outs[0][s.own * size:, :] = jnp.full((s.extra, lanes), small[0].astype(F32)).astype(BF16)


def sections(s, t, occ, scalar, rotated, cuts, pieces=2):
    cells, lanes = s.cells, s.lanes
    names = ["z_even", "y_even"] + (["y_odd", "z_odd"] if rotated else [])
    hbm = pl.BlockSpec(memory_space=pltpu.HBM)
    pin = lambda value: pltpu.with_memory_space_constraint(value, pltpu.HBM)
    scratch = [
        pltpu.SMEM(scalar.shape, jnp.int32),
        pltpu.VMEM(occ.shape[1:], jnp.int32),
        pltpu.VMEM((cells * ((s.size if rotated else cells) + 8), lanes), F32),
    ]
    scratch += [pltpu.VMEM(t[name].shape[-2:], BF16) for name in names]
    if rotated:
        scratch.append(pltpu.VMEM((cells * (cells + 8), lanes), F32))
    scratch.append(pltpu.SemaphoreType.DMA((1 + len(names) + pieces,)))
    rows = [s.own * s.size + (0 if rotated else s.extra)]
    rows += [(high - low) * s.size for low, high in zip(cuts, cuts[1:])]
    return pl.pallas_call(
        partial(section_kernel, s, pieces, rotated, cuts),
        in_specs=[hbm, pl.BlockSpec(memory_space=pl.ANY)] + [hbm] * len(names),
        out_specs=[pl.BlockSpec(memory_space=pltpu.VMEM)] * len(rows),
        out_shape=[jax.ShapeDtypeStruct((count, lanes), BF16) for count in rows],
        scratch_shapes=scratch,
        compiler_params=params(),
        cost_estimate=COST,
    )(pin(occ), scalar, *[pin(t[name]) for name in names])


def x_rows(s, cuts, own, others, plane):
    cut = place(cuts, plane)
    parts = []
    for ref, at in ((own, plane * s.size), (others[cut], (plane - cuts[cut]) * s.size)):
        for p in range(2):
            parts.append(ref[at + p * s.cells:at + (p + 1) * s.cells, :])
    return jnp.concatenate(parts, axis=1)


def unpacked_rows(s, own, others, unpack):
    cells = s.cells
    done = [dot(unpack, ref[:s.size, :]).astype(BF16) for ref in (own, others[0])]
    return [
        jnp.concatenate(
            [value[(2 * k + p) * cells:(2 * k + p + 1) * cells] for value in done for p in range(2)], axis=1
        )
        for k in range(2)
    ]


def spectrum_kernel(s, cuts, per, weight, table, unpack, own, *refs):
    others, (main, last) = refs[:-2], refs[-2:]
    volume = 1.0 / float(s.cells) ** 3
    core = lax.axis_index("fft")

    def put(ref, at, value):
        for channel in range(s.channels):
            lanes = slice(channel * s.size, (channel + 1) * s.size)
            ref[at:at + value.shape[0], lanes] = (value[:, lanes] * (weight[channel] * volume)).astype(BF16)

    for start in range(0, s.own, per):
        rows = [x_rows(s, cuts, own, others, plane) for plane in range(start, start + per)]
        if start == 0:
            rows[0], high = unpacked_rows(s, own, others, unpack[core])
            rows.append(high)
        done = dot(jnp.concatenate(rows, axis=0), table[core])
        put(main, start * s.cells, done[:per * s.cells])
        if start == 0:
            put(last, 0, done[per * s.cells:])


def spectrum(s, t, weight, own, others, cuts, per=4):
    width = s.channels * s.size
    vmem = pl.BlockSpec(memory_space=pltpu.VMEM)
    return pl.pallas_call(
        partial(spectrum_kernel, s, cuts, per),
        in_specs=[pl.BlockSpec(memory_space=pltpu.SMEM)] + [vmem] * (3 + len(others)),
        out_specs=[vmem] * 2,
        out_shape=[jax.ShapeDtypeStruct((s.own * s.cells, width), BF16), jax.ShapeDtypeStruct((s.cells, width), BF16)],
        compiler_params=params(),
        cost_estimate=COST,
    )(weight, t["x_forward"], t["unpack"], own, *others)


def cross_kernel(s, cuts, planes, per, table, unpack, x_inverse, y_inverse, *refs):
    poses, tops = refs[:LIG_STEPS], refs[LIG_STEPS:2 * LIG_STEPS]
    own, others = refs[2 * LIG_STEPS], refs[2 * LIG_STEPS + 1:-2]
    keep, send = refs[-2:]
    cells, width, lanes = s.cells, s.size, s.back
    core = lax.axis_index("fft")
    lane = lax.broadcasted_iota(jnp.int32, (cells, width), 1)
    is_real = lane < cells
    kept = lax.broadcasted_iota(jnp.int32, (cells // 2, lanes), 1) < lanes // 2

    def correlate(receptor, pose):
        straight = None
        for channel in range(s.channels):
            here = slice(channel * width, (channel + 1) * width)
            one = receptor[:, here]
            two = pose[:, here].astype(F32)
            terms = (one * two, pltpu.roll(one, cells, 1) * two)
            straight = terms if straight is None else (straight[0] + terms[0], straight[1] + terms[1])
        same, turned = straight
        return jnp.where(is_real, same + pltpu.roll(same, cells, 1), pltpu.roll(turned, cells, 1) - turned)

    for start in range(planes[0], planes[1], per):
        rows = [x_rows(s, cuts, own, others, plane) for plane in range(start, start + per)]
        if start == 0:
            rows[0], high = unpacked_rows(s, own, others, unpack[core])
            rows.append(high)
        done = dot(jnp.concatenate(rows, axis=0), table[core])
        cross = []
        for k in range(per):
            both = []
            for pose in range(LIG_STEPS):
                at = (start + k) * cells
                value = correlate(done[k * cells:(k + 1) * cells], poses[pose][at:at + cells, :])
                if start + k == 0:
                    row = lax.broadcasted_iota(jnp.int32, (cells, width), 0)
                    at_zero = (row == 0) & ((lane == 0) | (lane == cells)) & (core == 0)
                    value = jnp.where(at_zero, 0.0, value)
                    top = pltpu.roll(correlate(done[per * cells:], tops[pose][...]), cells, 1)
                    value = value + jnp.where(is_real, -top, top)
                both.append(value.astype(BF16))
            cross.append(jnp.concatenate(both, axis=1))
        back = dot(jnp.concatenate(cross, axis=0), x_inverse[core]).astype(BF16)
        for pair in range(0, per, 2):
            sides = []
            for k in range(2):
                here = back[(pair + k) * cells:(pair + k + 1) * cells]
                sides.append(jnp.concatenate([here[:, :lanes], here[:, lanes:]], axis=0))
            out = dot(y_inverse[...], jnp.concatenate(sides, axis=1))
            for k in range(2):
                for q in range(2):
                    value = out[q * cells:(q + 1) * cells, k * lanes:(k + 1) * lanes]
                    low, high = value[:cells // 2], value[cells // 2:]
                    at = (start - planes[0] + pair + k) * cells + q * cells // 2
                    at = slice(at, at + cells // 2)
                    keep[at, :] = jnp.where(kept, low, pltpu.roll(high, lanes // 2, 1)).astype(BF16)
                    send[at, :] = jnp.where(kept, pltpu.roll(low, lanes // 2, 1), high).astype(BF16)


def cross_back(s, t, own, others, poses, tops, cuts, planes, per=4):
    vmem = pl.BlockSpec(memory_space=pltpu.VMEM)
    shape = jax.ShapeDtypeStruct(((planes[1] - planes[0]) * s.cells, s.back), BF16)
    operands = [t["x_forward"], t["unpack"], t["x_inverse"], t["y_inverse"], *poses, *tops, own, *others]
    return pl.pallas_call(
        partial(cross_kernel, s, cuts, planes, per),
        in_specs=[vmem] * len(operands),
        out_specs=[vmem] * 2,
        out_shape=[shape] * 2,
        compiler_params=params(),
        cost_estimate=COST,
    )(*operands)


def peak_kernel(s, count, last, load, table, *refs):
    parts = refs[:count]
    earlier, out, held = refs[count:-2], refs[-2], refs[-1]
    cells = s.cells
    low = cells // 2
    core = lax.axis_index("fft")
    at = 0
    for part in parts:
        held[at:at + part.shape[0], :] = part[...].astype(F32)
        at += part.shape[0]
    best = None
    for pair in range(0, low, 2):
        columns = [held[pl.ds(pair + k, cells, stride=low), :] for k in range(2)]
        scores = dot(table[core], jnp.concatenate(columns, axis=1).astype(BF16))
        here = jnp.maximum(scores[:, :s.back], scores[:, s.back:])
        best = here if best is None else jnp.maximum(best, here)
    row = jnp.max(best, axis=0, keepdims=True)
    row = jnp.maximum(row, pltpu.roll(row, s.back // 2, 1)) * (1.0 / (cells * math.sqrt(cells)))
    plane = lax.broadcasted_iota(jnp.int32, row.shape, 1) % s.slab + core * s.slab
    extent = load[s.own * s.size:s.own * s.size + 1, :].astype(F32)
    row = jnp.where(plane.astype(F32) < extent, row, 0.0)
    if not last:
        out[...] = row
        return
    for index, value in enumerate([ref[...] for ref in earlier] + [row]):
        for pose in range(LIG_STEPS):
            out[0, index, pose:pose + 1, :] = value[:, pose * s.slab:(pose + 1) * s.slab]


def peaks(s, t, load, parts, earlier, last):
    vmem = pl.BlockSpec(memory_space=pltpu.VMEM)
    shape = (1, REC_STEPS, LIG_STEPS, s.slab) if last else (1, s.back)
    return pl.pallas_call(
        partial(peak_kernel, s, len(parts), last),
        in_specs=[vmem] * (2 + len(parts) + len(earlier)),
        out_specs=vmem,
        out_shape=jax.ShapeDtypeStruct(shape, F32),
        scratch_shapes=[pltpu.VMEM((s.cells * s.cells // 2, s.back), F32)],
        compiler_params=params(),
        cost_estimate=COST,
    )(load, t["z_inverse"], *parts, *earlier)


def passed_along(value, axis, steps=1):
    count = lax.axis_size(axis)
    return lax.ppermute(value, axis, [(source, (source + steps) % count) for source in range(count)])


def passed_across(value, axis):
    count, cores = lax.axis_size(axis), lax.axis_size("fft")
    pairs = [
        (place * cores + core, (place + 1) % count * cores + (core + 1) % cores)
        for place in range(count)
        for core in range(cores)
    ]
    return lax.ppermute(value, (axis, "fft"), pairs)


def after(value, *others):
    return lax.optimization_barrier((value, *others))[0]


def shards(tables, receptor_occupancy, ligand_occupancy, rot_index, receptor_extent, channel_weight):
    _, channels, slab, plane = receptor_occupancy.shape
    s = Sizes(channels, slab, plane, lax.axis_size("fft"))
    t = tables(s)
    swapped = lambda parts: [passed_along(part, "fft") for part in parts]

    own, *away = sections(s, t, receptor_occupancy, receptor_extent, False, s.halves)
    others = swapped(away)
    receptors = [(own, others)]
    receptors.append((passed_along(own, "rec"), [passed_across(part, "rec") for part in away]))

    ligand_occupancy = after(ligand_occupancy, *others)
    pose, *pose_away = sections(s, t, ligand_occupancy, rot_index, True, s.whole)
    pose_others = swapped(pose_away)
    next_pose, next_others = passed_along(pose, "lig"), [passed_across(part, "lig") for part in pose_away]
    spectra = [spectrum(s, t, channel_weight, pose, pose_others, s.whole)]

    own, others = receptors[1]
    own = after(own, spectra[0][0])
    receptors[1] = (own, others)
    receptors.append((passed_along(own, "rec"), [passed_along(part, "rec") for part in others]))

    spectra.append(spectrum(s, t, channel_weight, next_pose, next_others, s.whole))
    poses, tops = [main for main, _ in spectra], [top for _, top in spectra]

    rows = []
    for step, (own, others) in enumerate(receptors):
        last = step + 1 == REC_STEPS
        ranges = list(zip(s.halves, s.halves[1:])) if last else [s.whole]
        if last:
            own = after(own, *rows)
        sides = [cross_back(s, t, own, others, poses, tops, s.halves, planes) for planes in ranges]
        parts = [keep for keep, _ in sides] + swapped([send for _, send in sides])
        rows.append(peaks(s, t, own, parts, rows if last else [], last))
    return rows[-1]


def solution(mesh):
    placed = (
        P(("groups", "rec", "lig"), None, "fft", None),
        P(("groups", "rec", "lig"), None, "fft", None),
        P(("groups", "rec", "lig")),
        P(("groups", "rec", "lig")),
        P(),
    )
    tables = lambda s: build_tables(s.cells, s.channels, s.slab, s.cores)
    return jax.shard_map(
        partial(shards, tables),
        mesh=mesh,
        in_specs=placed,
        out_specs=P(("groups", "rec", "lig"), None, None, "fft"),
        check_vma=False,
    )
```

```python
from functools import partial
import math

import jax
import jax.numpy as jnp
import ml_dtypes
import numpy as np
from jax import lax
from jax.experimental import pallas as pl
from jax.experimental.pallas import tpu as pltpu
from jax.sharding import PartitionSpec as P

REC_STEPS = 3
LIG_STEPS = 2
MIB = 1024 * 1024
F32 = jnp.float32
BF16 = jnp.bfloat16


def trig(cells):
    phases = np.arange(cells)[:, None] * np.arange(cells)[None, :] % cells
    angles = phases * (2.0 * math.pi / cells)
    pair = []
    for table in (np.cos(angles), np.sin(angles)):
        table = np.where(np.abs(table) < 1e-9, 0.0, table)
        pair.append(table.astype(np.float32).astype(ml_dtypes.bfloat16).astype(np.float32))
    return pair


def complex_rows(real, imag):
    return np.block([[real, -imag], [imag, real]])


def build_tables(cells, channels, slab, cores):
    cosine, sine = trig(cells)
    half = cells // 2
    own = half // cores
    sign = np.where(np.arange(cells) % 2 == 0, 1.0, -1.0).astype(np.float32)
    tables = {}

    def half_rows(core):
        order = [(core + turn) % cores * own + j for turn in range(cores) for j in range(own)]
        real = cosine[order].copy()
        imag = -sine[order]
        imag[order.index(0)] = sign
        return np.concatenate([real, imag], axis=0)

    def half_mix(core):
        order = [(core + turn) % cores * own + j for turn in range(cores) for j in range(own)]
        top = np.concatenate([cosine[order], sine[order]], axis=1)
        low = np.concatenate([-sine[order], cosine[order]], axis=1)
        at = order.index(0)
        one = np.ones(cells, np.float32)
        top[at] = np.concatenate([one, -sign])
        low[at] = np.concatenate([sign, one])
        return np.concatenate([top, low], axis=0)

    def flips(table, width):
        blocks = table.reshape(table.shape[0], -1, width)
        return np.stack([table, blocks[:, :, ::-1].reshape(table.shape)])

    two = np.eye(2, dtype=np.float32)
    full_rows = np.concatenate([cosine, -sine], axis=0)
    forward = complex_rows(cosine, -sine)
    inverse = complex_rows(cosine, sine)
    tables["z_even"] = np.stack([flips(np.kron(two, half_rows(core)), cells) for core in range(cores)], axis=1)
    tables["y_even"] = flips(forward, cells)
    tables["y_odd"] = flips(np.kron(two, full_rows), cells)
    tables["z_odd"] = np.stack([flips(half_mix(core), cells) for core in range(cores)], axis=1)

    spread = []
    for core in range(cores):
        blocks = []
        for turn in range(cores):
            start = (core + turn) % cores * slab
            mix = forward.reshape(2, cells, 2, cells)[:, :, :, start:start + slab]
            for part in range(2):
                block = np.zeros((channels, slab, channels, 2, cells), np.float32)
                for channel in range(channels):
                    block[channel, :, channel] = mix[:, :, part].transpose(2, 0, 1)
                blocks.append(block.reshape(channels * slab, channels * 2 * cells))
        spread.append(np.concatenate(blocks, axis=0))
    tables["x_forward"] = np.stack(spread)

    mirror = np.zeros((cells, cells), np.float32)
    mirror[np.arange(cells), -np.arange(cells) % cells] = 1.0
    eye = np.eye(cells, dtype=np.float32)
    none = np.zeros((cells, cells), np.float32)
    low = 0.5 * np.block([[eye + mirror, none], [none, eye - mirror]])
    high = 0.5 * np.block([[none, eye + mirror], [mirror - eye, none]])
    plain = np.eye(2 * cells, dtype=np.float32)
    tables["unpack"] = np.stack(
        [np.concatenate([low, high] if core == 0 else [plain, 0.0 * plain], axis=0) for core in range(cores)]
    )

    back = []
    for core in range(cores):
        block = np.zeros((LIG_STEPS, 2, cells, 2, cores, LIG_STEPS, slab), np.float32)
        parts = inverse.reshape(2, cells, 2, cells)
        for turn in range(cores):
            start = (core + turn) % cores * slab
            for pose in range(LIG_STEPS):
                block[pose, :, :, :, turn, pose] = parts[:, start:start + slab].transpose(2, 3, 0, 1)
        back.append(block.reshape(LIG_STEPS * 2 * cells, 2 * cores * LIG_STEPS * slab))
    tables["x_inverse"] = np.stack(back)
    tables["y_inverse"] = inverse

    last = []
    for core in range(cores):
        order = [(core + turn) % cores * own + j for turn in range(cores) for j in range(own)]
        real = 2.0 * cosine[order]
        imag = -2.0 * sine[order]
        at = order.index(0)
        real[at] = 1.0
        imag[at] = sign
        last.append(np.stack([real, imag], axis=1).reshape(2 * half, cells).T)
    tables["z_inverse"] = np.stack(last)
    return {name: jnp.asarray(table.astype(ml_dtypes.bfloat16)) for name, table in tables.items()}


COST = pl.CostEstimate(flops=1000, bytes_accessed=1000, transcendentals=0)


def params(limit=24):
    return pltpu.CompilerParams(vmem_limit_bytes=limit * MIB)


def lines(value):
    return value.astype(F32).astype(BF16)


def dot(left, right):
    return jnp.dot(left, right, preferred_element_type=F32)


def dot_lanes(left, right):
    return lax.dot_general(left, right, (((1,), (1,)), ((), ())), preferred_element_type=F32)


def place(cuts, plane):
    return max(k for k in range(len(cuts) - 1) if cuts[k] <= plane)


class Sizes:
    def __init__(self, channels, slab, plane, cores):
        self.channels, self.slab, self.cores = channels, slab, cores
        self.cells = slab * cores
        self.lanes = channels * slab
        self.fold = self.lanes // self.cells
        self.tiles = plane // self.lanes
        self.own = self.cells // 2 // cores
        self.whole = (0, self.own)
        self.parts = (0, self.own * 3 // 4, self.own)
        self.size = 2 * self.cells
        self.extra = 16
        self.back = cores * LIG_STEPS * slab


def section_kernel(s, pieces, rotated, cuts, occ, scalar, *refs):
    cells, lanes = s.cells, s.lanes
    half, size = cells // 2, s.size
    count = 4 if rotated else 2
    hbm, refs = refs[:count], refs[count:]
    outs, refs = refs[:len(cuts)], refs[len(cuts):]
    small, buffer, held = refs[:3]
    tables = refs[3:3 + count]
    turned = refs[-2] if rotated else None
    sems = refs[-1]
    core = lax.axis_index("fft")

    first = pltpu.make_async_copy(scalar, small, sems.at[0])
    first.start()
    if rotated:
        first.wait()
        turns = small[0]
        is_odd = turns % 2 == 1
        picks = (
            hbm[0].at[turns // 2, core],
            hbm[1].at[turns // 2],
            hbm[2].at[jnp.where(turns == 1, 1, 0)],
            hbm[3].at[jnp.where(turns == 3, 1, 0), core],
        )
    else:
        picks = (hbm[0].at[0, core], hbm[1].at[0])
    loads = [pltpu.make_async_copy(pick, table, sems.at[1 + k]) for k, (pick, table) in enumerate(zip(picks, tables))]
    width = s.tiles // pieces * lanes
    for k in range(pieces):
        here = slice(k * width, (k + 1) * width)
        loads.append(pltpu.make_async_copy(occ.at[0, :, :, here], buffer.at[:, :, here], sems.at[1 + count + k]))
    for load in loads:
        load.start()
    for load in loads[:count]:
        load.wait()

    def lay(table, height, step):
        for tile in range(0, s.tiles, 2):
            if tile % (s.tiles // pieces) == 0:
                loads[count + tile * pieces // s.tiles].wait()
            rows = [
                lines(buffer[:, :, (tile + k) * lanes:(tile + k + 1) * lanes].reshape(lanes, lanes)) for k in range(2)
            ]
            done = dot_lanes(table[...], jnp.concatenate(rows, axis=0))
            for k in range(2):
                for fold in range(s.fold):
                    at = ((tile + k) * s.fold + fold) * step
                    held[at:at + height, :] = done[fold * height:(fold + 1) * height, k * lanes:(k + 1) * lanes]

    def column(ref, at, step):
        return ref[pl.ds(at, cells, stride=step), :]

    def put(index, value):
        group, plane = divmod(index, s.own)
        if group == 0:
            outs[0][plane * size:(plane + 1) * size, :] = value
            return
        cut = place(cuts, plane)
        plane -= cuts[cut]
        outs[1 + cut][plane * size:(plane + 1) * size, :] = value

    def even():
        step = cells + 8
        lay(tables[0], cells, step)
        for pair in range(0, half, 2):
            rows = [
                jnp.concatenate([column(held, q * half + pair + k, step) for q in range(2)], axis=0) for k in range(2)
            ]
            done = dot(tables[1][...], jnp.concatenate(rows, axis=1).astype(BF16)).astype(BF16)
            for k in range(2):
                put(pair + k, done[:, k * lanes:(k + 1) * lanes])

    def odd():
        step, short = size + 8, cells + 8
        lay(tables[2], size, step)
        for pair in range(0, cells, 2):
            rows = [
                jnp.concatenate([column(held, q * cells + pair + k, step) for q in range(2)], axis=0) for k in range(2)
            ]
            done = dot(tables[3][...], jnp.concatenate(rows, axis=1).astype(BF16))
            for k in range(2):
                turned[(pair + k) * short:(pair + k) * short + cells, :] = done[:, k * lanes:(k + 1) * lanes]
        for plane in range(half):
            both = [column(turned, q * half + plane, short) for q in range(2)]
            put(plane, jnp.concatenate(both, axis=0).astype(BF16))

    if rotated:
        pl.when(jnp.logical_not(is_odd))(even)
        pl.when(is_odd)(odd)
    else:
        even()
        first.wait()
        outs[0][s.own * size:, :] = jnp.full((s.extra, lanes), small[0].astype(F32)).astype(BF16)


def sections(s, t, occ, scalar, rotated, cuts, pieces=2):
    cells, lanes = s.cells, s.lanes
    names = ["z_even", "y_even"] + (["y_odd", "z_odd"] if rotated else [])
    hbm = pl.BlockSpec(memory_space=pltpu.HBM)
    pin = lambda value: pltpu.with_memory_space_constraint(value, pltpu.HBM)
    scratch = [
        pltpu.SMEM(scalar.shape, jnp.int32),
        pltpu.VMEM(occ.shape[1:], jnp.int32),
        pltpu.VMEM((cells * ((s.size if rotated else cells) + 8), lanes), F32),
    ]
    scratch += [pltpu.VMEM(t[name].shape[-2:], BF16) for name in names]
    if rotated:
        scratch.append(pltpu.VMEM((cells * (cells + 8), lanes), F32))
    scratch.append(pltpu.SemaphoreType.DMA((1 + len(names) + pieces,)))
    rows = [s.own * s.size + (0 if rotated else s.extra)]
    rows += [(high - low) * s.size for low, high in zip(cuts, cuts[1:])]
    return pl.pallas_call(
        partial(section_kernel, s, pieces, rotated, cuts),
        in_specs=[hbm, pl.BlockSpec(memory_space=pl.ANY)] + [hbm] * len(names),
        out_specs=[pl.BlockSpec(memory_space=pltpu.VMEM)] * len(rows),
        out_shape=[jax.ShapeDtypeStruct((count, lanes), BF16) for count in rows],
        scratch_shapes=scratch,
        compiler_params=params(),
        cost_estimate=COST,
    )(pin(occ), scalar, *[pin(t[name]) for name in names])


def x_rows(s, cuts, own, others, plane):
    cut = place(cuts, plane)
    parts = []
    for ref, at in ((own, plane * s.size), (others[cut], (plane - cuts[cut]) * s.size)):
        for p in range(2):
            parts.append(ref[at + p * s.cells:at + (p + 1) * s.cells, :])
    return jnp.concatenate(parts, axis=1)


def unpacked_rows(s, own, others, unpack):
    cells = s.cells
    done = [dot(unpack, ref[:s.size, :]).astype(BF16) for ref in (own, others[0])]
    return [
        jnp.concatenate(
            [value[(2 * k + p) * cells:(2 * k + p + 1) * cells] for value in done for p in range(2)], axis=1
        )
        for k in range(2)
    ]


def spectrum_kernel(s, cuts, per, weight, table, unpack, own, *refs):
    others, (main, last) = refs[:-2], refs[-2:]
    volume = 1.0 / float(s.cells) ** 3
    core = lax.axis_index("fft")

    def put(ref, at, value):
        for channel in range(s.channels):
            lanes = slice(channel * s.size, (channel + 1) * s.size)
            ref[at:at + value.shape[0], lanes] = (value[:, lanes] * (weight[channel] * volume)).astype(BF16)

    for start in range(0, s.own, per):
        rows = [x_rows(s, cuts, own, others, plane) for plane in range(start, start + per)]
        if start == 0:
            rows[0], high = unpacked_rows(s, own, others, unpack[core])
            rows.append(high)
        done = dot(jnp.concatenate(rows, axis=0), table[core])
        put(main, start * s.cells, done[:per * s.cells])
        if start == 0:
            put(last, 0, done[per * s.cells:])


def spectrum(s, t, weight, own, others, cuts, per=4):
    width = s.channels * s.size
    vmem = pl.BlockSpec(memory_space=pltpu.VMEM)
    return pl.pallas_call(
        partial(spectrum_kernel, s, cuts, per),
        in_specs=[pl.BlockSpec(memory_space=pltpu.SMEM)] + [vmem] * (3 + len(others)),
        out_specs=[vmem] * 2,
        out_shape=[jax.ShapeDtypeStruct((s.own * s.cells, width), BF16), jax.ShapeDtypeStruct((s.cells, width), BF16)],
        compiler_params=params(),
        cost_estimate=COST,
    )(weight, t["x_forward"], t["unpack"], own, *others)


def cross_kernel(s, cuts, planes, per, table, unpack, x_inverse, y_inverse, *refs):
    poses, tops = refs[:LIG_STEPS], refs[LIG_STEPS:2 * LIG_STEPS]
    own, others = refs[2 * LIG_STEPS], refs[2 * LIG_STEPS + 1:-2]
    keep, send = refs[-2:]
    cells, width, lanes = s.cells, s.size, s.back
    core = lax.axis_index("fft")
    lane = lax.broadcasted_iota(jnp.int32, (cells, width), 1)
    is_real = lane < cells
    kept = lax.broadcasted_iota(jnp.int32, (cells // 2, lanes), 1) < lanes // 2

    def correlate(receptor, pose):
        straight = None
        for channel in range(s.channels):
            here = slice(channel * width, (channel + 1) * width)
            one = receptor[:, here]
            two = pose[:, here].astype(F32)
            terms = (one * two, pltpu.roll(one, cells, 1) * two)
            straight = terms if straight is None else (straight[0] + terms[0], straight[1] + terms[1])
        same, turned = straight
        return jnp.where(is_real, same + pltpu.roll(same, cells, 1), pltpu.roll(turned, cells, 1) - turned)

    for start in range(planes[0], planes[1], per):
        rows = [x_rows(s, cuts, own, others, plane) for plane in range(start, start + per)]
        if start == 0:
            rows[0], high = unpacked_rows(s, own, others, unpack[core])
            rows.append(high)
        done = dot(jnp.concatenate(rows, axis=0), table[core])
        cross = []
        for k in range(per):
            both = []
            for pose in range(LIG_STEPS):
                at = (start + k) * cells
                value = correlate(done[k * cells:(k + 1) * cells], poses[pose][at:at + cells, :])
                if start + k == 0:
                    row = lax.broadcasted_iota(jnp.int32, (cells, width), 0)
                    at_zero = (row == 0) & ((lane == 0) | (lane == cells)) & (core == 0)
                    value = jnp.where(at_zero, 0.0, value)
                    top = pltpu.roll(correlate(done[per * cells:], tops[pose][...]), cells, 1)
                    value = value + jnp.where(is_real, -top, top)
                both.append(value.astype(BF16))
            cross.append(jnp.concatenate(both, axis=1))
        back = dot(jnp.concatenate(cross, axis=0), x_inverse[core]).astype(BF16)
        for pair in range(0, per, 2):
            sides = []
            for k in range(2):
                here = back[(pair + k) * cells:(pair + k + 1) * cells]
                sides.append(jnp.concatenate([here[:, :lanes], here[:, lanes:]], axis=0))
            out = dot(y_inverse[...], jnp.concatenate(sides, axis=1))
            for k in range(2):
                for q in range(2):
                    value = out[q * cells:(q + 1) * cells, k * lanes:(k + 1) * lanes]
                    low, high = value[:cells // 2], value[cells // 2:]
                    at = (start - planes[0] + pair + k) * cells + q * cells // 2
                    at = slice(at, at + cells // 2)
                    keep[at, :] = jnp.where(kept, low, pltpu.roll(high, lanes // 2, 1)).astype(BF16)
                    send[at, :] = jnp.where(kept, pltpu.roll(low, lanes // 2, 1), high).astype(BF16)


def cross_back(s, t, own, others, poses, tops, cuts, planes, per=4):
    vmem = pl.BlockSpec(memory_space=pltpu.VMEM)
    shape = jax.ShapeDtypeStruct(((planes[1] - planes[0]) * s.cells, s.back), BF16)
    used = range(place(cuts, planes[0]), place(cuts, planes[1] - 1) + 1)
    others, cuts = [others[k] for k in used], tuple(cuts[used[0]:used[-1] + 2])
    operands = [t["x_forward"], t["unpack"], t["x_inverse"], t["y_inverse"], *poses, *tops, own, *others]
    return pl.pallas_call(
        partial(cross_kernel, s, cuts, planes, per),
        in_specs=[vmem] * len(operands),
        out_specs=[vmem] * 2,
        out_shape=[shape] * 2,
        compiler_params=params(),
        cost_estimate=COST,
    )(*operands)


def peak_kernel(s, count, last, load, table, *refs):
    parts = refs[:count]
    earlier, out, held = refs[count:-2], refs[-2], refs[-1]
    cells = s.cells
    low = cells // 2
    core = lax.axis_index("fft")
    at = 0
    for part in parts:
        held[at:at + part.shape[0], :] = part[...].astype(F32)
        at += part.shape[0]
    best = None
    for pair in range(0, low, 2):
        columns = [held[pl.ds(pair + k, cells, stride=low), :] for k in range(2)]
        scores = dot(table[core], jnp.concatenate(columns, axis=1).astype(BF16))
        here = jnp.maximum(scores[:, :s.back], scores[:, s.back:])
        best = here if best is None else jnp.maximum(best, here)
    row = jnp.max(best, axis=0, keepdims=True)
    row = jnp.maximum(row, pltpu.roll(row, s.back // 2, 1)) * (1.0 / (cells * math.sqrt(cells)))
    plane = lax.broadcasted_iota(jnp.int32, row.shape, 1) % s.slab + core * s.slab
    extent = load[s.own * s.size:s.own * s.size + 1, :].astype(F32)
    row = jnp.where(plane.astype(F32) < extent, row, 0.0)
    if not last:
        out[...] = row
        return
    for index, value in enumerate([ref[...] for ref in earlier] + [row]):
        for pose in range(LIG_STEPS):
            out[0, index, pose:pose + 1, :] = value[:, pose * s.slab:(pose + 1) * s.slab]


def peaks(s, t, load, parts, earlier, last):
    vmem = pl.BlockSpec(memory_space=pltpu.VMEM)
    shape = (1, REC_STEPS, LIG_STEPS, s.slab) if last else (1, s.back)
    return pl.pallas_call(
        partial(peak_kernel, s, len(parts), last),
        in_specs=[vmem] * (2 + len(parts) + len(earlier)),
        out_specs=vmem,
        out_shape=jax.ShapeDtypeStruct(shape, F32),
        scratch_shapes=[pltpu.VMEM((s.cells * s.cells // 2, s.back), F32)],
        compiler_params=params(),
        cost_estimate=COST,
    )(load, t["z_inverse"], *parts, *earlier)


def passed_along(value, axis, steps=1):
    count = lax.axis_size(axis)
    return lax.ppermute(value, axis, [(source, (source + steps) % count) for source in range(count)])


def passed_across(value, axis):
    count, cores = lax.axis_size(axis), lax.axis_size("fft")
    pairs = [
        (place * cores + core, (place + 1) % count * cores + (core + 1) % cores)
        for place in range(count)
        for core in range(cores)
    ]
    return lax.ppermute(value, (axis, "fft"), pairs)


def after(value, *others):
    return lax.optimization_barrier((value, *others))[0]


def shards(tables, receptor_occupancy, ligand_occupancy, rot_index, receptor_extent, channel_weight):
    _, channels, slab, plane = receptor_occupancy.shape
    s = Sizes(channels, slab, plane, lax.axis_size("fft"))
    t = tables(s)
    swapped = lambda parts: [passed_along(part, "fft") for part in parts]

    own, *away = sections(s, t, receptor_occupancy, receptor_extent, False, s.whole)
    others = swapped(away)
    receptors = [(own, others)]
    receptors.append((passed_along(own, "rec"), [passed_across(part, "rec") for part in away]))

    ligand_occupancy = after(ligand_occupancy, *others)
    pose, *pose_away = sections(s, t, ligand_occupancy, rot_index, True, s.whole)
    pose_others = swapped(pose_away)
    next_pose, next_others = passed_along(pose, "lig"), [passed_across(part, "lig") for part in pose_away]
    spectra = [spectrum(s, t, channel_weight, pose, pose_others, s.whole)]

    own, others = receptors[1]
    own = after(own, spectra[0][0])
    receptors[1] = (own, others)
    cuts = [others[0][low * s.size:high * s.size] for low, high in zip(s.parts, s.parts[1:])]
    receptors.append((passed_along(own, "rec"), [passed_along(part, "rec") for part in cuts]))

    spectra.append(spectrum(s, t, channel_weight, next_pose, next_others, s.whole))
    poses, tops = [main for main, _ in spectra], [top for _, top in spectra]

    rows = []
    for step, (own, others) in enumerate(receptors):
        last = step + 1 == REC_STEPS
        cuts = s.parts if last else s.whole
        ranges = list(zip(cuts, cuts[1:]))
        if last:
            own = after(own, *rows)
        sides = [cross_back(s, t, own, others, poses, tops, cuts, planes) for planes in ranges]
        parts = [keep for keep, _ in sides] + swapped([send for _, send in sides])
        rows.append(peaks(s, t, own, parts, rows if last else [], last))
    return rows[-1]


def solution(mesh):
    placed = (
        P(("groups", "rec", "lig"), None, "fft", None),
        P(("groups", "rec", "lig"), None, "fft", None),
        P(("groups", "rec", "lig")),
        P(("groups", "rec", "lig")),
        P(),
    )
    tables = lambda s: build_tables(s.cells, s.channels, s.slab, s.cores)
    return jax.shard_map(
        partial(shards, tables),
        mesh=mesh,
        in_specs=placed,
        out_specs=P(("groups", "rec", "lig"), None, None, "fft"),
        check_vma=False,
    )
```

```python
from functools import partial
import math

import jax
import jax.numpy as jnp
import ml_dtypes
import numpy as np
from jax import lax
from jax.experimental import pallas as pl
from jax.experimental.pallas import tpu as pltpu
from jax.sharding import PartitionSpec as P

REC_STEPS = 3
LIG_STEPS = 2
MIB = 1024 * 1024
F32 = jnp.float32
BF16 = jnp.bfloat16


def trig(cells):
    phases = np.arange(cells)[:, None] * np.arange(cells)[None, :] % cells
    angles = phases * (2.0 * math.pi / cells)
    pair = []
    for table in (np.cos(angles), np.sin(angles)):
        table = np.where(np.abs(table) < 1e-9, 0.0, table)
        pair.append(table.astype(np.float32).astype(ml_dtypes.bfloat16).astype(np.float32))
    return pair


def complex_rows(real, imag):
    return np.block([[real, -imag], [imag, real]])


def build_tables(cells, channels, slab, cores):
    cosine, sine = trig(cells)
    half = cells // 2
    own = half // cores
    sign = np.where(np.arange(cells) % 2 == 0, 1.0, -1.0).astype(np.float32)
    tables = {}

    def half_rows(core):
        order = [(core + turn) % cores * own + j for turn in range(cores) for j in range(own)]
        real = cosine[order].copy()
        imag = -sine[order]
        imag[order.index(0)] = sign
        return np.concatenate([real, imag], axis=0)

    def half_mix(core):
        order = [(core + turn) % cores * own + j for turn in range(cores) for j in range(own)]
        top = np.concatenate([cosine[order], sine[order]], axis=1)
        low = np.concatenate([-sine[order], cosine[order]], axis=1)
        at = order.index(0)
        one = np.ones(cells, np.float32)
        top[at] = np.concatenate([one, -sign])
        low[at] = np.concatenate([sign, one])
        return np.concatenate([top, low], axis=0)

    def flips(table, width):
        blocks = table.reshape(table.shape[0], -1, width)
        return np.stack([table, blocks[:, :, ::-1].reshape(table.shape)])

    two = np.eye(2, dtype=np.float32)
    full_rows = np.concatenate([cosine, -sine], axis=0)
    forward = complex_rows(cosine, -sine)
    inverse = complex_rows(cosine, sine)
    tables["z_even"] = np.stack([flips(np.kron(two, half_rows(core)), cells) for core in range(cores)], axis=1)
    tables["y_even"] = flips(forward, cells)
    tables["y_odd"] = flips(np.kron(two, full_rows), cells)
    tables["z_odd"] = np.stack([flips(half_mix(core), cells) for core in range(cores)], axis=1)

    group = channels // 2
    spread = []
    for core in range(cores):
        block = np.zeros((cores, 2, group, slab, 2, group, cells), np.float32)
        for turn in range(cores):
            start = (core + turn) % cores * slab
            mix = forward.reshape(2, cells, 2, cells)[:, :, :, start:start + slab]
            for channel in range(group):
                block[turn, :, channel, :, :, channel] = mix.transpose(2, 3, 0, 1)
        spread.append(block.reshape(cores * 2 * group * slab, 2 * group * cells))
    tables["x_forward"] = np.stack(spread)

    mirror = np.zeros((cells, cells), np.float32)
    mirror[np.arange(cells), -np.arange(cells) % cells] = 1.0
    eye = np.eye(cells, dtype=np.float32)
    none = np.zeros((cells, cells), np.float32)
    low = 0.5 * np.block([[eye + mirror, none], [none, eye - mirror]])
    high = 0.5 * np.block([[none, eye + mirror], [mirror - eye, none]])
    plain = np.eye(2 * cells, dtype=np.float32)
    tables["unpack"] = np.stack(
        [np.concatenate([low, high] if core == 0 else [plain, 0.0 * plain], axis=0) for core in range(cores)]
    )

    back = []
    for core in range(cores):
        block = np.zeros((LIG_STEPS, 2, cells, 2, cores, LIG_STEPS, slab), np.float32)
        parts = inverse.reshape(2, cells, 2, cells)
        for turn in range(cores):
            start = (core + turn) % cores * slab
            for pose in range(LIG_STEPS):
                block[pose, :, :, :, turn, pose] = parts[:, start:start + slab].transpose(2, 3, 0, 1)
        back.append(block.reshape(LIG_STEPS * 2 * cells, 2 * cores * LIG_STEPS * slab))
    tables["x_inverse"] = np.stack(back)
    tables["y_inverse"] = inverse

    last = []
    for core in range(cores):
        order = [(core + turn) % cores * own + j for turn in range(cores) for j in range(own)]
        real = 2.0 * cosine[order]
        imag = -2.0 * sine[order]
        at = order.index(0)
        real[at] = 1.0
        imag[at] = sign
        last.append(np.stack([real, imag], axis=1).reshape(2 * half, cells).T)
    tables["z_inverse"] = np.stack(last)
    return {name: jnp.asarray(table.astype(ml_dtypes.bfloat16)) for name, table in tables.items()}


COST = pl.CostEstimate(flops=1000, bytes_accessed=1000, transcendentals=0)


def params(limit=24):
    return pltpu.CompilerParams(vmem_limit_bytes=limit * MIB)


def lines(value):
    return value.astype(F32).astype(BF16)


def dot(left, right):
    return jnp.dot(left, right, preferred_element_type=F32)


def dot_lanes(left, right):
    return lax.dot_general(left, right, (((1,), (1,)), ((), ())), preferred_element_type=F32)


def place(cuts, plane):
    return max(k for k in range(len(cuts) - 1) if cuts[k] <= plane)


class Sizes:
    def __init__(self, channels, slab, plane, cores):
        self.channels, self.slab, self.cores = channels, slab, cores
        self.cells = slab * cores
        self.lanes = channels * slab
        self.fold = self.lanes // self.cells
        self.tiles = plane // self.lanes
        self.own = self.cells // 2 // cores
        self.whole = (0, self.own)
        self.parts = (0, self.own * 3 // 4, self.own)
        self.size = 2 * self.cells
        self.extra = 16
        self.back = cores * LIG_STEPS * slab


def section_kernel(s, pieces, rotated, cuts, occ, scalar, *refs):
    cells, lanes = s.cells, s.lanes
    half, size = cells // 2, s.size
    count = 4 if rotated else 2
    hbm, refs = refs[:count], refs[count:]
    outs, refs = refs[:len(cuts)], refs[len(cuts):]
    small, buffer, held = refs[:3]
    tables = refs[3:3 + count]
    turned = refs[-2] if rotated else None
    sems = refs[-1]
    core = lax.axis_index("fft")

    first = pltpu.make_async_copy(scalar, small, sems.at[0])
    first.start()
    if rotated:
        first.wait()
        turns = small[0]
        is_odd = turns % 2 == 1
        picks = (
            hbm[0].at[turns // 2, core],
            hbm[1].at[turns // 2],
            hbm[2].at[jnp.where(turns == 1, 1, 0)],
            hbm[3].at[jnp.where(turns == 3, 1, 0), core],
        )
    else:
        picks = (hbm[0].at[0, core], hbm[1].at[0])
    loads = [pltpu.make_async_copy(pick, table, sems.at[1 + k]) for k, (pick, table) in enumerate(zip(picks, tables))]
    width = s.tiles // pieces * lanes
    for k in range(pieces):
        here = slice(k * width, (k + 1) * width)
        loads.append(pltpu.make_async_copy(occ.at[0, :, :, here], buffer.at[:, :, here], sems.at[1 + count + k]))
    for load in loads:
        load.start()
    for load in loads[:count]:
        load.wait()

    def lay(table, height, step):
        for tile in range(0, s.tiles, 2):
            if tile % (s.tiles // pieces) == 0:
                loads[count + tile * pieces // s.tiles].wait()
            rows = [
                lines(buffer[:, :, (tile + k) * lanes:(tile + k + 1) * lanes].reshape(lanes, lanes)) for k in range(2)
            ]
            done = dot_lanes(table[...], jnp.concatenate(rows, axis=0))
            for k in range(2):
                for fold in range(s.fold):
                    at = ((tile + k) * s.fold + fold) * step
                    held[at:at + height, :] = done[fold * height:(fold + 1) * height, k * lanes:(k + 1) * lanes]

    def column(ref, at, step):
        return ref[pl.ds(at, cells, stride=step), :]

    def put(index, value):
        group, plane = divmod(index, s.own)
        if group == 0:
            outs[0][plane * size:(plane + 1) * size, :] = value
            return
        cut = place(cuts, plane)
        plane -= cuts[cut]
        outs[1 + cut][plane * size:(plane + 1) * size, :] = value

    def even():
        step = cells + 8
        lay(tables[0], cells, step)
        for pair in range(0, half, 2):
            rows = [
                jnp.concatenate([column(held, q * half + pair + k, step) for q in range(2)], axis=0) for k in range(2)
            ]
            done = dot(tables[1][...], jnp.concatenate(rows, axis=1).astype(BF16)).astype(BF16)
            for k in range(2):
                put(pair + k, done[:, k * lanes:(k + 1) * lanes])

    def odd():
        step, short = size + 8, cells + 8
        lay(tables[2], size, step)
        for pair in range(0, cells, 2):
            rows = [
                jnp.concatenate([column(held, q * cells + pair + k, step) for q in range(2)], axis=0) for k in range(2)
            ]
            done = dot(tables[3][...], jnp.concatenate(rows, axis=1).astype(BF16))
            for k in range(2):
                turned[(pair + k) * short:(pair + k) * short + cells, :] = done[:, k * lanes:(k + 1) * lanes]
        for plane in range(half):
            both = [column(turned, q * half + plane, short) for q in range(2)]
            put(plane, jnp.concatenate(both, axis=0).astype(BF16))

    if rotated:
        pl.when(jnp.logical_not(is_odd))(even)
        pl.when(is_odd)(odd)
    else:
        even()
        first.wait()
        outs[0][s.own * size:, :] = jnp.full((s.extra, lanes), small[0].astype(F32)).astype(BF16)


def sections(s, t, occ, scalar, rotated, cuts, pieces=2):
    cells, lanes = s.cells, s.lanes
    names = ["z_even", "y_even"] + (["y_odd", "z_odd"] if rotated else [])
    hbm = pl.BlockSpec(memory_space=pltpu.HBM)
    pin = lambda value: pltpu.with_memory_space_constraint(value, pltpu.HBM)
    scratch = [
        pltpu.SMEM(scalar.shape, jnp.int32),
        pltpu.VMEM(occ.shape[1:], jnp.int32),
        pltpu.VMEM((cells * ((s.size if rotated else cells) + 8), lanes), F32),
    ]
    scratch += [pltpu.VMEM(t[name].shape[-2:], BF16) for name in names]
    if rotated:
        scratch.append(pltpu.VMEM((cells * (cells + 8), lanes), F32))
    scratch.append(pltpu.SemaphoreType.DMA((1 + len(names) + pieces,)))
    rows = [s.own * s.size + (0 if rotated else s.extra)]
    rows += [(high - low) * s.size for low, high in zip(cuts, cuts[1:])]
    return pl.pallas_call(
        partial(section_kernel, s, pieces, rotated, cuts),
        in_specs=[hbm, pl.BlockSpec(memory_space=pl.ANY)] + [hbm] * len(names),
        out_specs=[pl.BlockSpec(memory_space=pltpu.VMEM)] * len(rows),
        out_shape=[jax.ShapeDtypeStruct((count, lanes), BF16) for count in rows],
        scratch_shapes=scratch,
        compiler_params=params(),
        cost_estimate=COST,
    )(pin(occ), scalar, *[pin(t[name]) for name in names])


def regroup(s, parts):
    half = s.lanes // 2
    lane = lax.broadcasted_iota(jnp.int32, parts[0].shape, 1)
    low, high = [], []
    for one, two in zip(parts[::2], parts[1::2]):
        low.append(jnp.where(lane < half, one, pltpu.roll(two, half, 1)))
        high.append(jnp.where(lane < half, pltpu.roll(one, half, 1), two))
    return [jnp.concatenate(low, axis=1), jnp.concatenate(high, axis=1)]


def x_rows(s, cuts, own, others, plane):
    cut = place(cuts, plane)
    parts = []
    for ref, at in ((own, plane * s.size), (others[cut], (plane - cuts[cut]) * s.size)):
        for p in range(2):
            parts.append(ref[at + p * s.cells:at + (p + 1) * s.cells, :])
    return regroup(s, parts)


def unpacked_rows(s, own, others, unpack):
    cells = s.cells
    done = [dot(unpack, ref[:s.size, :]).astype(BF16) for ref in (own, others[0])]
    return [
        regroup(s, [value[(2 * k + p) * cells:(2 * k + p + 1) * cells] for value in done for p in range(2)])
        for k in range(2)
    ]


def x_transform(s, rows, table):
    done = dot(jnp.concatenate([row[k] for k in range(2) for row in rows], axis=0), table)
    count = len(rows) * s.cells
    return done[:count], done[count:]


def spectrum_kernel(s, cuts, per, weight, table, unpack, own, *refs):
    others, (main, last) = refs[:-2], refs[-2:]
    volume = 1.0 / float(s.cells) ** 3
    core = lax.axis_index("fft")

    lane = lax.broadcasted_iota(jnp.int32, (s.cells, s.size), 1)
    scales = [
        jnp.where(lane < s.cells, weight[2 * k], weight[2 * k + 1]) * volume for k in range(2)
    ]

    def put(ref, at, values):
        for k, value in enumerate(values):
            for q in range(2):
                from_lanes = slice(q * s.size, (q + 1) * s.size)
                to_lanes = slice((2 * k + q) * s.size, (2 * k + q + 1) * s.size)
                for row in range(0, value.shape[0], s.cells):
                    ref[at + row:at + row + s.cells, to_lanes] = (
                        value[row:row + s.cells, from_lanes] * scales[k]
                    ).astype(BF16)

    for start in range(0, s.own, per):
        rows = [x_rows(s, cuts, own, others, plane) for plane in range(start, start + per)]
        if start == 0:
            rows[0], high = unpacked_rows(s, own, others, unpack[core])
            rows.append(high)
        done = x_transform(s, rows, table[core])
        put(main, start * s.cells, [value[:per * s.cells] for value in done])
        if start == 0:
            put(last, 0, [value[per * s.cells:] for value in done])


def spectrum(s, t, weight, own, others, cuts, per=4):
    width = s.channels * s.size
    vmem = pl.BlockSpec(memory_space=pltpu.VMEM)
    return pl.pallas_call(
        partial(spectrum_kernel, s, cuts, per),
        in_specs=[pl.BlockSpec(memory_space=pltpu.SMEM)] + [vmem] * (3 + len(others)),
        out_specs=[vmem] * 2,
        out_shape=[jax.ShapeDtypeStruct((s.own * s.cells, width), BF16), jax.ShapeDtypeStruct((s.cells, width), BF16)],
        compiler_params=params(),
        cost_estimate=COST,
    )(weight, t["x_forward"], t["unpack"], own, *others)


def cross_kernel(s, cuts, planes, most, table, unpack, x_inverse, y_inverse, *refs):
    poses, tops = refs[:LIG_STEPS], refs[LIG_STEPS:2 * LIG_STEPS]
    own, others = refs[2 * LIG_STEPS], refs[2 * LIG_STEPS + 1:-2]
    keep, send = refs[-2:]
    cells, width, lanes = s.cells, s.size, s.back
    core = lax.axis_index("fft")
    lane = lax.broadcasted_iota(jnp.int32, (cells, width), 1)
    is_real = lane < cells
    kept = lax.broadcasted_iota(jnp.int32, (cells // 2, lanes), 1) < lanes // 2

    def correlate(receptor, pose):
        real = imag = None
        for k, value in enumerate(receptor):
            one = [value[:, q * width:(q + 1) * width] for q in range(2)]
            two = [pose[:, (2 * k + q) * width:(2 * k + q + 1) * width].astype(F32) for q in range(2)]
            same = one[0] * two[0] + one[1] * two[1]
            turned = one[1] * two[0] - one[0] * two[1]
            real = same if real is None else real + same
            imag = turned if imag is None else imag + turned
        return jnp.where(is_real, real, imag) + pltpu.roll(jnp.where(is_real, imag, real), cells, 1)

    for start in range(planes[0], planes[1], most):
        per = min(most, planes[1] - start)
        rows = [x_rows(s, cuts, own, others, plane) for plane in range(start, start + per)]
        if start == 0:
            rows[0], high = unpacked_rows(s, own, others, unpack[core])
            rows.append(high)
        done = x_transform(s, rows, table[core])
        cross = []
        for k in range(per):
            both = []
            for pose in range(LIG_STEPS):
                at = (start + k) * cells
                value = correlate([half[k * cells:(k + 1) * cells] for half in done], poses[pose][at:at + cells, :])
                if start + k == 0:
                    row = lax.broadcasted_iota(jnp.int32, (cells, width), 0)
                    at_zero = (row == 0) & ((lane == 0) | (lane == cells)) & (core == 0)
                    value = jnp.where(at_zero, 0.0, value)
                    top = pltpu.roll(correlate([half[per * cells:] for half in done], tops[pose][...]), cells, 1)
                    value = value + jnp.where(is_real, -top, top)
                both.append(value.astype(BF16))
            cross.append(jnp.concatenate(both, axis=1))
        back = dot(jnp.concatenate(cross, axis=0), x_inverse[core]).astype(BF16)
        for pair in range(0, per, 2):
            sides = []
            for k in range(2):
                here = back[(pair + k) * cells:(pair + k + 1) * cells]
                sides.append(jnp.concatenate([here[:, :lanes], here[:, lanes:]], axis=0))
            out = dot(y_inverse[...], jnp.concatenate(sides, axis=1))
            for k in range(2):
                for q in range(2):
                    value = out[q * cells:(q + 1) * cells, k * lanes:(k + 1) * lanes]
                    low, high = value[:cells // 2], value[cells // 2:]
                    at = (start - planes[0] + pair + k) * cells + q * cells // 2
                    at = slice(at, at + cells // 2)
                    keep[at, :] = jnp.where(kept, low, pltpu.roll(high, lanes // 2, 1)).astype(BF16)
                    send[at, :] = jnp.where(kept, pltpu.roll(low, lanes // 2, 1), high).astype(BF16)


def cross_back(s, t, own, others, poses, tops, cuts, planes, per=4):
    vmem = pl.BlockSpec(memory_space=pltpu.VMEM)
    shape = jax.ShapeDtypeStruct(((planes[1] - planes[0]) * s.cells, s.back), BF16)
    used = range(place(cuts, planes[0]), place(cuts, planes[1] - 1) + 1)
    others, cuts = [others[k] for k in used], tuple(cuts[used[0]:used[-1] + 2])
    operands = [t["x_forward"], t["unpack"], t["x_inverse"], t["y_inverse"], *poses, *tops, own, *others]
    return pl.pallas_call(
        partial(cross_kernel, s, cuts, planes, per),
        in_specs=[vmem] * len(operands),
        out_specs=[vmem] * 2,
        out_shape=[shape] * 2,
        compiler_params=params(),
        cost_estimate=COST,
    )(*operands)


def peak_kernel(s, count, last, load, table, *refs):
    parts = refs[:count]
    earlier, out, held = refs[count:-2], refs[-2], refs[-1]
    cells = s.cells
    low = cells // 2
    core = lax.axis_index("fft")
    step = low + 8
    at = 0
    for part in parts:
        for row in range(0, part.shape[0], low):
            held[at:at + low, :] = part[row:row + low, :].astype(F32)
            at += step
    best = None
    for pair in range(0, low, 2):
        columns = [held[pl.ds(pair + k, cells, stride=step), :] for k in range(2)]
        scores = dot(table[core], jnp.concatenate(columns, axis=1).astype(BF16))
        here = jnp.maximum(scores[:, :s.back], scores[:, s.back:])
        best = here if best is None else jnp.maximum(best, here)
    row = jnp.max(best, axis=0, keepdims=True)
    row = jnp.maximum(row, pltpu.roll(row, s.back // 2, 1)) * (1.0 / (cells * math.sqrt(cells)))
    plane = lax.broadcasted_iota(jnp.int32, row.shape, 1) % s.slab + core * s.slab
    extent = load[s.own * s.size:s.own * s.size + 1, :].astype(F32)
    row = jnp.where(plane.astype(F32) < extent, row, 0.0)
    if not last:
        out[...] = row
        return
    for index, value in enumerate([ref[...] for ref in earlier] + [row]):
        for pose in range(LIG_STEPS):
            out[0, index, pose:pose + 1, :] = value[:, pose * s.slab:(pose + 1) * s.slab]


def peaks(s, t, load, parts, earlier, last):
    vmem = pl.BlockSpec(memory_space=pltpu.VMEM)
    shape = (1, REC_STEPS, LIG_STEPS, s.slab) if last else (1, s.back)
    return pl.pallas_call(
        partial(peak_kernel, s, len(parts), last),
        in_specs=[vmem] * (2 + len(parts) + len(earlier)),
        out_specs=vmem,
        out_shape=jax.ShapeDtypeStruct(shape, F32),
        scratch_shapes=[pltpu.VMEM((s.cells * (s.cells // 2 + 8), s.back), F32)],
        compiler_params=params(),
        cost_estimate=COST,
    )(load, t["z_inverse"], *parts, *earlier)


def passed_along(value, axis, steps=1):
    count = lax.axis_size(axis)
    return lax.ppermute(value, axis, [(source, (source + steps) % count) for source in range(count)])


def passed_across(value, axis):
    count, cores = lax.axis_size(axis), lax.axis_size("fft")
    pairs = [
        (place * cores + core, (place + 1) % count * cores + (core + 1) % cores)
        for place in range(count)
        for core in range(cores)
    ]
    return lax.ppermute(value, (axis, "fft"), pairs)


def after(value, *others):
    return lax.optimization_barrier((value, *others))[0]


def shards(tables, receptor_occupancy, ligand_occupancy, rot_index, receptor_extent, channel_weight):
    _, channels, slab, plane = receptor_occupancy.shape
    s = Sizes(channels, slab, plane, lax.axis_size("fft"))
    t = tables(s)
    swapped = lambda parts: [passed_along(part, "fft") for part in parts]

    own, *away = sections(s, t, receptor_occupancy, receptor_extent, False, s.whole)
    others = swapped(away)
    receptors = [(own, others)]
    receptors.append((passed_along(own, "rec"), [passed_across(part, "rec") for part in away]))

    ligand_occupancy = after(ligand_occupancy, *others)
    pose, *pose_away = sections(s, t, ligand_occupancy, rot_index, True, s.whole)
    pose_others = swapped(pose_away)
    next_pose, next_others = passed_along(pose, "lig"), [passed_across(part, "lig") for part in pose_away]
    spectra = [spectrum(s, t, channel_weight, pose, pose_others, s.whole)]

    own, others = receptors[1]
    own = after(own, spectra[0][0])
    receptors[1] = (own, others)
    cuts = [others[0][low * s.size:high * s.size] for low, high in zip(s.parts, s.parts[1:])]
    receptors.append((passed_along(own, "rec"), [passed_along(part, "rec") for part in cuts]))

    spectra.append(spectrum(s, t, channel_weight, next_pose, next_others, s.whole))
    poses, tops = [main for main, _ in spectra], [top for _, top in spectra]

    rows = []
    for step, (own, others) in enumerate(receptors):
        last = step + 1 == REC_STEPS
        cuts = s.parts if last else s.whole
        ranges = list(zip(cuts, cuts[1:]))
        if last:
            own = after(own, *rows)
        sides = [cross_back(s, t, own, others, poses, tops, cuts, planes) for planes in ranges]
        parts = [keep for keep, _ in sides] + swapped([send for _, send in sides])
        rows.append(peaks(s, t, own, parts, rows if last else [], last))
    return rows[-1]


def solution(mesh):
    placed = (
        P(("groups", "rec", "lig"), None, "fft", None),
        P(("groups", "rec", "lig"), None, "fft", None),
        P(("groups", "rec", "lig")),
        P(("groups", "rec", "lig")),
        P(),
    )
    tables = lambda s: build_tables(s.cells, s.channels, s.slab, s.cores)
    return jax.shard_map(
        partial(shards, tables),
        mesh=mesh,
        in_specs=placed,
        out_specs=P(("groups", "rec", "lig"), None, None, "fft"),
        check_vma=False,
    )
```

```python
from functools import partial
import math

import jax
import jax.numpy as jnp
import ml_dtypes
import numpy as np
from jax import lax
from jax.experimental import pallas as pl
from jax.experimental.pallas import tpu as pltpu
from jax.sharding import PartitionSpec as P

REC_STEPS = 3
LIG_STEPS = 2
MIB = 1024 * 1024
F32 = jnp.float32
BF16 = jnp.bfloat16


def trig(cells):
    phases = np.arange(cells)[:, None] * np.arange(cells)[None, :] % cells
    angles = phases * (2.0 * math.pi / cells)
    pair = []
    for table in (np.cos(angles), np.sin(angles)):
        table = np.where(np.abs(table) < 1e-9, 0.0, table)
        pair.append(table.astype(np.float32).astype(ml_dtypes.bfloat16).astype(np.float32))
    return pair


def complex_rows(real, imag):
    return np.block([[real, -imag], [imag, real]])


def build_tables(cells, channels, slab, cores):
    cosine, sine = trig(cells)
    half = cells // 2
    own = half // cores
    sign = np.where(np.arange(cells) % 2 == 0, 1.0, -1.0).astype(np.float32)
    tables = {}

    def half_rows(core):
        order = [(core + turn) % cores * own + j for turn in range(cores) for j in range(own)]
        real = cosine[order].copy()
        imag = -sine[order]
        imag[order.index(0)] = sign
        return np.concatenate([real, imag], axis=0)

    def half_mix(core):
        order = [(core + turn) % cores * own + j for turn in range(cores) for j in range(own)]
        top = np.concatenate([cosine[order], sine[order]], axis=1)
        low = np.concatenate([-sine[order], cosine[order]], axis=1)
        at = order.index(0)
        one = np.ones(cells, np.float32)
        top[at] = np.concatenate([one, -sign])
        low[at] = np.concatenate([sign, one])
        return np.concatenate([top, low], axis=0)

    def flips(table, width):
        blocks = table.reshape(table.shape[0], -1, width)
        return np.stack([table, blocks[:, :, ::-1].reshape(table.shape)])

    two = np.eye(2, dtype=np.float32)
    full_rows = np.concatenate([cosine, -sine], axis=0)
    forward = complex_rows(cosine, -sine)
    inverse = complex_rows(cosine, sine)
    tables["z_even"] = np.stack([flips(np.kron(two, half_rows(core)), cells) for core in range(cores)], axis=1)
    tables["y_even"] = flips(forward, cells)
    tables["y_odd"] = flips(np.kron(two, full_rows), cells)
    tables["z_odd"] = np.stack([flips(half_mix(core), cells) for core in range(cores)], axis=1)

    group = channels // 2
    spread = []
    for core in range(cores):
        block = np.zeros((cores, 2, group, slab, 2, group, cells), np.float32)
        for turn in range(cores):
            start = (core + turn) % cores * slab
            mix = forward.reshape(2, cells, 2, cells)[:, :, :, start:start + slab]
            for channel in range(group):
                block[turn, :, channel, :, :, channel] = mix.transpose(2, 3, 0, 1)
        spread.append(block.reshape(cores * 2 * group * slab, 2 * group * cells))
    tables["x_forward"] = np.stack(spread)

    mirror = np.zeros((cells, cells), np.float32)
    mirror[np.arange(cells), -np.arange(cells) % cells] = 1.0
    eye = np.eye(cells, dtype=np.float32)
    none = np.zeros((cells, cells), np.float32)
    low = 0.5 * np.block([[eye + mirror, none], [none, eye - mirror]])
    high = 0.5 * np.block([[none, eye + mirror], [mirror - eye, none]])
    plain = np.eye(2 * cells, dtype=np.float32)
    tables["unpack"] = np.stack(
        [np.concatenate([low, high] if core == 0 else [plain, 0.0 * plain], axis=0) for core in range(cores)]
    )

    back = []
    for core in range(cores):
        block = np.zeros((LIG_STEPS, 2, cells, 2, cores, LIG_STEPS, slab), np.float32)
        parts = inverse.reshape(2, cells, 2, cells)
        for turn in range(cores):
            start = (core + turn) % cores * slab
            for pose in range(LIG_STEPS):
                block[pose, :, :, :, turn, pose] = parts[:, start:start + slab].transpose(2, 3, 0, 1)
        back.append(block.reshape(LIG_STEPS * 2 * cells, 2 * cores * LIG_STEPS * slab))
    tables["x_inverse"] = np.stack(back)
    tables["y_inverse"] = inverse

    last = []
    for core in range(cores):
        order = [(core + turn) % cores * own + j for turn in range(cores) for j in range(own)]
        real = 2.0 * cosine[order]
        imag = -2.0 * sine[order]
        at = order.index(0)
        real[at] = 1.0
        imag[at] = sign
        last.append(np.stack([real, imag], axis=1).reshape(2 * half, cells).T)
    tables["z_inverse"] = np.stack(last)
    return {name: jnp.asarray(table.astype(ml_dtypes.bfloat16)) for name, table in tables.items()}


COST = pl.CostEstimate(flops=1000, bytes_accessed=1000, transcendentals=0)


def params(limit=24):
    return pltpu.CompilerParams(vmem_limit_bytes=limit * MIB)


def lines(value):
    return value.astype(F32).astype(BF16)


def dot(left, right):
    return jnp.dot(left, right, preferred_element_type=F32)


def dot_lanes(left, right):
    return lax.dot_general(left, right, (((1,), (1,)), ((), ())), preferred_element_type=F32)


def place(cuts, plane):
    return max(k for k in range(len(cuts) - 1) if cuts[k] <= plane)


class Sizes:
    def __init__(self, channels, slab, plane, cores):
        self.channels, self.slab, self.cores = channels, slab, cores
        self.cells = slab * cores
        self.lanes = channels * slab
        self.fold = self.lanes // self.cells
        self.tiles = plane // self.lanes
        self.own = self.cells // 2 // cores
        self.whole = (0, self.own)
        self.parts = (0, self.own * 3 // 4, self.own)
        self.size = 2 * self.cells
        self.extra = 16
        self.back = cores * LIG_STEPS * slab


def section_kernel(s, pieces, rotated, cuts, occ, scalar, *refs):
    cells, lanes = s.cells, s.lanes
    half, size = cells // 2, s.size
    count = 4 if rotated else 2
    hbm, refs = refs[:count], refs[count:]
    outs, refs = refs[:len(cuts)], refs[len(cuts):]
    small, buffer, held = refs[:3]
    tables = refs[3:3 + count]
    turned = refs[-2] if rotated else None
    sems = refs[-1]
    core = lax.axis_index("fft")

    first = pltpu.make_async_copy(scalar, small, sems.at[0])
    first.start()
    if rotated:
        first.wait()
        turns = small[0]
        is_odd = turns % 2 == 1
        picks = (
            hbm[0].at[turns // 2, core],
            hbm[1].at[turns // 2],
            hbm[2].at[jnp.where(turns == 1, 1, 0)],
            hbm[3].at[jnp.where(turns == 3, 1, 0), core],
        )
    else:
        picks = (hbm[0].at[0, core], hbm[1].at[0])
    loads = [pltpu.make_async_copy(pick, table, sems.at[1 + k]) for k, (pick, table) in enumerate(zip(picks, tables))]
    width = s.tiles // pieces * lanes
    for k in range(pieces):
        here = slice(k * width, (k + 1) * width)
        loads.append(pltpu.make_async_copy(occ.at[0, :, :, here], buffer.at[:, :, here], sems.at[1 + count + k]))
    for load in loads:
        load.start()
    for load in loads[:count]:
        load.wait()

    def lay(table, height, step):
        for tile in range(0, s.tiles, 2):
            if tile % (s.tiles // pieces) == 0:
                loads[count + tile * pieces // s.tiles].wait()
            rows = [
                lines(buffer[:, :, (tile + k) * lanes:(tile + k + 1) * lanes].reshape(lanes, lanes)) for k in range(2)
            ]
            done = dot_lanes(table[...], jnp.concatenate(rows, axis=0))
            for k in range(2):
                for fold in range(s.fold):
                    at = ((tile + k) * s.fold + fold) * step
                    held[at:at + height, :] = done[fold * height:(fold + 1) * height, k * lanes:(k + 1) * lanes]

    def column(ref, at, step):
        return ref[pl.ds(at, cells, stride=step), :]

    def put(index, value):
        group, plane = divmod(index, s.own)
        if group == 0:
            outs[0][plane * size:(plane + 1) * size, :] = value
            return
        cut = place(cuts, plane)
        plane -= cuts[cut]
        outs[1 + cut][plane * size:(plane + 1) * size, :] = value

    def even():
        step = cells + 8
        lay(tables[0], cells, step)
        for pair in range(0, half, 2):
            rows = [
                jnp.concatenate([column(held, q * half + pair + k, step) for q in range(2)], axis=0) for k in range(2)
            ]
            done = dot(tables[1][...], jnp.concatenate(rows, axis=1).astype(BF16)).astype(BF16)
            for k in range(2):
                put(pair + k, done[:, k * lanes:(k + 1) * lanes])

    def odd():
        step, short = size + 8, cells + 8
        lay(tables[2], size, step)
        for pair in range(0, cells, 2):
            rows = [
                jnp.concatenate([column(held, q * cells + pair + k, step) for q in range(2)], axis=0) for k in range(2)
            ]
            done = dot(tables[3][...], jnp.concatenate(rows, axis=1).astype(BF16))
            for k in range(2):
                turned[(pair + k) * short:(pair + k) * short + cells, :] = done[:, k * lanes:(k + 1) * lanes]
        for plane in range(half):
            both = [column(turned, q * half + plane, short) for q in range(2)]
            put(plane, jnp.concatenate(both, axis=0).astype(BF16))

    if rotated:
        pl.when(jnp.logical_not(is_odd))(even)
        pl.when(is_odd)(odd)
    else:
        even()
        first.wait()
        outs[0][s.own * size:, :] = jnp.full((s.extra, lanes), small[0].astype(F32)).astype(BF16)


def sections(s, t, occ, scalar, rotated, cuts, pieces=2):
    cells, lanes = s.cells, s.lanes
    names = ["z_even", "y_even"] + (["y_odd", "z_odd"] if rotated else [])
    hbm = pl.BlockSpec(memory_space=pltpu.HBM)
    pin = lambda value: pltpu.with_memory_space_constraint(value, pltpu.HBM)
    scratch = [
        pltpu.SMEM(scalar.shape, jnp.int32),
        pltpu.VMEM(occ.shape[1:], jnp.int32),
        pltpu.VMEM(((cells + 1) * ((s.size if rotated else cells) + 8), lanes), F32),
    ]
    scratch += [pltpu.VMEM(t[name].shape[-2:], BF16) for name in names]
    if rotated:
        scratch.append(pltpu.VMEM(((cells + 1) * (cells + 8), lanes), F32))
    scratch.append(pltpu.SemaphoreType.DMA((1 + len(names) + pieces,)))
    rows = [s.own * s.size + (0 if rotated else s.extra)]
    rows += [(high - low) * s.size for low, high in zip(cuts, cuts[1:])]
    return pl.pallas_call(
        partial(section_kernel, s, pieces, rotated, cuts),
        in_specs=[hbm, pl.BlockSpec(memory_space=pl.ANY)] + [hbm] * len(names),
        out_specs=[pl.BlockSpec(memory_space=pltpu.VMEM)] * len(rows),
        out_shape=[jax.ShapeDtypeStruct((count, lanes), BF16) for count in rows],
        scratch_shapes=scratch,
        compiler_params=params(),
        cost_estimate=COST,
    )(pin(occ), scalar, *[pin(t[name]) for name in names])


def regroup(s, parts):
    half = s.lanes // 2
    lane = lax.broadcasted_iota(jnp.int32, parts[0].shape, 1)
    low, high = [], []
    for one, two in zip(parts[::2], parts[1::2]):
        low.append(jnp.where(lane < half, one, pltpu.roll(two, half, 1)))
        high.append(jnp.where(lane < half, pltpu.roll(one, half, 1), two))
    return [jnp.concatenate(low, axis=1), jnp.concatenate(high, axis=1)]


def x_rows(s, cuts, own, others, plane):
    cut = place(cuts, plane)
    parts = []
    for ref, at in ((own, plane * s.size), (others[cut], (plane - cuts[cut]) * s.size)):
        for p in range(2):
            parts.append(ref[at + p * s.cells:at + (p + 1) * s.cells, :])
    return regroup(s, parts)


def unpacked_rows(s, own, others, unpack):
    cells = s.cells
    done = [dot(unpack, ref[:s.size, :]).astype(BF16) for ref in (own, others[0])]
    return [
        regroup(s, [value[(2 * k + p) * cells:(2 * k + p + 1) * cells] for value in done for p in range(2)])
        for k in range(2)
    ]


def x_transform(s, rows, table):
    done = dot(jnp.concatenate([row[k] for k in range(2) for row in rows], axis=0), table)
    count = len(rows) * s.cells
    return done[:count], done[count:]


def spectrum_kernel(s, cuts, per, weight, table, unpack, own, *refs):
    others, (main, last) = refs[:-2], refs[-2:]
    volume = 1.0 / float(s.cells) ** 3
    core = lax.axis_index("fft")

    lane = lax.broadcasted_iota(jnp.int32, (s.cells, s.size), 1)
    scales = [
        jnp.where(lane < s.cells, weight[2 * k], weight[2 * k + 1]) * volume for k in range(2)
    ]

    def put(ref, at, values):
        for k, value in enumerate(values):
            for q in range(2):
                from_lanes = slice(q * s.size, (q + 1) * s.size)
                to_lanes = slice((2 * k + q) * s.size, (2 * k + q + 1) * s.size)
                for row in range(0, value.shape[0], s.cells):
                    ref[at + row:at + row + s.cells, to_lanes] = (
                        value[row:row + s.cells, from_lanes] * scales[k]
                    ).astype(BF16)

    for start in range(0, s.own, per):
        rows = [x_rows(s, cuts, own, others, plane) for plane in range(start, start + per)]
        if start == 0:
            rows[0], high = unpacked_rows(s, own, others, unpack[core])
            rows.append(high)
        done = x_transform(s, rows, table[core])
        put(main, start * s.cells, [value[:per * s.cells] for value in done])
        if start == 0:
            put(last, 0, [value[per * s.cells:] for value in done])


def spectrum(s, t, weight, own, others, cuts, per=4):
    width = s.channels * s.size
    vmem = pl.BlockSpec(memory_space=pltpu.VMEM)
    return pl.pallas_call(
        partial(spectrum_kernel, s, cuts, per),
        in_specs=[pl.BlockSpec(memory_space=pltpu.SMEM)] + [vmem] * (3 + len(others)),
        out_specs=[vmem] * 2,
        out_shape=[jax.ShapeDtypeStruct((s.own * s.cells, width), BF16), jax.ShapeDtypeStruct((s.cells, width), BF16)],
        compiler_params=params(),
        cost_estimate=COST,
    )(weight, t["x_forward"], t["unpack"], own, *others)


def cross_kernel(s, cuts, planes, most, table, unpack, x_inverse, y_inverse, *refs):
    poses, tops = refs[:LIG_STEPS], refs[LIG_STEPS:2 * LIG_STEPS]
    own, others = refs[2 * LIG_STEPS], refs[2 * LIG_STEPS + 1:-2]
    keep, send = refs[-2:]
    cells, width, lanes = s.cells, s.size, s.back
    core = lax.axis_index("fft")
    lane = lax.broadcasted_iota(jnp.int32, (cells, width), 1)
    is_real = lane < cells
    kept = lax.broadcasted_iota(jnp.int32, (cells // 2, lanes), 1) < lanes // 2

    def correlate(receptor, pose):
        real = imag = None
        for k, value in enumerate(receptor):
            one = [value[:, q * width:(q + 1) * width] for q in range(2)]
            two = [pose[:, (2 * k + q) * width:(2 * k + q + 1) * width].astype(F32) for q in range(2)]
            same = one[0] * two[0] + one[1] * two[1]
            turned = one[1] * two[0] - one[0] * two[1]
            real = same if real is None else real + same
            imag = turned if imag is None else imag + turned
        return jnp.where(is_real, real, imag) + pltpu.roll(jnp.where(is_real, imag, real), cells, 1)

    for start in range(planes[0], planes[1], most):
        per = min(most, planes[1] - start)
        rows = [x_rows(s, cuts, own, others, plane) for plane in range(start, start + per)]
        if start == 0:
            rows[0], high = unpacked_rows(s, own, others, unpack[core])
            rows.append(high)
        done = x_transform(s, rows, table[core])
        cross = []
        for k in range(per):
            both = []
            for pose in range(LIG_STEPS):
                at = (start + k) * cells
                value = correlate([half[k * cells:(k + 1) * cells] for half in done], poses[pose][at:at + cells, :])
                if start + k == 0:
                    row = lax.broadcasted_iota(jnp.int32, (cells, width), 0)
                    at_zero = (row == 0) & ((lane == 0) | (lane == cells)) & (core == 0)
                    value = jnp.where(at_zero, 0.0, value)
                    top = pltpu.roll(correlate([half[per * cells:] for half in done], tops[pose][...]), cells, 1)
                    value = value + jnp.where(is_real, -top, top)
                both.append(value.astype(BF16))
            cross.append(jnp.concatenate(both, axis=1))
        back = dot(jnp.concatenate(cross, axis=0), x_inverse[core]).astype(BF16)
        for pair in range(0, per, 2):
            sides = []
            for k in range(2):
                here = back[(pair + k) * cells:(pair + k + 1) * cells]
                sides.append(jnp.concatenate([here[:, :lanes], here[:, lanes:]], axis=0))
            out = dot(y_inverse[...], jnp.concatenate(sides, axis=1))
            for k in range(2):
                for q in range(2):
                    value = out[q * cells:(q + 1) * cells, k * lanes:(k + 1) * lanes]
                    low, high = value[:cells // 2], value[cells // 2:]
                    at = (start - planes[0] + pair + k) * cells + q * cells // 2
                    at = slice(at, at + cells // 2)
                    keep[at, :] = jnp.where(kept, low, pltpu.roll(high, lanes // 2, 1)).astype(BF16)
                    send[at, :] = jnp.where(kept, pltpu.roll(low, lanes // 2, 1), high).astype(BF16)


def cross_back(s, t, own, others, poses, tops, cuts, planes, per=4):
    vmem = pl.BlockSpec(memory_space=pltpu.VMEM)
    shape = jax.ShapeDtypeStruct(((planes[1] - planes[0]) * s.cells, s.back), BF16)
    used = range(place(cuts, planes[0]), place(cuts, planes[1] - 1) + 1)
    others, cuts = [others[k] for k in used], tuple(cuts[used[0]:used[-1] + 2])
    operands = [t["x_forward"], t["unpack"], t["x_inverse"], t["y_inverse"], *poses, *tops, own, *others]
    return pl.pallas_call(
        partial(cross_kernel, s, cuts, planes, per),
        in_specs=[vmem] * len(operands),
        out_specs=[vmem] * 2,
        out_shape=[shape] * 2,
        compiler_params=params(),
        cost_estimate=COST,
    )(*operands)


def peak_kernel(s, count, last, load, table, *refs):
    parts = refs[:count]
    earlier, out, held = refs[count:-2], refs[-2], refs[-1]
    cells = s.cells
    low = cells // 2
    core = lax.axis_index("fft")
    step = low + 8
    at = 0
    for part in parts:
        for row in range(0, part.shape[0], low):
            held[at:at + low, :] = part[row:row + low, :].astype(F32)
            at += step
    best = None
    for pair in range(0, low, 2):
        columns = [held[pl.ds(pair + k, cells, stride=step), :] for k in range(2)]
        scores = dot(table[core], jnp.concatenate(columns, axis=1).astype(BF16))
        here = jnp.maximum(scores[:, :s.back], scores[:, s.back:])
        best = here if best is None else jnp.maximum(best, here)
    row = jnp.max(best, axis=0, keepdims=True)
    row = jnp.maximum(row, pltpu.roll(row, s.back // 2, 1)) * (1.0 / (cells * math.sqrt(cells)))
    plane = lax.broadcasted_iota(jnp.int32, row.shape, 1) % s.slab + core * s.slab
    extent = load[s.own * s.size:, :].astype(F32)[:1]
    row = jnp.where(plane.astype(F32) < extent, row, 0.0)
    if not last:
        out[...] = row
        return
    for index, value in enumerate([ref[...] for ref in earlier] + [row]):
        for pose in range(LIG_STEPS):
            out[0, index, pose:pose + 1, :] = value[:, pose * s.slab:(pose + 1) * s.slab]


def peaks(s, t, load, parts, earlier, last):
    vmem = pl.BlockSpec(memory_space=pltpu.VMEM)
    shape = (1, REC_STEPS, LIG_STEPS, s.slab) if last else (1, s.back)
    return pl.pallas_call(
        partial(peak_kernel, s, len(parts), last),
        in_specs=[vmem] * (2 + len(parts) + len(earlier)),
        out_specs=vmem,
        out_shape=jax.ShapeDtypeStruct(shape, F32),
        scratch_shapes=[pltpu.VMEM(((s.cells + 1) * (s.cells // 2 + 8), s.back), F32)],
        compiler_params=params(),
        cost_estimate=COST,
    )(load, t["z_inverse"], *parts, *earlier)


def passed_along(value, axis, steps=1):
    count = lax.axis_size(axis)
    return lax.ppermute(value, axis, [(source, (source + steps) % count) for source in range(count)])


def passed_across(value, axis):
    count, cores = lax.axis_size(axis), lax.axis_size("fft")
    pairs = [
        (place * cores + core, (place + 1) % count * cores + (core + 1) % cores)
        for place in range(count)
        for core in range(cores)
    ]
    return lax.ppermute(value, (axis, "fft"), pairs)


def after(value, *others):
    return lax.optimization_barrier((value, *others))[0]


def shards(tables, receptor_occupancy, ligand_occupancy, rot_index, receptor_extent, channel_weight):
    _, channels, slab, plane = receptor_occupancy.shape
    s = Sizes(channels, slab, plane, lax.axis_size("fft"))
    t = tables(s)
    swapped = lambda parts: [passed_along(part, "fft") for part in parts]

    own, *away = sections(s, t, receptor_occupancy, receptor_extent, False, s.whole)
    others = swapped(away)
    receptors = [(own, others)]
    receptors.append((passed_along(own, "rec"), [passed_across(part, "rec") for part in away]))

    ligand_occupancy = after(ligand_occupancy, *others)
    pose, *pose_away = sections(s, t, ligand_occupancy, rot_index, True, s.whole)
    pose_others = swapped(pose_away)
    next_pose, next_others = passed_along(pose, "lig"), [passed_across(part, "lig") for part in pose_away]
    spectra = [spectrum(s, t, channel_weight, pose, pose_others, s.whole)]

    own, others = receptors[1]
    own = after(own, spectra[0][0])
    receptors[1] = (own, others)
    cuts = [others[0][low * s.size:high * s.size] for low, high in zip(s.parts, s.parts[1:])]
    receptors.append((passed_along(own, "rec"), [passed_along(part, "rec") for part in cuts]))

    spectra.append(spectrum(s, t, channel_weight, next_pose, next_others, s.whole))
    poses, tops = [main for main, _ in spectra], [top for _, top in spectra]

    rows = []
    for step, (own, others) in enumerate(receptors):
        last = step + 1 == REC_STEPS
        cuts = s.parts if last else s.whole
        ranges = list(zip(cuts, cuts[1:]))
        if last:
            own = after(own, *rows)
        sides = [cross_back(s, t, own, others, poses, tops, cuts, planes) for planes in ranges]
        parts = [keep for keep, _ in sides] + swapped([send for _, send in sides])
        rows.append(peaks(s, t, own, parts, rows if last else [], last))
    return rows[-1]


def solution(mesh):
    placed = (
        P(("groups", "rec", "lig"), None, "fft", None),
        P(("groups", "rec", "lig"), None, "fft", None),
        P(("groups", "rec", "lig")),
        P(("groups", "rec", "lig")),
        P(),
    )
    tables = lambda s: build_tables(s.cells, s.channels, s.slab, s.cores)
    return jax.shard_map(
        partial(shards, tables),
        mesh=mesh,
        in_specs=placed,
        out_specs=P(("groups", "rec", "lig"), None, None, "fft"),
        check_vma=False,
    )
```

```python
from functools import partial
import math

import jax
import jax.numpy as jnp
import ml_dtypes
import numpy as np
from jax import lax
from jax.experimental import pallas as pl
from jax.experimental.pallas import tpu as pltpu
from jax.sharding import PartitionSpec as P

REC_STEPS = 3
LIG_STEPS = 2
MIB = 1024 * 1024
F32 = jnp.float32
BF16 = jnp.bfloat16


def trig(cells):
    phases = np.arange(cells)[:, None] * np.arange(cells)[None, :] % cells
    angles = phases * (2.0 * math.pi / cells)
    pair = []
    for table in (np.cos(angles), np.sin(angles)):
        table = np.where(np.abs(table) < 1e-9, 0.0, table)
        pair.append(table.astype(np.float32).astype(ml_dtypes.bfloat16).astype(np.float32))
    return pair


def complex_rows(real, imag):
    return np.block([[real, -imag], [imag, real]])


def build_tables(cells, channels, slab, cores):
    cosine, sine = trig(cells)
    half = cells // 2
    own = half // cores
    sign = np.where(np.arange(cells) % 2 == 0, 1.0, -1.0).astype(np.float32)
    tables = {}

    def half_rows(core):
        order = [(core + turn) % cores * own + j for turn in range(cores) for j in range(own)]
        real = cosine[order].copy()
        imag = -sine[order]
        imag[order.index(0)] = sign
        return np.concatenate([real, imag], axis=0)

    def half_mix(core):
        order = [(core + turn) % cores * own + j for turn in range(cores) for j in range(own)]
        top = np.concatenate([cosine[order], sine[order]], axis=1)
        low = np.concatenate([-sine[order], cosine[order]], axis=1)
        at = order.index(0)
        one = np.ones(cells, np.float32)
        top[at] = np.concatenate([one, -sign])
        low[at] = np.concatenate([sign, one])
        return np.concatenate([top, low], axis=0)

    def flips(table, width):
        blocks = table.reshape(table.shape[0], -1, width)
        return np.stack([table, blocks[:, :, ::-1].reshape(table.shape)])

    two = np.eye(2, dtype=np.float32)
    full_rows = np.concatenate([cosine, -sine], axis=0)
    forward = complex_rows(cosine, -sine)
    inverse = complex_rows(cosine, sine)
    tables["z_even"] = np.stack([flips(np.kron(two, half_rows(core)), cells) for core in range(cores)], axis=1)
    tables["y_even"] = flips(forward, cells)
    tables["y_odd"] = flips(np.kron(two, full_rows), cells)
    tables["z_odd"] = np.stack([flips(half_mix(core), cells) for core in range(cores)], axis=1)

    group = channels // 2
    spread = []
    for core in range(cores):
        block = np.zeros((cores, 2, group, slab, 2, group, cells), np.float32)
        for turn in range(cores):
            start = (core + turn) % cores * slab
            mix = forward.reshape(2, cells, 2, cells)[:, :, :, start:start + slab]
            for channel in range(group):
                block[turn, :, channel, :, :, channel] = mix.transpose(2, 3, 0, 1)
        spread.append(block.reshape(cores * 2 * group * slab, 2 * group * cells))
    tables["x_forward"] = np.stack(spread)

    mirror = np.zeros((cells, cells), np.float32)
    mirror[np.arange(cells), -np.arange(cells) % cells] = 1.0
    eye = np.eye(cells, dtype=np.float32)
    none = np.zeros((cells, cells), np.float32)
    low = 0.5 * np.block([[eye + mirror, none], [none, eye - mirror]])
    high = 0.5 * np.block([[none, eye + mirror], [mirror - eye, none]])
    plain = np.eye(2 * cells, dtype=np.float32)
    tables["unpack"] = np.stack(
        [np.concatenate([low, high] if core == 0 else [plain, 0.0 * plain], axis=0) for core in range(cores)]
    )

    back = []
    for core in range(cores):
        block = np.zeros((LIG_STEPS, 2, cells, 2, cores, LIG_STEPS, slab), np.float32)
        parts = inverse.reshape(2, cells, 2, cells)
        for turn in range(cores):
            start = (core + turn) % cores * slab
            for pose in range(LIG_STEPS):
                block[pose, :, :, :, turn, pose] = parts[:, start:start + slab].transpose(2, 3, 0, 1)
        back.append(block.reshape(LIG_STEPS * 2 * cells, 2 * cores * LIG_STEPS * slab))
    tables["x_inverse"] = np.stack(back)
    tables["y_inverse"] = inverse

    last = []
    for core in range(cores):
        order = [(core + turn) % cores * own + j for turn in range(cores) for j in range(own)]
        real = 2.0 * cosine[order]
        imag = -2.0 * sine[order]
        at = order.index(0)
        real[at] = 1.0
        imag[at] = sign
        last.append(np.stack([real, imag], axis=1).reshape(2 * half, cells).T)
    tables["z_inverse"] = np.stack(last)
    return {name: jnp.asarray(table.astype(ml_dtypes.bfloat16)) for name, table in tables.items()}


COST = pl.CostEstimate(flops=1000, bytes_accessed=1000, transcendentals=0)


def params(limit=24):
    return pltpu.CompilerParams(vmem_limit_bytes=limit * MIB)


def lines(value):
    return value.astype(F32).astype(BF16)


def dot(left, right):
    return jnp.dot(left, right, preferred_element_type=F32)


def dot_lanes(left, right):
    return lax.dot_general(left, right, (((1,), (1,)), ((), ())), preferred_element_type=F32)


def place(cuts, plane):
    return max(k for k in range(len(cuts) - 1) if cuts[k] <= plane)


class Sizes:
    def __init__(self, channels, slab, plane, cores):
        self.channels, self.slab, self.cores = channels, slab, cores
        self.cells = slab * cores
        self.lanes = channels * slab
        self.fold = self.lanes // self.cells
        self.tiles = plane // self.lanes
        self.own = self.cells // 2 // cores
        self.whole = (0, self.own)
        self.parts = (0, self.own * 3 // 4, self.own)
        self.size = 2 * self.cells
        self.extra = 16
        self.back = cores * LIG_STEPS * slab


def section_kernel(s, pieces, rotated, cuts, occ, scalar, *refs):
    cells, lanes = s.cells, s.lanes
    half, size = cells // 2, s.size
    count = 4 if rotated else 2
    hbm, refs = refs[:count], refs[count:]
    outs, refs = refs[:len(cuts)], refs[len(cuts):]
    small, buffer, held = refs[:3]
    tables = refs[3:3 + count]
    turned = refs[-2] if rotated else None
    sems = refs[-1]
    core = lax.axis_index("fft")

    first = pltpu.make_async_copy(scalar, small, sems.at[0])
    first.start()
    if rotated:
        first.wait()
        turns = small[0]
        is_odd = turns % 2 == 1
        picks = (
            hbm[0].at[turns // 2, core],
            hbm[1].at[turns // 2],
            hbm[2].at[jnp.where(turns == 1, 1, 0)],
            hbm[3].at[jnp.where(turns == 3, 1, 0), core],
        )
    else:
        picks = (hbm[0].at[0, core], hbm[1].at[0])
    loads = [pltpu.make_async_copy(pick, table, sems.at[1 + k]) for k, (pick, table) in enumerate(zip(picks, tables))]
    width = s.tiles // pieces * lanes
    for k in range(pieces):
        here = slice(k * width, (k + 1) * width)
        loads.append(pltpu.make_async_copy(occ.at[0, :, :, here], buffer.at[:, :, here], sems.at[1 + count + k]))
    for load in loads:
        load.start()
    for load in loads[:count]:
        load.wait()

    def lay(table, height, step):
        for tile in range(0, s.tiles, 2):
            if tile % (s.tiles // pieces) == 0:
                loads[count + tile * pieces // s.tiles].wait()
            rows = [
                lines(buffer[:, :, (tile + k) * lanes:(tile + k + 1) * lanes].reshape(lanes, lanes)) for k in range(2)
            ]
            done = dot_lanes(table[...], jnp.concatenate(rows, axis=0))
            for k in range(2):
                for fold in range(s.fold):
                    at = ((tile + k) * s.fold + fold) * step
                    held[at:at + height, :] = done[fold * height:(fold + 1) * height, k * lanes:(k + 1) * lanes]

    def column(ref, at, step):
        return ref[pl.ds(at, cells, stride=step), :]

    def put(index, value):
        group, plane = divmod(index, s.own)
        if group == 0:
            outs[0][plane * size:(plane + 1) * size, :] = value
            return
        cut = place(cuts, plane)
        plane -= cuts[cut]
        outs[1 + cut][plane * size:(plane + 1) * size, :] = value

    def even():
        step = cells + 8
        lay(tables[0], cells, step)
        for pair in range(0, half, 2):
            rows = [
                jnp.concatenate([column(held, q * half + pair + k, step) for q in range(2)], axis=0) for k in range(2)
            ]
            done = dot(tables[1][...], jnp.concatenate(rows, axis=1).astype(BF16)).astype(BF16)
            for k in range(2):
                put(pair + k, done[:, k * lanes:(k + 1) * lanes])

    def odd():
        step, short = size + 8, cells + 8
        lay(tables[2], size, step)
        for pair in range(0, cells, 2):
            rows = [
                jnp.concatenate([column(held, q * cells + pair + k, step) for q in range(2)], axis=0) for k in range(2)
            ]
            done = dot(tables[3][...], jnp.concatenate(rows, axis=1).astype(BF16))
            for k in range(2):
                turned[(pair + k) * short:(pair + k) * short + cells, :] = done[:, k * lanes:(k + 1) * lanes]
        for plane in range(half):
            both = [column(turned, q * half + plane, short) for q in range(2)]
            put(plane, jnp.concatenate(both, axis=0).astype(BF16))

    if rotated:
        pl.when(jnp.logical_not(is_odd))(even)
        pl.when(is_odd)(odd)
    else:
        even()
        first.wait()
        outs[0][s.own * size:, :] = jnp.full((s.extra, lanes), small[0].astype(F32)).astype(BF16)


def sections(s, t, occ, scalar, rotated, cuts, pieces=2):
    cells, lanes = s.cells, s.lanes
    names = ["z_even", "y_even"] + (["y_odd", "z_odd"] if rotated else [])
    hbm = pl.BlockSpec(memory_space=pltpu.HBM)
    pin = lambda value: pltpu.with_memory_space_constraint(value, pltpu.HBM)
    scratch = [
        pltpu.SMEM(scalar.shape, jnp.int32),
        pltpu.VMEM(occ.shape[1:], jnp.int32),
        pltpu.VMEM(((cells + 1) * ((s.size if rotated else cells) + 8), lanes), F32),
    ]
    scratch += [pltpu.VMEM(t[name].shape[-2:], BF16) for name in names]
    if rotated:
        scratch.append(pltpu.VMEM(((cells + 1) * (cells + 8), lanes), F32))
    scratch.append(pltpu.SemaphoreType.DMA((1 + len(names) + pieces,)))
    rows = [s.own * s.size + (0 if rotated else s.extra)]
    rows += [(high - low) * s.size for low, high in zip(cuts, cuts[1:])]
    return pl.pallas_call(
        partial(section_kernel, s, pieces, rotated, cuts),
        in_specs=[hbm, pl.BlockSpec(memory_space=pl.ANY)] + [hbm] * len(names),
        out_specs=[pl.BlockSpec(memory_space=pltpu.VMEM)] * len(rows),
        out_shape=[jax.ShapeDtypeStruct((count, lanes), BF16) for count in rows],
        scratch_shapes=scratch,
        compiler_params=params(),
        cost_estimate=COST,
    )(pin(occ), scalar, *[pin(t[name]) for name in names])


def regroup(s, parts):
    half = s.lanes // 2
    lane = lax.broadcasted_iota(jnp.int32, parts[0].shape, 1)
    low, high = [], []
    for one, two in zip(parts[::2], parts[1::2]):
        low.append(jnp.where(lane < half, one, pltpu.roll(two, half, 1)))
        high.append(jnp.where(lane < half, pltpu.roll(one, half, 1), two))
    return [jnp.concatenate(low, axis=1), jnp.concatenate(high, axis=1)]


def x_rows(s, cuts, own, others, plane):
    cut = place(cuts, plane)
    parts = []
    for ref, at in ((own, plane * s.size), (others[cut], (plane - cuts[cut]) * s.size)):
        for p in range(2):
            parts.append(ref[at + p * s.cells:at + (p + 1) * s.cells, :])
    return regroup(s, parts)


def unpacked_rows(s, own, others, unpack):
    cells = s.cells
    done = [dot(unpack, ref[:s.size, :]).astype(BF16) for ref in (own, others[0])]
    return [
        regroup(s, [value[(2 * k + p) * cells:(2 * k + p + 1) * cells] for value in done for p in range(2)])
        for k in range(2)
    ]


def x_transform(s, rows, table):
    done = dot(jnp.concatenate([row[k] for k in range(2) for row in rows], axis=0), table)
    count = len(rows) * s.cells
    return done[:count], done[count:]


def spectrum_kernel(s, cuts, per, weight, table, unpack, own, *refs):
    others, (main, last) = refs[:-2], refs[-2:]
    volume = 1.0 / float(s.cells) ** 3
    core = lax.axis_index("fft")

    lane = lax.broadcasted_iota(jnp.int32, (s.cells, s.size), 1)
    scales = [
        jnp.where(lane < s.cells, weight[2 * k], weight[2 * k + 1]) * volume for k in range(2)
    ]

    def put(ref, at, values):
        for k, value in enumerate(values):
            for q in range(2):
                from_lanes = slice(q * s.size, (q + 1) * s.size)
                to_lanes = slice((2 * k + q) * s.size, (2 * k + q + 1) * s.size)
                for row in range(0, value.shape[0], s.cells):
                    ref[at + row:at + row + s.cells, to_lanes] = (
                        value[row:row + s.cells, from_lanes] * scales[k]
                    ).astype(BF16)

    for start in range(0, s.own, per):
        rows = [x_rows(s, cuts, own, others, plane) for plane in range(start, start + per)]
        if start == 0:
            rows[0], high = unpacked_rows(s, own, others, unpack[core])
            rows.append(high)
        done = x_transform(s, rows, table[core])
        put(main, start * s.cells, [value[:per * s.cells] for value in done])
        if start == 0:
            put(last, 0, [value[per * s.cells:] for value in done])


def spectrum(s, t, weight, own, others, cuts, per=4):
    width = s.channels * s.size
    vmem = pl.BlockSpec(memory_space=pltpu.VMEM)
    return pl.pallas_call(
        partial(spectrum_kernel, s, cuts, per),
        in_specs=[pl.BlockSpec(memory_space=pltpu.SMEM)] + [vmem] * (3 + len(others)),
        out_specs=[vmem] * 2,
        out_shape=[jax.ShapeDtypeStruct((s.own * s.cells, width), BF16), jax.ShapeDtypeStruct((s.cells, width), BF16)],
        compiler_params=params(),
        cost_estimate=COST,
    )(weight, t["x_forward"], t["unpack"], own, *others)


def cross_kernel(s, cuts, planes, most, table, unpack, x_inverse, y_inverse, *refs):
    poses, tops = refs[:LIG_STEPS], refs[LIG_STEPS:2 * LIG_STEPS]
    own, others = refs[2 * LIG_STEPS], refs[2 * LIG_STEPS + 1:-2]
    keep, send = refs[-2:]
    cells, width, lanes = s.cells, s.size, s.back
    core = lax.axis_index("fft")
    lane = lax.broadcasted_iota(jnp.int32, (cells, width), 1)
    is_real = lane < cells
    kept = lax.broadcasted_iota(jnp.int32, (cells // 2, lanes), 1) < lanes // 2

    def correlate(receptor, pose):
        real = imag = None
        for k, value in enumerate(receptor):
            one = [value[:, q * width:(q + 1) * width] for q in range(2)]
            two = [pose[:, (2 * k + q) * width:(2 * k + q + 1) * width].astype(F32) for q in range(2)]
            same = one[0] * two[0] + one[1] * two[1]
            turned = one[1] * two[0] - one[0] * two[1]
            real = same if real is None else real + same
            imag = turned if imag is None else imag + turned
        return jnp.where(is_real, real, imag) + pltpu.roll(jnp.where(is_real, imag, real), cells, 1)

    for start in range(planes[0], planes[1], most):
        per = min(most, planes[1] - start)
        rows = [x_rows(s, cuts, own, others, plane) for plane in range(start, start + per)]
        if start == 0:
            rows[0], high = unpacked_rows(s, own, others, unpack[core])
            rows.append(high)
        done = x_transform(s, rows, table[core])
        cross = []
        for k in range(per):
            both = []
            for pose in range(LIG_STEPS):
                at = (start + k) * cells
                value = correlate([half[k * cells:(k + 1) * cells] for half in done], poses[pose][at:at + cells, :])
                if start + k == 0:
                    row = lax.broadcasted_iota(jnp.int32, (cells, width), 0)
                    at_zero = (row == 0) & ((lane == 0) | (lane == cells)) & (core == 0)
                    value = jnp.where(at_zero, 0.0, value)
                    top = pltpu.roll(correlate([half[per * cells:] for half in done], tops[pose][...]), cells, 1)
                    value = value + jnp.where(is_real, -top, top)
                both.append(value.astype(BF16))
            cross.append(jnp.concatenate(both, axis=1))
        back = dot(jnp.concatenate(cross, axis=0), x_inverse[core]).astype(BF16)
        for pair in range(0, per, 2):
            sides = []
            for k in range(2):
                here = back[(pair + k) * cells:(pair + k + 1) * cells]
                sides.append(jnp.concatenate([here[:, :lanes], here[:, lanes:]], axis=0))
            out = dot(y_inverse[...], jnp.concatenate(sides, axis=1))
            for k in range(2):
                for q in range(2):
                    value = out[q * cells:(q + 1) * cells, k * lanes:(k + 1) * lanes]
                    low, high = value[:cells // 2], value[cells // 2:]
                    at = (start - planes[0] + pair + k) * cells + q * cells // 2
                    at = slice(at, at + cells // 2)
                    keep[at, :] = jnp.where(kept, low, pltpu.roll(high, lanes // 2, 1)).astype(BF16)
                    send[at, :] = jnp.where(kept, pltpu.roll(low, lanes // 2, 1), high).astype(BF16)


def cross_back(s, t, own, others, poses, tops, cuts, planes, per=4):
    vmem = pl.BlockSpec(memory_space=pltpu.VMEM)
    shape = jax.ShapeDtypeStruct(((planes[1] - planes[0]) * s.cells, s.back), BF16)
    used = range(place(cuts, planes[0]), place(cuts, planes[1] - 1) + 1)
    others, cuts = [others[k] for k in used], tuple(cuts[used[0]:used[-1] + 2])
    operands = [t["x_forward"], t["unpack"], t["x_inverse"], t["y_inverse"], *poses, *tops, own, *others]
    return pl.pallas_call(
        partial(cross_kernel, s, cuts, planes, per),
        in_specs=[vmem] * len(operands),
        out_specs=[vmem] * 2,
        out_shape=[shape] * 2,
        compiler_params=params(),
        cost_estimate=COST,
    )(*operands)


def peak_kernel(s, count, last, load, table, *refs):
    parts = refs[:count]
    earlier, out, held = refs[count:-2], refs[-2], refs[-1]
    cells = s.cells
    low = cells // 2
    core = lax.axis_index("fft")
    step = low + 8
    at = 0
    for part in parts:
        for row in range(0, part.shape[0], low):
            held[at:at + low, :] = part[row:row + low, :].astype(F32)
            at += step
    best = None
    for pair in range(0, low, 2):
        columns = [held[pl.ds(pair + k, cells, stride=step), :] for k in range(2)]
        scores = dot(table[core], jnp.concatenate(columns, axis=1).astype(BF16))
        here = jnp.maximum(scores[:, :s.back], scores[:, s.back:])
        best = here if best is None else jnp.maximum(best, here)
    row = jnp.max(best, axis=0, keepdims=True)
    row = jnp.maximum(row, pltpu.roll(row, s.back // 2, 1)) * (1.0 / (cells * math.sqrt(cells)))
    plane = lax.broadcasted_iota(jnp.int32, row.shape, 1) % s.slab + core * s.slab
    extent = load[s.own * s.size:, :].astype(F32)[:1]
    row = jnp.where(plane.astype(F32) < extent, row, 0.0)
    if not last:
        out[...] = row
        return
    for index, value in enumerate([ref[...] for ref in earlier] + [row]):
        for pose in range(LIG_STEPS):
            out[0, index, pose:pose + 1, :] = value[:, pose * s.slab:(pose + 1) * s.slab]


def peaks(s, t, load, parts, earlier, last):
    vmem = pl.BlockSpec(memory_space=pltpu.VMEM)
    shape = (1, REC_STEPS, LIG_STEPS, s.slab) if last else (1, s.back)
    return pl.pallas_call(
        partial(peak_kernel, s, len(parts), last),
        in_specs=[vmem] * (2 + len(parts) + len(earlier)),
        out_specs=vmem,
        out_shape=jax.ShapeDtypeStruct(shape, F32),
        scratch_shapes=[pltpu.VMEM(((s.cells + 1) * (s.cells // 2 + 8), s.back), F32)],
        compiler_params=params(),
        cost_estimate=COST,
    )(load, t["z_inverse"], *parts, *earlier)


def passed_along(value, axis, steps=1):
    count = lax.axis_size(axis)
    return lax.ppermute(value, axis, [(source, (source + steps) % count) for source in range(count)])


def passed_across(value, axis):
    count, cores = lax.axis_size(axis), lax.axis_size("fft")
    pairs = [
        (place * cores + core, (place + 1) % count * cores + (core + 1) % cores)
        for place in range(count)
        for core in range(cores)
    ]
    return lax.ppermute(value, (axis, "fft"), pairs)


def after(value, *others):
    return lax.optimization_barrier((value, *others))[0]


def shards(tables, receptor_occupancy, ligand_occupancy, rot_index, receptor_extent, channel_weight):
    _, channels, slab, plane = receptor_occupancy.shape
    s = Sizes(channels, slab, plane, lax.axis_size("fft"))
    t = tables(s)
    swapped = lambda parts: [passed_along(part, "fft") for part in parts]

    own, *away = sections(s, t, receptor_occupancy, receptor_extent, False, s.whole)
    receptors = []
    receptors.append((passed_along(own, "rec"), [passed_across(part, "rec") for part in away]))

    ligand_occupancy = after(ligand_occupancy, *away)
    pose, *pose_away = sections(s, t, ligand_occupancy, rot_index, True, s.whole)
    pose_others = swapped([after(part, receptors[0][0]) for part in pose_away])
    next_pose, next_others = passed_along(pose, "lig"), [passed_across(part, "lig") for part in pose_away]
    receptors.insert(0, (own, swapped([after(part, next_pose) for part in away])))
    spectra = [spectrum(s, t, channel_weight, pose, pose_others, s.whole)]

    own, others = receptors[1]
    receptors[1] = (own, others)
    cuts = [others[0][low * s.size:high * s.size] for low, high in zip(s.parts, s.parts[1:])]
    receptors.append((passed_along(own, "rec"), [passed_along(part, "rec") for part in cuts]))

    spectra.append(spectrum(s, t, channel_weight, next_pose, next_others, s.whole))
    poses, tops = [main for main, _ in spectra], [top for _, top in spectra]

    rows = []
    for step, (own, others) in enumerate(receptors):
        last = step + 1 == REC_STEPS
        cuts = s.parts if last else s.whole
        ranges = list(zip(cuts, cuts[1:]))
        if last:
            own = after(own, *rows)
        sides = [cross_back(s, t, own, others, poses, tops, cuts, planes) for planes in ranges]
        parts = [keep for keep, _ in sides] + swapped([send for _, send in sides])
        rows.append(peaks(s, t, own, parts, rows if last else [], last))
    return rows[-1]


def solution(mesh):
    placed = (
        P(("groups", "rec", "lig"), None, "fft", None),
        P(("groups", "rec", "lig"), None, "fft", None),
        P(("groups", "rec", "lig")),
        P(("groups", "rec", "lig")),
        P(),
    )
    tables = lambda s: build_tables(s.cells, s.channels, s.slab, s.cores)
    return jax.shard_map(
        partial(shards, tables),
        mesh=mesh,
        in_specs=placed,
        out_specs=P(("groups", "rec", "lig"), None, None, "fft"),
        check_vma=False,
    )
```

```python
from functools import partial
import math

import jax
import jax.numpy as jnp
import ml_dtypes
import numpy as np
from jax import lax
from jax.experimental import pallas as pl
from jax.experimental.pallas import tpu as pltpu
from jax.sharding import PartitionSpec as P

REC_STEPS = 3
LIG_STEPS = 2
MIB = 1024 * 1024
F32 = jnp.float32
BF16 = jnp.bfloat16


def trig(cells):
    phases = np.arange(cells)[:, None] * np.arange(cells)[None, :] % cells
    angles = phases * (2.0 * math.pi / cells)
    pair = []
    for table in (np.cos(angles), np.sin(angles)):
        table = np.where(np.abs(table) < 1e-9, 0.0, table)
        pair.append(table.astype(np.float32).astype(ml_dtypes.bfloat16).astype(np.float32))
    return pair


def complex_rows(real, imag):
    return np.block([[real, -imag], [imag, real]])


def build_tables(cells, channels, slab, cores):
    cosine, sine = trig(cells)
    half = cells // 2
    own = half // cores
    sign = np.where(np.arange(cells) % 2 == 0, 1.0, -1.0).astype(np.float32)
    tables = {}

    def half_rows(core):
        order = [(core + turn) % cores * own + j for turn in range(cores) for j in range(own)]
        real = cosine[order].copy()
        imag = -sine[order]
        imag[order.index(0)] = sign
        return np.concatenate([real, imag], axis=0)

    def half_mix(core):
        order = [(core + turn) % cores * own + j for turn in range(cores) for j in range(own)]
        top = np.concatenate([cosine[order], sine[order]], axis=1)
        low = np.concatenate([-sine[order], cosine[order]], axis=1)
        at = order.index(0)
        one = np.ones(cells, np.float32)
        top[at] = np.concatenate([one, -sign])
        low[at] = np.concatenate([sign, one])
        return np.concatenate([top, low], axis=0)

    def flips(table, width):
        blocks = table.reshape(table.shape[0], -1, width)
        return np.stack([table, blocks[:, :, ::-1].reshape(table.shape)])

    two = np.eye(2, dtype=np.float32)
    full_rows = np.concatenate([cosine, -sine], axis=0)
    forward = complex_rows(cosine, -sine)
    inverse = complex_rows(cosine, sine)
    tables["z_even"] = np.stack([flips(np.kron(two, half_rows(core)), cells) for core in range(cores)], axis=1)
    tables["y_even"] = flips(forward, cells)
    tables["y_odd"] = flips(np.kron(two, full_rows), cells)
    tables["z_odd"] = np.stack([flips(half_mix(core), cells) for core in range(cores)], axis=1)

    group = channels // 2
    spread = []
    for core in range(cores):
        block = np.zeros((cores, 2, group, slab, 2, group, cells), np.float32)
        for turn in range(cores):
            start = (core + turn) % cores * slab
            mix = forward.reshape(2, cells, 2, cells)[:, :, :, start:start + slab]
            for channel in range(group):
                block[turn, :, channel, :, :, channel] = mix.transpose(2, 3, 0, 1)
        spread.append(block.reshape(cores * 2 * group * slab, 2 * group * cells))
    tables["x_forward"] = np.stack(spread)

    mirror = np.zeros((cells, cells), np.float32)
    mirror[np.arange(cells), -np.arange(cells) % cells] = 1.0
    eye = np.eye(cells, dtype=np.float32)
    none = np.zeros((cells, cells), np.float32)
    low = 0.5 * np.block([[eye + mirror, none], [none, eye - mirror]])
    high = 0.5 * np.block([[none, eye + mirror], [mirror - eye, none]])
    plain = np.eye(2 * cells, dtype=np.float32)
    tables["unpack"] = np.stack(
        [np.concatenate([low, high] if core == 0 else [plain, 0.0 * plain], axis=0) for core in range(cores)]
    )

    back = []
    for core in range(cores):
        block = np.zeros((LIG_STEPS, 2, cells, 2, cores, LIG_STEPS, slab), np.float32)
        parts = inverse.reshape(2, cells, 2, cells)
        for turn in range(cores):
            start = (core + turn) % cores * slab
            for pose in range(LIG_STEPS):
                block[pose, :, :, :, turn, pose] = parts[:, start:start + slab].transpose(2, 3, 0, 1)
        back.append(block.reshape(LIG_STEPS * 2 * cells, 2 * cores * LIG_STEPS * slab))
    tables["x_inverse"] = np.stack(back)
    tables["y_inverse"] = inverse

    last = []
    for core in range(cores):
        order = [(core + turn) % cores * own + j for turn in range(cores) for j in range(own)]
        real = 2.0 * cosine[order]
        imag = -2.0 * sine[order]
        at = order.index(0)
        real[at] = 1.0
        imag[at] = sign
        last.append(np.stack([real, imag], axis=1).reshape(2 * half, cells).T)
    tables["z_inverse"] = np.stack(last)
    return {name: jnp.asarray(table.astype(ml_dtypes.bfloat16)) for name, table in tables.items()}


COST = pl.CostEstimate(flops=1000, bytes_accessed=1000, transcendentals=0)


def params(limit=24):
    return pltpu.CompilerParams(vmem_limit_bytes=limit * MIB)


def lines(value):
    return value.astype(F32).astype(BF16)


def dot(left, right):
    return jnp.dot(left, right, preferred_element_type=F32)


def dot_lanes(left, right):
    return lax.dot_general(left, right, (((1,), (1,)), ((), ())), preferred_element_type=F32)


def place(cuts, plane):
    return max(k for k in range(len(cuts) - 1) if cuts[k] <= plane)


class Sizes:
    def __init__(self, channels, slab, plane, cores):
        self.channels, self.slab, self.cores = channels, slab, cores
        self.cells = slab * cores
        self.lanes = channels * slab
        self.fold = self.lanes // self.cells
        self.tiles = plane // self.lanes
        self.own = self.cells // 2 // cores
        self.whole = (0, self.own)
        self.parts = (0, self.own * 3 // 4, self.own)
        self.size = 2 * self.cells
        self.extra = 16
        self.back = cores * LIG_STEPS * slab


def y_planes(s, table, held, pair):
    half, step = s.cells // 2, s.cells + 8
    rows = [
        jnp.concatenate([held[pl.ds(q * half + pair + k, s.cells, stride=step), :] for q in range(2)], axis=0)
        for k in range(2)
    ]
    done = dot(table[...], jnp.concatenate(rows, axis=1).astype(BF16)).astype(BF16)
    return [done[:, k * s.lanes:(k + 1) * s.lanes] for k in range(2)]


def away_kernel(s, extent, held, table, out):
    for pair in range(0, s.own, 2):
        for k, plane in enumerate(y_planes(s, table.at[0], held, s.own + pair)):
            out[(pair + k) * s.size:(pair + k + 1) * s.size, :] = plane
    out[s.own * s.size:, :] = jnp.full((s.extra, s.lanes), extent[0].astype(F32)).astype(BF16)


def away_planes(s, t, extent, held):
    vmem = pl.BlockSpec(memory_space=pltpu.VMEM)
    return pl.pallas_call(
        partial(away_kernel, s),
        in_specs=[pl.BlockSpec(memory_space=pltpu.SMEM)] + [vmem] * 2,
        out_specs=vmem,
        out_shape=jax.ShapeDtypeStruct((s.own * s.size + s.extra, s.lanes), BF16),
        compiler_params=params(),
        cost_estimate=COST,
    )(extent, held, t["y_even"])


def section_kernel(s, pieces, rotated, cuts, occ, *refs):
    cells, lanes = s.cells, s.lanes
    half, size = cells // 2, s.size
    count = 4 if rotated else 2
    if rotated:
        scalar, refs = refs[0], refs[1:]
    hbm, refs = refs[:count], refs[count:]
    outs, refs = refs[:len(cuts)], refs[len(cuts):]
    if rotated:
        small, buffer, held = refs[:3]
    else:
        small, buffer, held = None, refs[0], outs[1]
        refs = (None, None, *refs)
    tables = refs[3:3 + count]
    turned = refs[-2] if rotated else None
    sems = refs[-1]
    core = lax.axis_index("fft")

    if rotated:
        first = pltpu.make_async_copy(scalar, small, sems.at[0])
        first.start()
        first.wait()
        turns = small[0]
        is_odd = turns % 2 == 1
        picks = (
            hbm[0].at[turns // 2, core],
            hbm[1].at[turns // 2],
            hbm[2].at[jnp.where(turns == 1, 1, 0)],
            hbm[3].at[jnp.where(turns == 3, 1, 0), core],
        )
    else:
        picks = (hbm[0].at[0, core], hbm[1].at[0])
    loads = [pltpu.make_async_copy(pick, table, sems.at[1 + k]) for k, (pick, table) in enumerate(zip(picks, tables))]
    width = s.tiles // pieces * lanes
    for k in range(pieces):
        here = slice(k * width, (k + 1) * width)
        loads.append(pltpu.make_async_copy(occ.at[0, :, :, here], buffer.at[:, :, here], sems.at[1 + count + k]))
    for load in loads:
        load.start()
    for load in loads[:count]:
        load.wait()

    def lay(table, height, step):
        for tile in range(0, s.tiles, 2):
            if tile % (s.tiles // pieces) == 0:
                loads[count + tile * pieces // s.tiles].wait()
            rows = [
                lines(buffer[:, :, (tile + k) * lanes:(tile + k + 1) * lanes].reshape(lanes, lanes)) for k in range(2)
            ]
            done = dot_lanes(table[...], jnp.concatenate(rows, axis=0))
            for k in range(2):
                for fold in range(s.fold):
                    at = ((tile + k) * s.fold + fold) * step
                    held[at:at + height, :] = done[fold * height:(fold + 1) * height, k * lanes:(k + 1) * lanes]

    def column(ref, at, step):
        return ref[pl.ds(at, cells, stride=step), :]

    def put(index, value):
        group, plane = divmod(index, s.own)
        if group == 0:
            outs[0][plane * size:(plane + 1) * size, :] = value
            return
        cut = place(cuts, plane)
        plane -= cuts[cut]
        outs[1 + cut][plane * size:(plane + 1) * size, :] = value

    def even():
        step = cells + 8
        lay(tables[0], cells, step)
        for pair in range(0, half if rotated else s.own, 2):
            for k, plane in enumerate(y_planes(s, tables[1], held, pair)):
                put(pair + k, plane)

    def odd():
        step, short = size + 8, cells + 8
        lay(tables[2], size, step)
        for pair in range(0, cells, 2):
            rows = [
                jnp.concatenate([column(held, q * cells + pair + k, step) for q in range(2)], axis=0) for k in range(2)
            ]
            done = dot(tables[3][...], jnp.concatenate(rows, axis=1).astype(BF16))
            for k in range(2):
                turned[(pair + k) * short:(pair + k) * short + cells, :] = done[:, k * lanes:(k + 1) * lanes]
        for plane in range(half):
            both = [column(turned, q * half + plane, short) for q in range(2)]
            put(plane, jnp.concatenate(both, axis=0).astype(BF16))

    if rotated:
        for out in outs:
            out[out.shape[0] - s.extra:, :] = jnp.zeros((s.extra, lanes), BF16)
        pl.when(jnp.logical_not(is_odd))(even)
        pl.when(is_odd)(odd)
    else:
        even()
        outs[0][s.own * size:, :] = jnp.zeros((2 * s.extra, lanes), BF16)


def sections(s, t, occ, scalar, rotated, cuts, pieces=2):
    cells, lanes = s.cells, s.lanes
    names = ["z_even", "y_even"] + (["y_odd", "z_odd"] if rotated else [])
    hbm = pl.BlockSpec(memory_space=pltpu.HBM)
    pin = lambda value: pltpu.with_memory_space_constraint(value, pltpu.HBM)
    scratch = [pltpu.VMEM(occ.shape[1:], jnp.int32)]
    if rotated:
        scratch.insert(0, pltpu.SMEM(scalar.shape, jnp.int32))
        scratch.append(pltpu.VMEM(((cells + 1) * (s.size + 8), lanes), F32))
    scratch += [pltpu.VMEM(t[name].shape[-2:], BF16) for name in names]
    if rotated:
        scratch.append(pltpu.VMEM(((cells + 1) * (cells + 8), lanes), F32))
    scratch.append(pltpu.SemaphoreType.DMA((1 + len(names) + pieces,)))
    rows = [s.own * s.size + (1 if rotated else 2) * s.extra]
    rows += [(high - low) * s.size + s.extra for low, high in zip(cuts, cuts[1:])]
    shapes = [jax.ShapeDtypeStruct((count, lanes), BF16) for count in rows]
    if not rotated:
        shapes[1:] = [jax.ShapeDtypeStruct(((cells + 1) * (cells + 8), lanes), F32)]
    return pl.pallas_call(
        partial(section_kernel, s, pieces, rotated, cuts),
        in_specs=[hbm] + [pl.BlockSpec(memory_space=pl.ANY)] * rotated + [hbm] * len(names),
        out_specs=[pl.BlockSpec(memory_space=pltpu.VMEM)] * len(shapes),
        out_shape=shapes,
        scratch_shapes=scratch,
        compiler_params=params(),
        cost_estimate=COST,
    )(pin(occ), *([scalar] if rotated else []), *[pin(t[name]) for name in names])


def regroup(s, parts):
    half = s.lanes // 2
    lane = lax.broadcasted_iota(jnp.int32, parts[0].shape, 1)
    low, high = [], []
    for one, two in zip(parts[::2], parts[1::2]):
        low.append(jnp.where(lane < half, one, pltpu.roll(two, half, 1)))
        high.append(jnp.where(lane < half, pltpu.roll(one, half, 1), two))
    return [jnp.concatenate(low, axis=1), jnp.concatenate(high, axis=1)]


def x_rows(s, cuts, own, others, plane):
    cut = place(cuts, plane)
    parts = []
    for ref, at in ((own, plane * s.size), (others[cut], (plane - cuts[cut]) * s.size)):
        for p in range(2):
            parts.append(ref[at + p * s.cells:at + (p + 1) * s.cells, :])
    return regroup(s, parts)


def unpacked_rows(s, own, others, unpack):
    cells = s.cells
    done = [dot(unpack, ref[:s.size, :]).astype(BF16) for ref in (own, others[0])]
    return [
        regroup(s, [value[(2 * k + p) * cells:(2 * k + p + 1) * cells] for value in done for p in range(2)])
        for k in range(2)
    ]


def x_transform(s, rows, table):
    done = dot(jnp.concatenate([row[k] for k in range(2) for row in rows], axis=0), table)
    count = len(rows) * s.cells
    return done[:count], done[count:]


def spectrum_kernel(s, cuts, per, weight, table, unpack, own, *refs):
    others, (main, last) = refs[:-2], refs[-2:]
    volume = 1.0 / float(s.cells) ** 3
    core = lax.axis_index("fft")

    lane = lax.broadcasted_iota(jnp.int32, (s.cells, s.size), 1)
    scales = [
        jnp.where(lane < s.cells, weight[2 * k], weight[2 * k + 1]) * volume for k in range(2)
    ]

    def put(ref, at, values):
        for k, value in enumerate(values):
            for q in range(2):
                from_lanes = slice(q * s.size, (q + 1) * s.size)
                to_lanes = slice((2 * k + q) * s.size, (2 * k + q + 1) * s.size)
                for row in range(0, value.shape[0], s.cells):
                    ref[at + row:at + row + s.cells, to_lanes] = (
                        value[row:row + s.cells, from_lanes] * scales[k]
                    ).astype(BF16)

    for start in range(0, s.own, per):
        rows = [x_rows(s, cuts, own, others, plane) for plane in range(start, start + per)]
        if start == 0:
            rows[0], high = unpacked_rows(s, own, others, unpack[core])
            rows.append(high)
        done = x_transform(s, rows, table[core])
        put(main, start * s.cells, [value[:per * s.cells] for value in done])
        if start == 0:
            put(last, 0, [value[per * s.cells:] for value in done])


def spectrum(s, t, weight, own, others, cuts, per=4):
    width = s.channels * s.size
    vmem = pl.BlockSpec(memory_space=pltpu.VMEM)
    return pl.pallas_call(
        partial(spectrum_kernel, s, cuts, per),
        in_specs=[pl.BlockSpec(memory_space=pltpu.SMEM)] + [vmem] * (3 + len(others)),
        out_specs=[vmem] * 2,
        out_shape=[jax.ShapeDtypeStruct((s.own * s.cells, width), BF16), jax.ShapeDtypeStruct((s.cells, width), BF16)],
        compiler_params=params(),
        cost_estimate=COST,
    )(weight, t["x_forward"], t["unpack"], own, *others)


def cross_kernel(s, cuts, planes, most, table, unpack, x_inverse, y_inverse, *refs):
    poses, tops = refs[:LIG_STEPS], refs[LIG_STEPS:2 * LIG_STEPS]
    own, others = refs[2 * LIG_STEPS], refs[2 * LIG_STEPS + 1:-2]
    keep, send = refs[-2:]
    cells, width, lanes = s.cells, s.size, s.back
    core = lax.axis_index("fft")
    lane = lax.broadcasted_iota(jnp.int32, (cells, width), 1)
    is_real = lane < cells
    kept = lax.broadcasted_iota(jnp.int32, (cells // 2, lanes), 1) < lanes // 2

    def correlate(receptor, pose):
        real = imag = None
        for k, value in enumerate(receptor):
            one = [value[:, q * width:(q + 1) * width] for q in range(2)]
            two = [pose[:, (2 * k + q) * width:(2 * k + q + 1) * width].astype(F32) for q in range(2)]
            same = one[0] * two[0] + one[1] * two[1]
            turned = one[1] * two[0] - one[0] * two[1]
            real = same if real is None else real + same
            imag = turned if imag is None else imag + turned
        return jnp.where(is_real, real, imag) + pltpu.roll(jnp.where(is_real, imag, real), cells, 1)

    for start in range(planes[0], planes[1], most):
        per = min(most, planes[1] - start)
        rows = [x_rows(s, cuts, own, others, plane) for plane in range(start, start + per)]
        if start == 0:
            rows[0], high = unpacked_rows(s, own, others, unpack[core])
            rows.append(high)
        done = x_transform(s, rows, table[core])
        cross = []
        for k in range(per):
            both = []
            for pose in range(LIG_STEPS):
                at = (start + k) * cells
                value = correlate([half[k * cells:(k + 1) * cells] for half in done], poses[pose][at:at + cells, :])
                if start + k == 0:
                    row = lax.broadcasted_iota(jnp.int32, (cells, width), 0)
                    at_zero = (row == 0) & ((lane == 0) | (lane == cells)) & (core == 0)
                    value = jnp.where(at_zero, 0.0, value)
                    top = pltpu.roll(correlate([half[per * cells:] for half in done], tops[pose][...]), cells, 1)
                    value = value + jnp.where(is_real, -top, top)
                both.append(value.astype(BF16))
            cross.append(jnp.concatenate(both, axis=1))
        back = dot(jnp.concatenate(cross, axis=0), x_inverse[core]).astype(BF16)
        for pair in range(0, per, 2):
            sides = []
            for k in range(2):
                here = back[(pair + k) * cells:(pair + k + 1) * cells]
                sides.append(jnp.concatenate([here[:, :lanes], here[:, lanes:]], axis=0))
            out = dot(y_inverse[...], jnp.concatenate(sides, axis=1))
            for k in range(2):
                for q in range(2):
                    value = out[q * cells:(q + 1) * cells, k * lanes:(k + 1) * lanes]
                    low, high = value[:cells // 2], value[cells // 2:]
                    at = (start - planes[0] + pair + k) * cells + q * cells // 2
                    at = slice(at, at + cells // 2)
                    keep[at, :] = jnp.where(kept, low, pltpu.roll(high, lanes // 2, 1)).astype(BF16)
                    send[at, :] = jnp.where(kept, pltpu.roll(low, lanes // 2, 1), high).astype(BF16)


def cross_back(s, t, own, others, poses, tops, cuts, planes, per=4):
    vmem = pl.BlockSpec(memory_space=pltpu.VMEM)
    shape = jax.ShapeDtypeStruct(((planes[1] - planes[0]) * s.cells, s.back), BF16)
    used = range(place(cuts, planes[0]), place(cuts, planes[1] - 1) + 1)
    others, cuts = [others[k] for k in used], tuple(cuts[used[0]:used[-1] + 2])
    operands = [t["x_forward"], t["unpack"], t["x_inverse"], t["y_inverse"], *poses, *tops, own, *others]
    return pl.pallas_call(
        partial(cross_kernel, s, cuts, planes, per),
        in_specs=[vmem] * len(operands),
        out_specs=[vmem] * 2,
        out_shape=[shape] * 2,
        compiler_params=params(),
        cost_estimate=COST,
    )(*operands)


def peak_kernel(s, count, last, load, table, *refs):
    parts = refs[:count]
    earlier, out, held = refs[count:-2], refs[-2], refs[-1]
    cells = s.cells
    low = cells // 2
    core = lax.axis_index("fft")
    step = low + 8
    at = 0
    for part in parts:
        for row in range(0, part.shape[0], low):
            held[at:at + low, :] = part[row:row + low, :].astype(F32)
            at += step
    best = None
    for pair in range(0, low, 2):
        columns = [held[pl.ds(pair + k, cells, stride=step), :] for k in range(2)]
        scores = dot(table[core], jnp.concatenate(columns, axis=1).astype(BF16))
        here = jnp.maximum(scores[:, :s.back], scores[:, s.back:])
        best = here if best is None else jnp.maximum(best, here)
    row = jnp.max(best, axis=0, keepdims=True)
    row = jnp.maximum(row, pltpu.roll(row, s.back // 2, 1)) * (1.0 / (cells * math.sqrt(cells)))
    plane = lax.broadcasted_iota(jnp.int32, row.shape, 1) % s.slab + core * s.slab
    extent = load[load.shape[0] - s.extra:, :].astype(F32)[:1]
    row = jnp.where(plane.astype(F32) < extent, row, 0.0)
    if not last:
        out[...] = row
        return
    for index, value in enumerate([ref[...] for ref in earlier] + [row]):
        for pose in range(LIG_STEPS):
            out[0, index, pose:pose + 1, :] = value[:, pose * s.slab:(pose + 1) * s.slab]


def peaks(s, t, load, parts, earlier, last):
    vmem = pl.BlockSpec(memory_space=pltpu.VMEM)
    shape = (1, REC_STEPS, LIG_STEPS, s.slab) if last else (1, s.back)
    return pl.pallas_call(
        partial(peak_kernel, s, len(parts), last),
        in_specs=[vmem] * (2 + len(parts) + len(earlier)),
        out_specs=vmem,
        out_shape=jax.ShapeDtypeStruct(shape, F32),
        scratch_shapes=[pltpu.VMEM(((s.cells + 1) * (s.cells // 2 + 8), s.back), F32)],
        compiler_params=params(),
        cost_estimate=COST,
    )(load, t["z_inverse"], *parts, *earlier)


def passed_along(value, axis, steps=1):
    count = lax.axis_size(axis)
    return lax.ppermute(value, axis, [(source, (source + steps) % count) for source in range(count)])


def passed_across(value, axis):
    count, cores = lax.axis_size(axis), lax.axis_size("fft")
    pairs = [
        (place * cores + core, (place + 1) % count * cores + (core + 1) % cores)
        for place in range(count)
        for core in range(cores)
    ]
    return lax.ppermute(value, (axis, "fft"), pairs)


def after(value, *others):
    return lax.optimization_barrier((value, *others))[0]


def shards(tables, receptor_occupancy, ligand_occupancy, rot_index, receptor_extent, channel_weight):
    _, channels, slab, plane = receptor_occupancy.shape
    s = Sizes(channels, slab, plane, lax.axis_size("fft"))
    t = tables(s)
    swapped = lambda parts: [passed_along(part, "fft") for part in parts]

    own, held = sections(s, t, receptor_occupancy, None, False, s.whole)
    away = [away_planes(s, t, after(receptor_extent, own), held)]
    receptors = []
    receptors.append((passed_along(own, "rec"), [passed_across(part, "rec") for part in away]))

    ligand_occupancy = after(ligand_occupancy, *away)
    pose, *pose_away = sections(s, t, ligand_occupancy, rot_index, True, s.whole)
    pose_others = swapped([after(part, receptors[0][0]) for part in pose_away])
    next_pose, next_others = passed_along(pose, "lig"), [passed_across(part, "lig") for part in pose_away]
    receptors.insert(0, (own, swapped([after(part, next_pose) for part in away])))
    spectra = [spectrum(s, t, channel_weight, pose, pose_others, s.whole)]

    own, others = receptors[1]
    receptors[1] = (own, others)
    ends = [part * s.size for part in s.parts[:-1]] + [None]
    cuts = [others[0][low:high] for low, high in zip(ends, ends[1:])]
    receptors.append((passed_along(own, "rec"), [passed_along(part, "rec") for part in cuts]))

    spectra.append(spectrum(s, t, channel_weight, next_pose, next_others, s.whole))
    poses, tops = [main for main, _ in spectra], [top for _, top in spectra]

    rows = []
    for step, (own, others) in enumerate(receptors):
        last = step + 1 == REC_STEPS
        cuts = s.parts if last else s.whole
        ranges = list(zip(cuts, cuts[1:]))
        if last:
            own = after(own, *rows)
        sides = [cross_back(s, t, own, others, poses, tops, cuts, planes) for planes in ranges]
        parts = [keep for keep, _ in sides] + swapped([send for _, send in sides])
        rows.append(peaks(s, t, others[-1], parts, rows if last else [], last))
    return rows[-1]


def solution(mesh):
    placed = (
        P(("groups", "rec", "lig"), None, "fft", None),
        P(("groups", "rec", "lig"), None, "fft", None),
        P(("groups", "rec", "lig")),
        P(("groups", "rec", "lig")),
        P(),
    )
    tables = lambda s: build_tables(s.cells, s.channels, s.slab, s.cores)
    return jax.shard_map(
        partial(shards, tables),
        mesh=mesh,
        in_specs=placed,
        out_specs=P(("groups", "rec", "lig"), None, None, "fft"),
        check_vma=False,
    )
```

```python
from functools import partial
import math

import jax
import jax.numpy as jnp
import ml_dtypes
import numpy as np
from jax import lax
from jax.experimental import pallas as pl
from jax.experimental.pallas import tpu as pltpu
from jax.sharding import PartitionSpec as P

REC_STEPS = 3
LIG_STEPS = 2
MIB = 1024 * 1024
F32 = jnp.float32
BF16 = jnp.bfloat16


def trig(cells):
    phases = np.arange(cells)[:, None] * np.arange(cells)[None, :] % cells
    angles = phases * (2.0 * math.pi / cells)
    pair = []
    for table in (np.cos(angles), np.sin(angles)):
        table = np.where(np.abs(table) < 1e-9, 0.0, table)
        pair.append(table.astype(np.float32).astype(ml_dtypes.bfloat16).astype(np.float32))
    return pair


def complex_rows(real, imag):
    return np.block([[real, -imag], [imag, real]])


def build_tables(cells, channels, slab, cores):
    cosine, sine = trig(cells)
    half = cells // 2
    own = half // cores
    sign = np.where(np.arange(cells) % 2 == 0, 1.0, -1.0).astype(np.float32)
    tables = {}

    def half_rows(core):
        order = [(core + turn) % cores * own + j for turn in range(cores) for j in range(own)]
        real = cosine[order].copy()
        imag = -sine[order]
        imag[order.index(0)] = sign
        return np.concatenate([real, imag], axis=0)

    def half_mix(core):
        order = [(core + turn) % cores * own + j for turn in range(cores) for j in range(own)]
        top = np.concatenate([cosine[order], sine[order]], axis=1)
        low = np.concatenate([-sine[order], cosine[order]], axis=1)
        at = order.index(0)
        one = np.ones(cells, np.float32)
        top[at] = np.concatenate([one, -sign])
        low[at] = np.concatenate([sign, one])
        return np.concatenate([top, low], axis=0)

    def flips(table, width):
        blocks = table.reshape(table.shape[0], -1, width)
        return np.stack([table, blocks[:, :, ::-1].reshape(table.shape)])

    two = np.eye(2, dtype=np.float32)
    full_rows = np.concatenate([cosine, -sine], axis=0)
    forward = complex_rows(cosine, -sine)
    inverse = complex_rows(cosine, sine)
    tables["z_even"] = np.stack([flips(np.kron(two, half_rows(core)), cells) for core in range(cores)], axis=1)
    tables["y_even"] = flips(forward, cells)
    tables["y_odd"] = flips(np.kron(two, full_rows), cells)
    tables["z_odd"] = np.stack([flips(half_mix(core), cells) for core in range(cores)], axis=1)

    group = channels // 2
    spread = []
    for core in range(cores):
        block = np.zeros((cores, 2, group, slab, 2, group, cells), np.float32)
        for turn in range(cores):
            start = (core + turn) % cores * slab
            mix = forward.reshape(2, cells, 2, cells)[:, :, :, start:start + slab]
            for channel in range(group):
                block[turn, :, channel, :, :, channel] = mix.transpose(2, 3, 0, 1)
        spread.append(block.reshape(cores * 2 * group * slab, 2 * group * cells))
    tables["x_forward"] = np.stack(spread)

    mirror = np.zeros((cells, cells), np.float32)
    mirror[np.arange(cells), -np.arange(cells) % cells] = 1.0
    eye = np.eye(cells, dtype=np.float32)
    none = np.zeros((cells, cells), np.float32)
    low = 0.5 * np.block([[eye + mirror, none], [none, eye - mirror]])
    high = 0.5 * np.block([[none, eye + mirror], [mirror - eye, none]])
    plain = np.eye(2 * cells, dtype=np.float32)
    tables["unpack"] = np.stack(
        [np.concatenate([low, high] if core == 0 else [plain, 0.0 * plain], axis=0) for core in range(cores)]
    )

    back = []
    for core in range(cores):
        block = np.zeros((LIG_STEPS, 2, cells, 2, cores, LIG_STEPS, slab), np.float32)
        parts = inverse.reshape(2, cells, 2, cells)
        for turn in range(cores):
            start = (core + turn) % cores * slab
            for pose in range(LIG_STEPS):
                block[pose, :, :, :, turn, pose] = parts[:, start:start + slab].transpose(2, 3, 0, 1)
        back.append(block.reshape(LIG_STEPS * 2 * cells, 2 * cores * LIG_STEPS * slab))
    tables["x_inverse"] = np.stack(back)
    tables["y_inverse"] = inverse

    last = []
    for core in range(cores):
        order = [(core + turn) % cores * own + j for turn in range(cores) for j in range(own)]
        real = 2.0 * cosine[order]
        imag = -2.0 * sine[order]
        at = order.index(0)
        real[at] = 1.0
        imag[at] = sign
        last.append(np.stack([real, imag], axis=1).reshape(2 * half, cells).T)
    tables["z_inverse"] = np.stack(last)
    return {name: jnp.asarray(table.astype(ml_dtypes.bfloat16)) for name, table in tables.items()}


COST = pl.CostEstimate(flops=1000, bytes_accessed=1000, transcendentals=0)


def params(limit=24):
    return pltpu.CompilerParams(vmem_limit_bytes=limit * MIB)


def lines(value):
    return value.astype(F32).astype(BF16)


def dot(left, right):
    return jnp.dot(left, right, preferred_element_type=F32)


def dot_lanes(left, right):
    return lax.dot_general(left, right, (((1,), (1,)), ((), ())), preferred_element_type=F32)


def place(cuts, plane):
    return max(k for k in range(len(cuts) - 1) if cuts[k] <= plane)


class Sizes:
    def __init__(self, channels, slab, plane, cores):
        self.channels, self.slab, self.cores = channels, slab, cores
        self.cells = slab * cores
        self.lanes = channels * slab
        self.fold = self.lanes // self.cells
        self.tiles = plane // self.lanes
        self.own = self.cells // 2 // cores
        self.whole = (0, self.own)
        self.parts = (0, self.own * 3 // 4, self.own)
        self.size = 2 * self.cells
        self.extra = 16
        self.back = cores * LIG_STEPS * slab


def y_planes(s, table, held, pair):
    half, step = s.cells // 2, s.cells + 8
    rows = [
        jnp.concatenate([held[pl.ds(q * half + pair + k, s.cells, stride=step), :] for q in range(2)], axis=0)
        for k in range(2)
    ]
    done = dot(table[...], jnp.concatenate(rows, axis=1).astype(BF16)).astype(BF16)
    return [done[:, k * s.lanes:(k + 1) * s.lanes] for k in range(2)]


def away_kernel(s, extent, held, table, out):
    for pair in range(0, s.own, 2):
        for k, plane in enumerate(y_planes(s, table.at[0], held, s.own + pair)):
            out[(pair + k) * s.size:(pair + k + 1) * s.size, :] = plane
    out[s.own * s.size:, :] = jnp.full((s.extra, s.lanes), extent[0].astype(F32)).astype(BF16)


def away_planes(s, t, extent, held):
    vmem = pl.BlockSpec(memory_space=pltpu.VMEM)
    return pl.pallas_call(
        partial(away_kernel, s),
        in_specs=[pl.BlockSpec(memory_space=pltpu.SMEM)] + [vmem] * 2,
        out_specs=vmem,
        out_shape=jax.ShapeDtypeStruct((s.own * s.size + s.extra, s.lanes), BF16),
        compiler_params=params(),
        cost_estimate=COST,
    )(extent, held, t["y_even"])


def section_kernel(s, pieces, rotated, cuts, occ, *refs):
    cells, lanes = s.cells, s.lanes
    half, size = cells // 2, s.size
    count = 4 if rotated else 2
    if rotated:
        scalar, refs = refs[0], refs[1:]
    hbm, refs = refs[:count], refs[count:]
    outs, refs = refs[:len(cuts)], refs[len(cuts):]
    if rotated:
        small, buffer, held = refs[:3]
    else:
        small, buffer, held = None, refs[0], outs[1]
        refs = (None, None, *refs)
    tables = refs[3:3 + count]
    turned = refs[-2] if rotated else None
    sems = refs[-1]
    core = lax.axis_index("fft")

    if rotated:
        first = pltpu.make_async_copy(scalar, small, sems.at[0])
        first.start()
        first.wait()
        turns = small[0]
        is_odd = turns % 2 == 1
        picks = (
            hbm[0].at[turns // 2, core],
            hbm[1].at[turns // 2],
            hbm[2].at[jnp.where(turns == 1, 1, 0)],
            hbm[3].at[jnp.where(turns == 3, 1, 0), core],
        )
    else:
        picks = (hbm[0].at[0, core], hbm[1].at[0])
    loads = [pltpu.make_async_copy(pick, table, sems.at[1 + k]) for k, (pick, table) in enumerate(zip(picks, tables))]
    width = s.tiles // pieces * lanes
    for k in range(pieces):
        here = slice(k * width, (k + 1) * width)
        loads.append(pltpu.make_async_copy(occ.at[0, :, :, here], buffer.at[:, :, here], sems.at[1 + count + k]))
    for load in loads:
        load.start()
    for load in loads[:count]:
        load.wait()

    def lay(table, height, step):
        for tile in range(0, s.tiles, 2):
            if tile % (s.tiles // pieces) == 0:
                loads[count + tile * pieces // s.tiles].wait()
            rows = [
                lines(buffer[:, :, (tile + k) * lanes:(tile + k + 1) * lanes].reshape(lanes, lanes)) for k in range(2)
            ]
            done = dot_lanes(table[...], jnp.concatenate(rows, axis=0))
            for k in range(2):
                for fold in range(s.fold):
                    at = ((tile + k) * s.fold + fold) * step
                    held[at:at + height, :] = done[fold * height:(fold + 1) * height, k * lanes:(k + 1) * lanes]

    def column(ref, at, step):
        return ref[pl.ds(at, cells, stride=step), :]

    def put(index, value):
        group, plane = divmod(index, s.own)
        if group == 0:
            outs[0][plane * size:(plane + 1) * size, :] = value
            return
        cut = place(cuts, plane)
        plane -= cuts[cut]
        outs[1 + cut][plane * size:(plane + 1) * size, :] = value

    def even():
        step = cells + 8
        lay(tables[0], cells, step)
        for pair in range(0, half if rotated else s.own, 2):
            for k, plane in enumerate(y_planes(s, tables[1], held, pair)):
                put(pair + k, plane)

    def odd():
        step, short = size + 8, cells + 8
        lay(tables[2], size, step)
        for pair in range(0, cells, 2):
            rows = [
                jnp.concatenate([column(held, q * cells + pair + k, step) for q in range(2)], axis=0) for k in range(2)
            ]
            done = dot(tables[3][...], jnp.concatenate(rows, axis=1).astype(BF16))
            for k in range(2):
                turned[(pair + k) * short:(pair + k) * short + cells, :] = done[:, k * lanes:(k + 1) * lanes]
        for plane in range(half):
            both = [column(turned, q * half + plane, short) for q in range(2)]
            put(plane, jnp.concatenate(both, axis=0).astype(BF16))

    if rotated:
        for out in outs:
            out[out.shape[0] - s.extra:, :] = jnp.zeros((s.extra, lanes), BF16)
        pl.when(jnp.logical_not(is_odd))(even)
        pl.when(is_odd)(odd)
    else:
        even()
        outs[0][s.own * size:, :] = jnp.zeros((s.extra, lanes), BF16)


def sections(s, t, occ, scalar, rotated, cuts, pieces=2):
    cells, lanes = s.cells, s.lanes
    names = ["z_even", "y_even"] + (["y_odd", "z_odd"] if rotated else [])
    hbm = pl.BlockSpec(memory_space=pltpu.HBM)
    pin = lambda value: pltpu.with_memory_space_constraint(value, pltpu.HBM)
    scratch = [pltpu.VMEM(occ.shape[1:], jnp.int32)]
    if rotated:
        scratch.insert(0, pltpu.SMEM(scalar.shape, jnp.int32))
        scratch.append(pltpu.VMEM(((cells + 1) * (s.size + 8), lanes), F32))
    scratch += [pltpu.VMEM(t[name].shape[-2:], BF16) for name in names]
    if rotated:
        scratch.append(pltpu.VMEM(((cells + 1) * (cells + 8), lanes), F32))
    scratch.append(pltpu.SemaphoreType.DMA((1 + len(names) + pieces,)))
    rows = [s.own * s.size + s.extra]
    rows += [(high - low) * s.size + s.extra for low, high in zip(cuts, cuts[1:])]
    shapes = [jax.ShapeDtypeStruct((count, lanes), BF16) for count in rows]
    if not rotated:
        shapes[1:] = [jax.ShapeDtypeStruct(((cells + 1) * (cells + 8), lanes), F32)]
    return pl.pallas_call(
        partial(section_kernel, s, pieces, rotated, cuts),
        in_specs=[hbm] + [pl.BlockSpec(memory_space=pl.ANY)] * rotated + [hbm] * len(names),
        out_specs=[pl.BlockSpec(memory_space=pltpu.VMEM)] * len(shapes),
        out_shape=shapes,
        scratch_shapes=scratch,
        compiler_params=params(),
        cost_estimate=COST,
    )(pin(occ), *([scalar] if rotated else []), *[pin(t[name]) for name in names])


def regroup(s, parts):
    half = s.lanes // 2
    lane = lax.broadcasted_iota(jnp.int32, parts[0].shape, 1)
    low, high = [], []
    for one, two in zip(parts[::2], parts[1::2]):
        low.append(jnp.where(lane < half, one, pltpu.roll(two, half, 1)))
        high.append(jnp.where(lane < half, pltpu.roll(one, half, 1), two))
    return [jnp.concatenate(low, axis=1), jnp.concatenate(high, axis=1)]


def x_rows(s, cuts, own, others, plane):
    cut = place(cuts, plane)
    parts = []
    for ref, at in ((own, plane * s.size), (others[cut], (plane - cuts[cut]) * s.size)):
        for p in range(2):
            parts.append(ref[at + p * s.cells:at + (p + 1) * s.cells, :])
    return regroup(s, parts)


def unpacked_rows(s, own, others, unpack):
    cells = s.cells
    done = [dot(unpack, ref[:s.size, :]).astype(BF16) for ref in (own, others[0])]
    return [
        regroup(s, [value[(2 * k + p) * cells:(2 * k + p + 1) * cells] for value in done for p in range(2)])
        for k in range(2)
    ]


def x_transform(s, rows, table):
    done = dot(jnp.concatenate([row[k] for k in range(2) for row in rows], axis=0), table)
    count = len(rows) * s.cells
    return done[:count], done[count:]


def spectrum_kernel(s, cuts, per, weight, table, unpack, own, *refs):
    others, (main, last) = refs[:-2], refs[-2:]
    volume = 1.0 / float(s.cells) ** 3
    core = lax.axis_index("fft")

    lane = lax.broadcasted_iota(jnp.int32, (s.cells, s.size), 1)
    scales = [
        jnp.where(lane < s.cells, weight[2 * k], weight[2 * k + 1]) * volume for k in range(2)
    ]

    def put(ref, at, values):
        for k, value in enumerate(values):
            for q in range(2):
                from_lanes = slice(q * s.size, (q + 1) * s.size)
                to_lanes = slice((2 * k + q) * s.size, (2 * k + q + 1) * s.size)
                for row in range(0, value.shape[0], s.cells):
                    ref[at + row:at + row + s.cells, to_lanes] = (
                        value[row:row + s.cells, from_lanes] * scales[k]
                    ).astype(BF16)

    for start in range(0, s.own, per):
        rows = [x_rows(s, cuts, own, others, plane) for plane in range(start, start + per)]
        if start == 0:
            rows[0], high = unpacked_rows(s, own, others, unpack[core])
            rows.append(high)
        done = x_transform(s, rows, table[core])
        put(main, start * s.cells, [value[:per * s.cells] for value in done])
        if start == 0:
            put(last, 0, [value[per * s.cells:] for value in done])


def spectrum(s, t, weight, own, others, cuts, per=4):
    width = s.channels * s.size
    vmem = pl.BlockSpec(memory_space=pltpu.VMEM)
    return pl.pallas_call(
        partial(spectrum_kernel, s, cuts, per),
        in_specs=[pl.BlockSpec(memory_space=pltpu.SMEM)] + [vmem] * (3 + len(others)),
        out_specs=[vmem] * 2,
        out_shape=[jax.ShapeDtypeStruct((s.own * s.cells, width), BF16), jax.ShapeDtypeStruct((s.cells, width), BF16)],
        compiler_params=params(),
        cost_estimate=COST,
    )(weight, t["x_forward"], t["unpack"], own, *others)


def cross_kernel(s, cuts, planes, most, table, unpack, x_inverse, y_inverse, *refs):
    poses, tops = refs[:LIG_STEPS], refs[LIG_STEPS:2 * LIG_STEPS]
    own, others = refs[2 * LIG_STEPS], refs[2 * LIG_STEPS + 1:-2]
    keep, send = refs[-2:]
    cells, width, lanes = s.cells, s.size, s.back
    core = lax.axis_index("fft")
    lane = lax.broadcasted_iota(jnp.int32, (cells, width), 1)
    is_real = lane < cells
    kept = lax.broadcasted_iota(jnp.int32, (cells // 2, lanes), 1) < lanes // 2

    def correlate(receptor, pose):
        real = imag = None
        for k, value in enumerate(receptor):
            one = [value[:, q * width:(q + 1) * width] for q in range(2)]
            two = [pose[:, (2 * k + q) * width:(2 * k + q + 1) * width].astype(F32) for q in range(2)]
            same = one[0] * two[0] + one[1] * two[1]
            turned = one[1] * two[0] - one[0] * two[1]
            real = same if real is None else real + same
            imag = turned if imag is None else imag + turned
        return jnp.where(is_real, real, imag) + pltpu.roll(jnp.where(is_real, imag, real), cells, 1)

    for start in range(planes[0], planes[1], most):
        per = min(most, planes[1] - start)
        rows = [x_rows(s, cuts, own, others, plane) for plane in range(start, start + per)]
        if start == 0:
            rows[0], high = unpacked_rows(s, own, others, unpack[core])
            rows.append(high)
        done = x_transform(s, rows, table[core])
        cross = []
        for k in range(per):
            both = []
            for pose in range(LIG_STEPS):
                at = (start + k) * cells
                value = correlate([half[k * cells:(k + 1) * cells] for half in done], poses[pose][at:at + cells, :])
                if start + k == 0:
                    row = lax.broadcasted_iota(jnp.int32, (cells, width), 0)
                    at_zero = (row == 0) & ((lane == 0) | (lane == cells)) & (core == 0)
                    value = jnp.where(at_zero, 0.0, value)
                    top = pltpu.roll(correlate([half[per * cells:] for half in done], tops[pose][...]), cells, 1)
                    value = value + jnp.where(is_real, -top, top)
                both.append(value.astype(BF16))
            cross.append(jnp.concatenate(both, axis=1))
        back = dot(jnp.concatenate(cross, axis=0), x_inverse[core]).astype(BF16)
        for pair in range(0, per, 2):
            sides = []
            for k in range(2):
                here = back[(pair + k) * cells:(pair + k + 1) * cells]
                sides.append(jnp.concatenate([here[:, :lanes], here[:, lanes:]], axis=0))
            out = dot(y_inverse[...], jnp.concatenate(sides, axis=1))
            for k in range(2):
                for q in range(2):
                    value = out[q * cells:(q + 1) * cells, k * lanes:(k + 1) * lanes]
                    low, high = value[:cells // 2], value[cells // 2:]
                    at = (start - planes[0] + pair + k) * cells + q * cells // 2
                    at = slice(at, at + cells // 2)
                    keep[at, :] = jnp.where(kept, low, pltpu.roll(high, lanes // 2, 1)).astype(BF16)
                    send[at, :] = jnp.where(kept, pltpu.roll(low, lanes // 2, 1), high).astype(BF16)


def cross_back(s, t, own, others, poses, tops, cuts, planes, per=4):
    vmem = pl.BlockSpec(memory_space=pltpu.VMEM)
    shape = jax.ShapeDtypeStruct(((planes[1] - planes[0]) * s.cells, s.back), BF16)
    used = range(place(cuts, planes[0]), place(cuts, planes[1] - 1) + 1)
    others, cuts = [others[k] for k in used], tuple(cuts[used[0]:used[-1] + 2])
    operands = [t["x_forward"], t["unpack"], t["x_inverse"], t["y_inverse"], *poses, *tops, own, *others]
    return pl.pallas_call(
        partial(cross_kernel, s, cuts, planes, per),
        in_specs=[vmem] * len(operands),
        out_specs=[vmem] * 2,
        out_shape=[shape] * 2,
        compiler_params=params(),
        cost_estimate=COST,
    )(*operands)


def peak_kernel(s, count, last, load, table, *refs):
    parts = refs[:count]
    earlier, out, held = refs[count:-2], refs[-2], refs[-1]
    cells = s.cells
    low = cells // 2
    core = lax.axis_index("fft")
    step = low + 8
    at = 0
    for part in parts:
        for row in range(0, part.shape[0], low):
            held[at:at + low, :] = part[row:row + low, :].astype(F32)
            at += step
    best = None
    for pair in range(0, low, 2):
        columns = [held[pl.ds(pair + k, cells, stride=step), :] for k in range(2)]
        scores = dot(table[core], jnp.concatenate(columns, axis=1).astype(BF16))
        here = jnp.maximum(scores[:, :s.back], scores[:, s.back:])
        best = here if best is None else jnp.maximum(best, here)
    row = jnp.max(best, axis=0, keepdims=True)
    row = jnp.maximum(row, pltpu.roll(row, s.back // 2, 1)) * (1.0 / (cells * math.sqrt(cells)))
    plane = lax.broadcasted_iota(jnp.int32, row.shape, 1) % s.slab + core * s.slab
    extent = load[load.shape[0] - s.extra:, :].astype(F32)[:1]
    row = jnp.where(plane.astype(F32) < extent, row, 0.0)
    if not last:
        out[...] = row
        return
    for index, value in enumerate([ref[...] for ref in earlier] + [row]):
        for pose in range(LIG_STEPS):
            out[0, index, pose:pose + 1, :] = value[:, pose * s.slab:(pose + 1) * s.slab]


def peaks(s, t, load, parts, earlier, last):
    vmem = pl.BlockSpec(memory_space=pltpu.VMEM)
    shape = (1, REC_STEPS, LIG_STEPS, s.slab) if last else (1, s.back)
    return pl.pallas_call(
        partial(peak_kernel, s, len(parts), last),
        in_specs=[vmem] * (2 + len(parts) + len(earlier)),
        out_specs=vmem,
        out_shape=jax.ShapeDtypeStruct(shape, F32),
        scratch_shapes=[pltpu.VMEM(((s.cells + 1) * (s.cells // 2 + 8), s.back), F32)],
        compiler_params=params(),
        cost_estimate=COST,
    )(load, t["z_inverse"], *parts, *earlier)


def passed_along(value, axis, steps=1):
    count = lax.axis_size(axis)
    return lax.ppermute(value, axis, [(source, (source + steps) % count) for source in range(count)])


def passed_across(value, axis):
    count, cores = lax.axis_size(axis), lax.axis_size("fft")
    pairs = [
        (place * cores + core, (place + 1) % count * cores + (core + 1) % cores)
        for place in range(count)
        for core in range(cores)
    ]
    return lax.ppermute(value, (axis, "fft"), pairs)


def after(value, *others):
    return lax.optimization_barrier((value, *others))[0]


def shards(tables, receptor_occupancy, ligand_occupancy, rot_index, receptor_extent, channel_weight):
    _, channels, slab, plane = receptor_occupancy.shape
    s = Sizes(channels, slab, plane, lax.axis_size("fft"))
    t = tables(s)
    swapped = lambda parts: [passed_along(part, "fft") for part in parts]

    own, held = sections(s, t, receptor_occupancy, None, False, s.whole)
    away = [away_planes(s, t, after(receptor_extent, own), held)]
    receptors = []
    receptors.append((passed_along(own, "rec"), [passed_across(part, "rec") for part in away]))

    ligand_occupancy = after(ligand_occupancy, *away)
    pose, *pose_away = sections(s, t, ligand_occupancy, rot_index, True, s.whole)
    pose_others = swapped([after(part, receptors[0][0]) for part in pose_away])
    next_pose, next_others = passed_along(pose, "lig"), [passed_across(part, "lig") for part in pose_away]
    receptors.insert(0, (own, swapped([after(part, next_pose) for part in away])))
    spectra = [spectrum(s, t, channel_weight, pose, pose_others, s.whole)]

    own, others = receptors[1]
    receptors[1] = (own, others)
    ends = [part * s.size for part in s.parts[:-1]] + [None]
    cuts = [others[0][low:high] for low, high in zip(ends, ends[1:])]
    receptors.append((passed_along(own, "rec"), [passed_along(part, "rec") for part in cuts]))

    spectra.append(spectrum(s, t, channel_weight, next_pose, next_others, s.whole))
    poses, tops = [main for main, _ in spectra], [top for _, top in spectra]

    rows = []
    for step, (own, others) in enumerate(receptors):
        last = step + 1 == REC_STEPS
        cuts = s.parts if last else s.whole
        ranges = list(zip(cuts, cuts[1:]))
        if last:
            own = after(own, *rows)
        sides = [cross_back(s, t, own, others, poses, tops, cuts, planes) for planes in ranges]
        parts = [keep for keep, _ in sides] + swapped([send for _, send in sides])
        rows.append(peaks(s, t, others[-1], parts, rows if last else [], last))
    return rows[-1]


def solution(mesh):
    placed = (
        P(("groups", "rec", "lig"), None, "fft", None),
        P(("groups", "rec", "lig"), None, "fft", None),
        P(("groups", "rec", "lig")),
        P(("groups", "rec", "lig")),
        P(),
    )
    tables = lambda s: build_tables(s.cells, s.channels, s.slab, s.cores)
    return jax.shard_map(
        partial(shards, tables),
        mesh=mesh,
        in_specs=placed,
        out_specs=P(("groups", "rec", "lig"), None, None, "fft"),
        check_vma=False,
    )
```

```python
from functools import partial
import math

import jax
import jax.numpy as jnp
import ml_dtypes
import numpy as np
from jax import lax
from jax.experimental import pallas as pl
from jax.experimental.pallas import tpu as pltpu
from jax.sharding import PartitionSpec as P

REC_STEPS = 3
LIG_STEPS = 2
MIB = 1024 * 1024
F32 = jnp.float32
BF16 = jnp.bfloat16


def trig(cells):
    phases = np.arange(cells)[:, None] * np.arange(cells)[None, :] % cells
    angles = phases * (2.0 * math.pi / cells)
    pair = []
    for table in (np.cos(angles), np.sin(angles)):
        table = np.where(np.abs(table) < 1e-9, 0.0, table)
        pair.append(table.astype(np.float32).astype(ml_dtypes.bfloat16).astype(np.float32))
    return pair


def complex_rows(real, imag):
    return np.block([[real, -imag], [imag, real]])


def build_tables(cells, channels, slab, cores):
    cosine, sine = trig(cells)
    half = cells // 2
    own = half // cores
    sign = np.where(np.arange(cells) % 2 == 0, 1.0, -1.0).astype(np.float32)
    tables = {}

    def half_rows(core):
        order = [(core + turn) % cores * own + j for turn in range(cores) for j in range(own)]
        real = cosine[order].copy()
        imag = -sine[order]
        imag[order.index(0)] = sign
        return np.concatenate([real, imag], axis=0)

    def half_mix(core):
        order = [(core + turn) % cores * own + j for turn in range(cores) for j in range(own)]
        top = np.concatenate([cosine[order], sine[order]], axis=1)
        low = np.concatenate([-sine[order], cosine[order]], axis=1)
        at = order.index(0)
        one = np.ones(cells, np.float32)
        top[at] = np.concatenate([one, -sign])
        low[at] = np.concatenate([sign, one])
        return np.concatenate([top, low], axis=0)

    def flips(table, width):
        blocks = table.reshape(table.shape[0], -1, width)
        return np.stack([table, blocks[:, :, ::-1].reshape(table.shape)])

    two = np.eye(2, dtype=np.float32)
    full_rows = np.concatenate([cosine, -sine], axis=0)
    forward = complex_rows(cosine, -sine)
    inverse = complex_rows(cosine, sine)
    tables["z_even"] = np.stack([flips(np.kron(two, half_rows(core)), cells) for core in range(cores)], axis=1)
    tables["y_even"] = flips(forward, cells)
    tables["y_odd"] = flips(np.kron(two, full_rows), cells)
    tables["z_odd"] = np.stack([flips(half_mix(core), cells) for core in range(cores)], axis=1)

    group = channels // 2
    spread = []
    for core in range(cores):
        block = np.zeros((cores, 2, group, slab, 2, group, cells), np.float32)
        for turn in range(cores):
            start = (core + turn) % cores * slab
            mix = forward.reshape(2, cells, 2, cells)[:, :, :, start:start + slab]
            for channel in range(group):
                block[turn, :, channel, :, :, channel] = mix.transpose(2, 3, 0, 1)
        spread.append(block.reshape(cores * 2 * group * slab, 2 * group * cells))
    tables["x_forward"] = np.stack(spread)

    mirror = np.zeros((cells, cells), np.float32)
    mirror[np.arange(cells), -np.arange(cells) % cells] = 1.0
    eye = np.eye(cells, dtype=np.float32)
    none = np.zeros((cells, cells), np.float32)
    low = 0.5 * np.block([[eye + mirror, none], [none, eye - mirror]])
    high = 0.5 * np.block([[none, eye + mirror], [mirror - eye, none]])
    plain = np.eye(2 * cells, dtype=np.float32)
    tables["unpack"] = np.stack(
        [np.concatenate([low, high] if core == 0 else [plain, 0.0 * plain], axis=0) for core in range(cores)]
    )

    back = []
    for core in range(cores):
        block = np.zeros((LIG_STEPS, 2, cells, 2, cores, LIG_STEPS, slab), np.float32)
        parts = inverse.reshape(2, cells, 2, cells)
        for turn in range(cores):
            start = (core + turn) % cores * slab
            for pose in range(LIG_STEPS):
                block[pose, :, :, :, turn, pose] = parts[:, start:start + slab].transpose(2, 3, 0, 1)
        back.append(block.reshape(LIG_STEPS * 2 * cells, 2 * cores * LIG_STEPS * slab))
    tables["x_inverse"] = np.stack(back)
    tables["y_inverse"] = inverse

    last = []
    for core in range(cores):
        order = [(core + turn) % cores * own + j for turn in range(cores) for j in range(own)]
        real = 2.0 * cosine[order]
        imag = -2.0 * sine[order]
        at = order.index(0)
        real[at] = 1.0
        imag[at] = sign
        last.append(np.stack([real, imag], axis=1).reshape(2 * half, cells).T)
    tables["z_inverse"] = np.stack(last)
    return {name: jnp.asarray(table.astype(ml_dtypes.bfloat16)) for name, table in tables.items()}


COST = pl.CostEstimate(flops=1000, bytes_accessed=1000, transcendentals=0)


def params(limit=24):
    return pltpu.CompilerParams(vmem_limit_bytes=limit * MIB)


def lines(value):
    return value.astype(F32).astype(BF16)


def dot(left, right):
    return jnp.dot(left, right, preferred_element_type=F32)


def dot_lanes(left, right):
    return lax.dot_general(left, right, (((1,), (1,)), ((), ())), preferred_element_type=F32)


def place(cuts, plane):
    return max(k for k in range(len(cuts) - 1) if cuts[k] <= plane)


class Sizes:
    def __init__(self, channels, slab, plane, cores):
        self.channels, self.slab, self.cores = channels, slab, cores
        self.cells = slab * cores
        self.lanes = channels * slab
        self.fold = self.lanes // self.cells
        self.tiles = plane // self.lanes
        self.own = self.cells // 2 // cores
        self.whole = (0, self.own)
        self.parts = (0, self.own * 3 // 4, self.own)
        self.size = 2 * self.cells
        self.extra = 16
        self.back = cores * LIG_STEPS * slab


def y_planes(s, table, held, pair):
    half, step = s.cells // 2, s.cells + 8
    rows = [
        jnp.concatenate([held[pl.ds(q * half + pair + k, s.cells, stride=step), :] for q in range(2)], axis=0)
        for k in range(2)
    ]
    done = dot(table[...], jnp.concatenate(rows, axis=1).astype(BF16)).astype(BF16)
    return [done[:, k * s.lanes:(k + 1) * s.lanes] for k in range(2)]


def away_kernel(s, extent, held, table, out):
    for pair in range(0, s.own, 2):
        for k, plane in enumerate(y_planes(s, table.at[0], held, s.own + pair)):
            out[(pair + k) * s.size:(pair + k + 1) * s.size, :] = plane
    out[s.own * s.size:, :] = jnp.full((s.extra, s.lanes), extent[0].astype(F32)).astype(BF16)


def away_planes(s, t, extent, held):
    vmem = pl.BlockSpec(memory_space=pltpu.VMEM)
    return pl.pallas_call(
        partial(away_kernel, s),
        in_specs=[pl.BlockSpec(memory_space=pltpu.SMEM)] + [vmem] * 2,
        out_specs=vmem,
        out_shape=jax.ShapeDtypeStruct((s.own * s.size + s.extra, s.lanes), BF16),
        compiler_params=params(),
        cost_estimate=COST,
    )(extent, held, t["y_even"])


def section_kernel(s, pieces, rotated, cuts, occ, *refs):
    cells, lanes = s.cells, s.lanes
    half, size = cells // 2, s.size
    count = 4 if rotated else 2
    if rotated:
        scalar, refs = refs[0], refs[1:]
    hbm, refs = refs[:count], refs[count:]
    outs, refs = refs[:len(cuts)], refs[len(cuts):]
    if rotated:
        small, buffer, held = refs[:3]
    else:
        small, buffer, held = None, refs[0], outs[1]
        refs = (None, None, *refs)
    tables = refs[3:3 + count]
    turned = refs[-2] if rotated else None
    sems = refs[-1]
    core = lax.axis_index("fft")

    if rotated:
        first = pltpu.make_async_copy(scalar, small, sems.at[0])
        first.start()
        first.wait()
        turns = small[0]
        is_odd = turns % 2 == 1
        picks = (
            hbm[0].at[turns // 2, core],
            hbm[1].at[turns // 2],
            hbm[2].at[jnp.where(turns == 1, 1, 0)],
            hbm[3].at[jnp.where(turns == 3, 1, 0), core],
        )
    else:
        picks = (hbm[0].at[0, core], hbm[1].at[0])
    loads = [pltpu.make_async_copy(pick, table, sems.at[1 + k]) for k, (pick, table) in enumerate(zip(picks, tables))]
    width = s.tiles // pieces * lanes
    for k in range(pieces):
        here = slice(k * width, (k + 1) * width)
        loads.append(pltpu.make_async_copy(occ.at[0, :, :, here], buffer.at[:, :, here], sems.at[1 + count + k]))
    for load in loads:
        load.start()
    for load in loads[:count]:
        load.wait()

    def lay(table, height, step):
        for tile in range(0, s.tiles, 2):
            if tile % (s.tiles // pieces) == 0:
                loads[count + tile * pieces // s.tiles].wait()
            rows = [
                lines(buffer[:, :, (tile + k) * lanes:(tile + k + 1) * lanes].reshape(lanes, lanes)) for k in range(2)
            ]
            done = dot_lanes(table[...], jnp.concatenate(rows, axis=0))
            for k in range(2):
                for fold in range(s.fold):
                    at = ((tile + k) * s.fold + fold) * step
                    held[at:at + height, :] = done[fold * height:(fold + 1) * height, k * lanes:(k + 1) * lanes]

    def column(ref, at, step):
        return ref[pl.ds(at, cells, stride=step), :]

    def put(index, value):
        group, plane = divmod(index, s.own)
        if group == 0:
            outs[0][plane * size:(plane + 1) * size, :] = value
            return
        cut = place(cuts, plane)
        plane -= cuts[cut]
        outs[1 + cut][plane * size:(plane + 1) * size, :] = value

    def even():
        step = cells + 8
        lay(tables[0], cells, step)
        for pair in range(0, half if rotated else s.own, 2):
            for k, plane in enumerate(y_planes(s, tables[1], held, pair)):
                put(pair + k, plane)

    def odd():
        step, short = size + 8, cells + 8
        lay(tables[2], size, step)
        for pair in range(0, cells, 2):
            rows = [
                jnp.concatenate([column(held, q * cells + pair + k, step) for q in range(2)], axis=0) for k in range(2)
            ]
            done = dot(tables[3][...], jnp.concatenate(rows, axis=1).astype(BF16))
            for k in range(2):
                turned[(pair + k) * short:(pair + k) * short + cells, :] = done[:, k * lanes:(k + 1) * lanes]
        for plane in range(half):
            both = [column(turned, q * half + plane, short) for q in range(2)]
            put(plane, jnp.concatenate(both, axis=0).astype(BF16))

    if rotated:
        for out in outs:
            out[out.shape[0] - s.extra:, :] = jnp.zeros((s.extra, lanes), BF16)
        pl.when(jnp.logical_not(is_odd))(even)
        pl.when(is_odd)(odd)
    else:
        even()
        outs[0][s.own * size:, :] = jnp.zeros((s.extra, lanes), BF16)


def sections(s, t, occ, scalar, rotated, cuts, pieces=2):
    cells, lanes = s.cells, s.lanes
    names = ["z_even", "y_even"] + (["y_odd", "z_odd"] if rotated else [])
    hbm = pl.BlockSpec(memory_space=pltpu.HBM)
    pin = lambda value: pltpu.with_memory_space_constraint(value, pltpu.HBM)
    scratch = [pltpu.VMEM(occ.shape[1:], jnp.int32)]
    if rotated:
        scratch.insert(0, pltpu.SMEM(scalar.shape, jnp.int32))
        scratch.append(pltpu.VMEM(((cells + 1) * (s.size + 8), lanes), F32))
    scratch += [pltpu.VMEM(t[name].shape[-2:], BF16) for name in names]
    if rotated:
        scratch.append(pltpu.VMEM(((cells + 1) * (cells + 8), lanes), F32))
    scratch.append(pltpu.SemaphoreType.DMA((1 + len(names) + pieces,)))
    rows = [s.own * s.size + s.extra]
    rows += [(high - low) * s.size + s.extra for low, high in zip(cuts, cuts[1:])]
    shapes = [jax.ShapeDtypeStruct((count, lanes), BF16) for count in rows]
    if not rotated:
        shapes[1:] = [jax.ShapeDtypeStruct(((cells + 1) * (cells + 8), lanes), F32)]
    return pl.pallas_call(
        partial(section_kernel, s, pieces, rotated, cuts),
        in_specs=[hbm] + [pl.BlockSpec(memory_space=pl.ANY)] * rotated + [hbm] * len(names),
        out_specs=[pl.BlockSpec(memory_space=pltpu.VMEM)] * len(shapes),
        out_shape=shapes,
        scratch_shapes=scratch,
        compiler_params=params(),
        cost_estimate=COST,
    )(pin(occ), *([scalar] if rotated else []), *[pin(t[name]) for name in names])


def regroup(s, parts):
    half = s.lanes // 2
    lane = lax.broadcasted_iota(jnp.int32, parts[0].shape, 1)
    low, high = [], []
    for one, two in zip(parts[::2], parts[1::2]):
        low.append(jnp.where(lane < half, one, pltpu.roll(two, half, 1)))
        high.append(jnp.where(lane < half, pltpu.roll(one, half, 1), two))
    return [jnp.concatenate(low, axis=1), jnp.concatenate(high, axis=1)]


def x_rows(s, cuts, own, others, plane):
    cut = place(cuts, plane)
    parts = []
    for ref, at in ((own, plane * s.size), (others[cut], (plane - cuts[cut]) * s.size)):
        for p in range(2):
            parts.append(ref[at + p * s.cells:at + (p + 1) * s.cells, :])
    return regroup(s, parts)


def unpacked_rows(s, own, others, unpack):
    cells = s.cells
    done = [dot(unpack, ref[:s.size, :]).astype(BF16) for ref in (own, others[0])]
    return [
        regroup(s, [value[(2 * k + p) * cells:(2 * k + p + 1) * cells] for value in done for p in range(2)])
        for k in range(2)
    ]


def x_transform(s, rows, table):
    done = dot(jnp.concatenate([row[k] for k in range(2) for row in rows], axis=0), table)
    count = len(rows) * s.cells
    return done[:count], done[count:]


def spectrum_kernel(s, cuts, per, weight, table, unpack, own, *refs):
    others, (main, last) = refs[:-2], refs[-2:]
    volume = 1.0 / float(s.cells) ** 3
    core = lax.axis_index("fft")

    lane = lax.broadcasted_iota(jnp.int32, (s.cells, s.size), 1)
    scales = [
        jnp.where(lane < s.cells, weight[2 * k], weight[2 * k + 1]) * volume for k in range(2)
    ]

    def put(ref, at, values):
        for k, value in enumerate(values):
            for q in range(2):
                from_lanes = slice(q * s.size, (q + 1) * s.size)
                to_lanes = slice((2 * k + q) * s.size, (2 * k + q + 1) * s.size)
                for row in range(0, value.shape[0], s.cells):
                    ref[at + row:at + row + s.cells, to_lanes] = (
                        value[row:row + s.cells, from_lanes] * scales[k]
                    ).astype(BF16)

    for start in range(0, s.own, per):
        rows = [x_rows(s, cuts, own, others, plane) for plane in range(start, start + per)]
        if start == 0:
            rows[0], high = unpacked_rows(s, own, others, unpack[core])
            rows.append(high)
        done = x_transform(s, rows, table[core])
        put(main, start * s.cells, [value[:per * s.cells] for value in done])
        if start == 0:
            put(last, 0, [value[per * s.cells:] for value in done])


def spectrum(s, t, weight, own, others, cuts, per=4):
    width = s.channels * s.size
    vmem = pl.BlockSpec(memory_space=pltpu.VMEM)
    return pl.pallas_call(
        partial(spectrum_kernel, s, cuts, per),
        in_specs=[pl.BlockSpec(memory_space=pltpu.SMEM)] + [vmem] * (3 + len(others)),
        out_specs=[vmem] * 2,
        out_shape=[jax.ShapeDtypeStruct((s.own * s.cells, width), BF16), jax.ShapeDtypeStruct((s.cells, width), BF16)],
        compiler_params=params(),
        cost_estimate=COST,
    )(weight, t["x_forward"], t["unpack"], own, *others)


def cross_kernel(s, cuts, planes, most, table, unpack, x_inverse, y_inverse, *refs):
    poses, tops = refs[:LIG_STEPS], refs[LIG_STEPS:2 * LIG_STEPS]
    own, others = refs[2 * LIG_STEPS], refs[2 * LIG_STEPS + 1:-2]
    keep, send = refs[-2:]
    cells, width, lanes = s.cells, s.size, s.back
    core = lax.axis_index("fft")
    lane = lax.broadcasted_iota(jnp.int32, (cells, width), 1)
    is_real = lane < cells
    kept = lax.broadcasted_iota(jnp.int32, (cells // 2, lanes), 1) < lanes // 2

    def correlate(receptor, pose):
        real = imag = None
        for k, value in enumerate(receptor):
            one = [value[:, q * width:(q + 1) * width] for q in range(2)]
            two = [pose[:, (2 * k + q) * width:(2 * k + q + 1) * width].astype(F32) for q in range(2)]
            same = one[0] * two[0] + one[1] * two[1]
            turned = one[1] * two[0] - one[0] * two[1]
            real = same if real is None else real + same
            imag = turned if imag is None else imag + turned
        return jnp.where(is_real, real, imag) + pltpu.roll(jnp.where(is_real, imag, real), cells, 1)

    groups = []
    for start in range(planes[0], planes[1], most):
        per = min(most, planes[1] - start)
        rows = [x_rows(s, cuts, own, others, plane) for plane in range(start, start + per)]
        if start == 0:
            rows[0], high = unpacked_rows(s, own, others, unpack[core])
            rows.append(high)
        groups.append((start, per, x_transform(s, rows, table[core])))
    for start, per, done in groups:
        cross = []
        for k in range(per):
            both = []
            for pose in range(LIG_STEPS):
                at = (start + k) * cells
                value = correlate([half[k * cells:(k + 1) * cells] for half in done], poses[pose][at:at + cells, :])
                if start + k == 0:
                    row = lax.broadcasted_iota(jnp.int32, (cells, width), 0)
                    at_zero = (row == 0) & ((lane == 0) | (lane == cells)) & (core == 0)
                    value = jnp.where(at_zero, 0.0, value)
                    top = pltpu.roll(correlate([half[per * cells:] for half in done], tops[pose][...]), cells, 1)
                    value = value + jnp.where(is_real, -top, top)
                both.append(value.astype(BF16))
            cross.append(jnp.concatenate(both, axis=1))
        back = dot(jnp.concatenate(cross, axis=0), x_inverse[core]).astype(BF16)
        for pair in range(0, per, 2):
            sides = []
            for k in range(2):
                here = back[(pair + k) * cells:(pair + k + 1) * cells]
                sides.append(jnp.concatenate([here[:, :lanes], here[:, lanes:]], axis=0))
            out = dot(y_inverse[...], jnp.concatenate(sides, axis=1))
            for k in range(2):
                for q in range(2):
                    value = out[q * cells:(q + 1) * cells, k * lanes:(k + 1) * lanes]
                    low, high = value[:cells // 2], value[cells // 2:]
                    at = (start - planes[0] + pair + k) * cells + q * cells // 2
                    at = slice(at, at + cells // 2)
                    keep[at, :] = jnp.where(kept, low, pltpu.roll(high, lanes // 2, 1)).astype(BF16)
                    send[at, :] = jnp.where(kept, pltpu.roll(low, lanes // 2, 1), high).astype(BF16)


def cross_back(s, t, own, others, poses, tops, cuts, planes, per=4):
    vmem = pl.BlockSpec(memory_space=pltpu.VMEM)
    shape = jax.ShapeDtypeStruct(((planes[1] - planes[0]) * s.cells, s.back), BF16)
    used = range(place(cuts, planes[0]), place(cuts, planes[1] - 1) + 1)
    others, cuts = [others[k] for k in used], tuple(cuts[used[0]:used[-1] + 2])
    operands = [t["x_forward"], t["unpack"], t["x_inverse"], t["y_inverse"], *poses, *tops, own, *others]
    return pl.pallas_call(
        partial(cross_kernel, s, cuts, planes, per),
        in_specs=[vmem] * len(operands),
        out_specs=[vmem] * 2,
        out_shape=[shape] * 2,
        compiler_params=params(),
        cost_estimate=COST,
    )(*operands)


def peak_kernel(s, count, last, load, table, *refs):
    parts = refs[:count]
    earlier, out, held = refs[count:-2], refs[-2], refs[-1]
    cells = s.cells
    low = cells // 2
    core = lax.axis_index("fft")
    step = low + 8
    at = 0
    for part in parts:
        for row in range(0, part.shape[0], low):
            held[at:at + low, :] = part[row:row + low, :].astype(F32)
            at += step
    best = None
    for pair in range(0, low, 2):
        columns = [held[pl.ds(pair + k, cells, stride=step), :] for k in range(2)]
        scores = dot(table[core], jnp.concatenate(columns, axis=1).astype(BF16))
        here = jnp.maximum(scores[:, :s.back], scores[:, s.back:])
        best = here if best is None else jnp.maximum(best, here)
    row = jnp.max(best, axis=0, keepdims=True)
    row = jnp.maximum(row, pltpu.roll(row, s.back // 2, 1)) * (1.0 / (cells * math.sqrt(cells)))
    plane = lax.broadcasted_iota(jnp.int32, row.shape, 1) % s.slab + core * s.slab
    extent = load[load.shape[0] - s.extra:, :].astype(F32)[:1]
    row = jnp.where(plane.astype(F32) < extent, row, 0.0)
    if not last:
        out[...] = row
        return
    for index, value in enumerate([ref[...] for ref in earlier] + [row]):
        for pose in range(LIG_STEPS):
            out[0, index, pose:pose + 1, :] = value[:, pose * s.slab:(pose + 1) * s.slab]


def peaks(s, t, load, parts, earlier, last):
    vmem = pl.BlockSpec(memory_space=pltpu.VMEM)
    shape = (1, REC_STEPS, LIG_STEPS, s.slab) if last else (1, s.back)
    return pl.pallas_call(
        partial(peak_kernel, s, len(parts), last),
        in_specs=[vmem] * (2 + len(parts) + len(earlier)),
        out_specs=vmem,
        out_shape=jax.ShapeDtypeStruct(shape, F32),
        scratch_shapes=[pltpu.VMEM(((s.cells + 1) * (s.cells // 2 + 8), s.back), F32)],
        compiler_params=params(),
        cost_estimate=COST,
    )(load, t["z_inverse"], *parts, *earlier)


def passed_along(value, axis, steps=1):
    count = lax.axis_size(axis)
    return lax.ppermute(value, axis, [(source, (source + steps) % count) for source in range(count)])


def passed_across(value, axis):
    count, cores = lax.axis_size(axis), lax.axis_size("fft")
    pairs = [
        (place * cores + core, (place + 1) % count * cores + (core + 1) % cores)
        for place in range(count)
        for core in range(cores)
    ]
    return lax.ppermute(value, (axis, "fft"), pairs)


def after(value, *others):
    return lax.optimization_barrier((value, *others))[0]


def shards(tables, receptor_occupancy, ligand_occupancy, rot_index, receptor_extent, channel_weight):
    _, channels, slab, plane = receptor_occupancy.shape
    s = Sizes(channels, slab, plane, lax.axis_size("fft"))
    t = tables(s)
    swapped = lambda parts: [passed_along(part, "fft") for part in parts]

    own, held = sections(s, t, receptor_occupancy, None, False, s.whole)
    away = [away_planes(s, t, after(receptor_extent, own), held)]
    receptors = []
    receptors.append((passed_along(own, "rec"), [passed_across(part, "rec") for part in away]))

    ligand_occupancy = after(ligand_occupancy, *away)
    pose, *pose_away = sections(s, t, ligand_occupancy, rot_index, True, s.whole)
    pose_others = swapped([after(part, receptors[0][0]) for part in pose_away])
    next_pose, next_others = passed_along(pose, "lig"), [passed_across(part, "lig") for part in pose_away]
    receptors.insert(0, (own, swapped([after(part, next_pose) for part in away])))
    spectra = [spectrum(s, t, channel_weight, pose, pose_others, s.whole)]

    own, others = receptors[1]
    receptors[1] = (own, others)
    ends = [part * s.size for part in s.parts[:-1]] + [None]
    cuts = [others[0][low:high] for low, high in zip(ends, ends[1:])]
    receptors.append((passed_along(own, "rec"), [passed_along(part, "rec") for part in cuts]))

    spectra.append(spectrum(s, t, channel_weight, next_pose, next_others, s.whole))
    poses, tops = [main for main, _ in spectra], [top for _, top in spectra]

    rows = []
    for step, (own, others) in enumerate(receptors):
        last = step + 1 == REC_STEPS
        cuts = s.parts if last else s.whole
        ranges = list(zip(cuts, cuts[1:]))
        if last:
            own = after(own, *rows)
        sides = [cross_back(s, t, own, others, poses, tops, cuts, planes) for planes in ranges]
        parts = [keep for keep, _ in sides] + swapped([send for _, send in sides])
        rows.append(peaks(s, t, others[-1], parts, rows if last else [], last))
    return rows[-1]


def solution(mesh):
    placed = (
        P(("groups", "rec", "lig"), None, "fft", None),
        P(("groups", "rec", "lig"), None, "fft", None),
        P(("groups", "rec", "lig")),
        P(("groups", "rec", "lig")),
        P(),
    )
    tables = lambda s: build_tables(s.cells, s.channels, s.slab, s.cores)
    return jax.shard_map(
        partial(shards, tables),
        mesh=mesh,
        in_specs=placed,
        out_specs=P(("groups", "rec", "lig"), None, None, "fft"),
        check_vma=False,
    )
```
